32 devices in a mesh: fsdp: 16 (over z, y, core), tp: 2 (over x).
Axes of the slice: x: 2, y: 2, z: 4, core: 2. Of those that a mesh axis runs over, the one named last changes fastest.
Arguments:
- tokens: bfloat16 [16384, 1024], P(('fsdp', 'tp')), may hold values from -6 to 6
- out_cotangent: bfloat16 [16384, 1024], P(('fsdp', 'tp')), may hold values from -6 to 6
- attn_gain: float32 [1024], replicated, may hold values from 0.5 to 1.5
- query_weight: bfloat16 [1024, 1024], P('fsdp', 'tp'), may hold values from -0.1875 to 0.1875
- key_weight: bfloat16 [1024, 512], P('fsdp', 'tp'), may hold values from -0.1875 to 0.1875
- value_weight: bfloat16 [1024, 512], P('fsdp', 'tp'), may hold values from -0.1875 to 0.1875
- query_gain: float32 [64], replicated, may hold values from 0.5 to 1.5
- key_gain: float32 [64], replicated, may hold values from 0.5 to 1.5
- out_weight: bfloat16 [1024, 1024], P('tp', 'fsdp'), may hold values from -1.5 to 1.5
- ffn_gain: float32 [1024], replicated, may hold values from 0.5 to 1.5
- gate_weight: bfloat16 [1024, 4608], P('fsdp', 'tp'), may hold values from -0.1875 to 0.1875
- up_weight: bfloat16 [1024, 4608], P('fsdp', 'tp'), may hold values from -0.1875 to 0.1875
- down_weight: bfloat16 [4608, 1024], P('tp', 'fsdp'), may hold values from -0.09375 to 0.09375
Outputs:
- output: bfloat16 [16384, 1024], P(('fsdp', 'tp'))
- tokens_grad: float32 [16384, 1024], P(('fsdp', 'tp'))
- attn_gain_grad: float32 [1024], replicated
- query_weight_grad: float32 [1024, 1024], P('fsdp', 'tp')
- key_weight_grad: float32 [1024, 512], P('fsdp', 'tp')
- value_weight_grad: float32 [1024, 512], P('fsdp', 'tp')
- query_gain_grad: float32 [64], replicated
- key_gain_grad: float32 [64], replicated
- out_weight_grad: float32 [1024, 1024], P('tp', 'fsdp')
- ffn_gain_grad: float32 [1024], replicated
- gate_weight_grad: float32 [1024, 4608], P('fsdp', 'tp')
- up_weight_grad: float32 [1024, 4608], P('fsdp', 'tp')
- down_weight_grad: float32 [4608, 1024], P('tp', 'fsdp')
The draws below stay inside these ranges and needn't reach their ends.
All inputs are finite; a program needn't handle non-finite values.
Results may differ from the reference program's by a relative error of at most 0.02.
Values may be sent and summed in bfloat16 or wider, within the bound.
No kernel may reach another device: no remote copies, remote signals or barrier semaphores. Data moves between devices by JAX's collectives and lax.ppermute only.
A program may use at most 256 MiB of HBM per device.

```python
import jax
import jax.numpy as jnp
from jax import lax

D = 1024
NH = 16
KV = 8
HD = 64
FF = 4608
SEQ = 1024
TOKENS = 16384


def strengthened(array, own_key, source, target, shards_of, factor):
    owner, partner = [(jnp.arange(array.shape[axis_at]) // (array.shape[axis_at] // shards_of)).reshape([-1 if axis == axis_at else 1 for axis in range(array.ndim)]) for axis_at in (source, target)]
    chosen = jax.random.permutation(own_key, shards_of)[partner]
    strong = (owner == chosen) | (owner == (partner + shards_of // 2) % shards_of)
    return jnp.where(strong, factor * array, array)


def level_of(own_key, extent, cuts, least, largest):
    def one(dim, shards_of):
        draws = jax.random.uniform(jax.random.fold_in(jax.random.fold_in(own_key, 6), dim), (shards_of,), jnp.float32, least / len(cuts), largest / len(cuts))
        return jnp.repeat(jnp.exp(draws), extent[dim] // shards_of).reshape((-1,) + (1,) * (len(extent) - dim - 1))

    level = one(*cuts[0])
    for cut in cuts[1:]:
        level = level * one(*cut)
    return level


def scatter_about(own_key, shape, width, bound, pieces=(), kind=jnp.bfloat16):
    entries = width * jax.random.normal(own_key, shape, jnp.float32)
    if pieces:
        entries = entries * level_of(own_key, shape, pieces, -0.22, 0.18)
    return jnp.clip(entries, -bound, bound).astype(kind)


def bell_draw_with(rng, extent, scale, bound, cuts, heavy, kind=jnp.bfloat16):
    values = scale * jax.random.normal(rng, extent, jnp.float32)
    if cuts:
        values = values * level_of(rng, extent, cuts, -0.22, 0.18)
    return jnp.clip(strengthened(values, jax.random.fold_in(rng, 3), *heavy), -bound, bound).astype(kind)


def setup_inputs(seed: int = 0) -> dict:
    seeds = jax.random.split(jax.random.key(seed), 14)
    tokens = scatter_about(seeds[0], (TOKENS, D), 1.0, 6.0, ((0, 32),))
    out_cotangent = bell_draw_with(seeds[1], (TOKENS, D), 1.0, 6.0, ((0, 32),), (0, 1, 32, 2.75))
    attn_gain = jnp.clip(1.0 + 0.1 * jax.random.normal(seeds[2], (D,), jnp.float32), 0.5, 1.5)
    query_weight = scatter_about(seeds[3], (D, NH * HD), D ** -0.5, 0.1875, ((0, 16), (1, 2)))
    key_weight = scatter_about(seeds[4], (D, KV * HD), D ** -0.5, 0.1875, ((0, 16), (1, 2)))
    value_weight = scatter_about(seeds[5], (D, KV * HD), D ** -0.5, 0.1875, ((0, 16), (1, 2)))
    query_gain = jnp.clip(1.0 + 0.1 * jax.random.normal(seeds[6], (HD,), jnp.float32), 0.5, 1.5)
    key_gain = jnp.clip(1.0 + 0.1 * jax.random.normal(seeds[7], (HD,), jnp.float32), 0.5, 1.5)
    out_weight = scatter_about(seeds[8], (NH * HD, D), (HD // 4) ** -0.5, 1.5, ((0, 2), (1, 16)))
    ffn_gain = jnp.clip(1.0 + 0.1 * jax.random.normal(seeds[9], (D,), jnp.float32), 0.5, 1.5)
    gate_weight = scatter_about(seeds[10], (D, FF), D ** -0.5, 0.1875, ((0, 16), (1, 2)))
    up_weight = scatter_about(seeds[11], (D, FF), D ** -0.5, 0.1875, ((0, 16), (1, 2)))
    down_weight = scatter_about(seeds[12], (FF, D), FF ** -0.5, 0.09375, ((0, 2), (1, 16)))
    return dict(tokens=tokens, out_cotangent=out_cotangent, attn_gain=attn_gain, query_weight=query_weight, key_weight=key_weight, value_weight=value_weight, query_gain=query_gain, key_gain=key_gain, out_weight=out_weight, ffn_gain=ffn_gain, gate_weight=gate_weight, up_weight=up_weight, down_weight=down_weight)


eps = 1e-05
theta_base = 1000000.0
highest = lax.Precision.HIGHEST

@jax.custom_vjp
def low(v):
    return lax.optimization_barrier(v.astype(jnp.bfloat16)).astype(jnp.float32)

@jax.custom_vjp
def low_back(v):
    return v

def low_keep(v):
    return (low(v), None)

def low_pass(kept, grad):
    return (grad,)

def back_keep(v):
    return (v, None)

def back_low(kept, grad):
    return (low(grad),)
low.defvjp(low_keep, low_pass)
low_back.defvjp(back_keep, back_low)

def rms_norm(values, gain):
    return values * lax.rsqrt(lax.optimization_barrier(jnp.mean(values * values, axis=-1, keepdims=True)) + eps) * gain

def rotary_tables(length):
    half_size = HD // 2
    frequency = theta_base ** (-jnp.arange(half_size, dtype=jnp.float32) * 2.0 / HD)
    angles = jnp.arange(length, dtype=jnp.float32)[:, None] * frequency[None, :]
    cosine = jnp.concatenate([jnp.cos(angles), jnp.cos(angles)], axis=-1)
    sine_table = jnp.concatenate([jnp.sin(angles), jnp.sin(angles)], axis=-1)
    return (cosine, sine_table)

def rotate(values, cosine, sine_table):
    half_size = values.shape[-1] // 2
    turned = jnp.concatenate([-values[..., half_size:], values[..., :half_size]], axis=-1)
    return values * cosine[:, None, :] + turned * sine_table[:, None, :]

def layer(tokens, attn_gain, query_weight, key_weight, value_weight, query_gain, key_gain, out_weight, ffn_gain, gate_weight, up_weight, down_weight):
    length = tokens.shape[0]
    cosine, sine_table = rotary_tables(length)
    normed = low(rms_norm(tokens, attn_gain))
    query_raw = low_back(jnp.dot(normed, query_weight, precision=highest))
    key_raw = low_back(jnp.dot(normed, key_weight, precision=highest))
    value_raw = low_back(jnp.dot(normed, value_weight, precision=highest))
    query_rows = low(rotate(rms_norm(query_raw.reshape(length, NH, HD), query_gain), cosine, sine_table))
    key_rows = low(rotate(rms_norm(key_raw.reshape(length, KV, HD), key_gain), cosine, sine_table))
    value_rows = low(value_raw.reshape(length, KV, HD))
    group_size = NH // KV
    key_rows = jnp.repeat(key_rows, group_size, axis=1)
    value_rows = jnp.repeat(value_rows, group_size, axis=1)
    scores = low_back(jnp.einsum('qhd,khd->hqk', query_rows, key_rows, precision=highest) * HD ** (-0.5))
    causal = jnp.arange(length)[:, None] >= jnp.arange(length)[None, :]
    scores = jnp.where(causal[None], scores, -1e+30)
    probs = jax.nn.softmax(scores, axis=-1)
    attended = low_back(low(jnp.einsum('hqk,khd->qhd', low(probs), value_rows, precision=highest)))
    branch = low_back(jnp.dot(attended.reshape(length, NH * HD), out_weight, precision=highest))
    middle = tokens + branch
    ffn_rows = low(rms_norm(middle, ffn_gain))
    gate_rows = low_back(jnp.dot(ffn_rows, gate_weight, precision=highest))
    up_rows = low_back(jnp.dot(ffn_rows, up_weight, precision=highest))
    hidden = low(jax.nn.silu(gate_rows) * up_rows)
    return middle + low_back(jnp.dot(hidden, down_weight, precision=highest))

def reference(tokens, out_cotangent, attn_gain, query_weight, key_weight, value_weight, query_gain, key_gain, out_weight, ffn_gain, gate_weight, up_weight, down_weight):
    params = tuple((item.astype(jnp.float32) for item in (attn_gain, query_weight, key_weight, value_weight, query_gain, key_gain, out_weight, ffn_gain, gate_weight, up_weight, down_weight)))
    count = TOKENS // SEQ
    seq_rows = tokens.astype(jnp.float32).reshape(count, SEQ, D)
    seq_cotangent = out_cotangent.astype(jnp.float32).reshape(count, SEQ, D)

    def one_sequence(carry, item):
        rows, cotangent = item
        result, pullback = jax.vjp(layer, rows, *params)
        grads = pullback(cotangent)
        return (tuple((total + grad for total, grad in zip(carry, grads[1:]))), (result, grads[0]))
    zeros = tuple((jnp.zeros(item.shape, jnp.float32) for item in params))
    totals, (results, input_grads) = lax.scan(one_sequence, zeros, (seq_rows, seq_cotangent))
    return (results.reshape(TOKENS, D).astype(jnp.bfloat16), input_grads.reshape(TOKENS, D), totals[0], totals[1], totals[2], totals[3], totals[4], totals[5], totals[6], totals[7], totals[8], totals[9], totals[10])
```

```python
from functools import partial

import jax
import jax.numpy as jnp
from jax import lax
from jax.experimental import pallas as pl
from jax.experimental.pallas import tpu as pltpu
from jax.sharding import PartitionSpec as P

HD = 64

eps = 1e-05
theta_base = 1000000.0
f32 = jnp.float32
bf16 = jnp.bfloat16


def rms_norm(values, gain):
    return values * lax.rsqrt(jnp.mean(values * values, axis=-1, keepdims=True) + eps) * gain


def rotary_tables(length):
    half_size = HD // 2
    frequency = theta_base ** (-jnp.arange(half_size, dtype=f32) * 2.0 / HD)
    angles = jnp.arange(length, dtype=f32)[:, None] * frequency[None, :]
    cosine = jnp.concatenate([jnp.cos(angles), jnp.cos(angles)], axis=-1)
    sine_table = jnp.concatenate([jnp.sin(angles), jnp.sin(angles)], axis=-1)
    return (cosine, sine_table)


def rotate(values, cosine, sine_table):
    half_size = values.shape[-1] // 2
    turned = jnp.concatenate([-values[..., half_size:], values[..., :half_size]], axis=-1)
    return values * cosine[:, None, :] + turned * sine_table[:, None, :]


def prepare(cosine, sine_table, query_raw, key_raw, query_gain, key_gain):
    length = query_raw.shape[0]
    query_rows = rotate(rms_norm(query_raw.reshape(length, -1, HD), query_gain), cosine, sine_table)
    key_rows = rotate(rms_norm(key_raw.reshape(length, -1, HD), key_gain), cosine, sine_table)
    return (query_rows, key_rows)


def dot(former, latter):
    return jnp.dot(former, latter, preferred_element_type=f32)


def dot_transposed(former, latter):
    return lax.dot_general(former, latter, (((1,), (1,)), ((), ())), preferred_element_type=f32)


def dot_leading(former, latter):
    return lax.dot_general(former, latter, (((0,), (0,)), ((), ())), preferred_element_type=f32)


def swap(values, axis_name, bit=1):
    count = lax.axis_size(axis_name)
    return lax.ppermute(values, axis_name, [(i, i ^ bit) for i in range(count)])


def widen(rows):
    if lax.axis_size("tp") == 2:
        return (rows, swap(rows, "tp"))
    return (lax.all_gather(rows, "tp", axis=0, tiled=True),)


def narrow(parts):
    if len(parts) == 2:
        return parts[0].astype(f32) + swap(parts[1].astype(bf16), "tp").astype(f32)
    return lax.psum_scatter(
        parts[0].astype(bf16), "tp", scatter_dimension=0, tiled=True
    ).astype(f32)


def in_order(parts):
    if len(parts) == 1:
        return parts[0]
    first = lax.axis_index("tp") == 0
    return jnp.concatenate(
        [jnp.where(first, parts[0], parts[1]), jnp.where(first, parts[1], parts[0])], axis=0
    )


def in_parts(rows):
    if lax.axis_size("tp") != 2:
        return (rows,)
    half = rows.shape[0] // 2
    index = lax.axis_index("tp")
    return (
        lax.dynamic_slice_in_dim(rows, index * half, half, 0),
        lax.dynamic_slice_in_dim(rows, (1 - index) * half, half, 0),
    )


def sum_everywhere(values):
    for axis_name in ("tp", "fsdp"):
        bit = 1
        while bit < lax.axis_size(axis_name):
            values = values + swap(values, axis_name, bit)
            bit *= 2
    return values


def ffn_body(count, width, *refs):
    rows_in = refs[:count]
    cotangent_in = refs[count : 2 * count]
    weights = refs[2 * count]
    outs = refs[2 * count + 1 : 3 * count + 1]
    grads = refs[3 * count + 1 : 4 * count + 1]
    weight_grads = refs[4 * count + 1]
    rows_turned, cotangent_turned, out_sum, grad_sum, hidden_all, pair_all = refs[4 * count + 2 :]
    step = pl.program_id(0)
    part_rows = rows_in[0].shape[0]

    @pl.when(step == 0)
    def _():
        for part in range(count):
            span = pl.ds(part * part_rows, part_rows)
            rows_turned[:, span] = rows_in[part][...].T
            cotangent_turned[:, span] = cotangent_in[part][...].T
        out_sum[...] = jnp.zeros_like(out_sum)
        grad_sum[...] = jnp.zeros_like(grad_sum)

    pair_weights = weights[:, : 2 * width]
    down = weights[:, 2 * width :]
    chunk = min(256, part_rows)
    for part in range(count):
        for start in range(0, part_rows, chunk):
            here = pl.ds(start, chunk)
            span = pl.ds(part * part_rows + start, chunk)
            both = dot(rows_in[part][here, :], pair_weights)
            gate = both[:, :width]
            up = both[:, width:]
            hidden_grad = dot(cotangent_in[part][here, :], down)
            sigmoid = 1.0 / (1.0 + jnp.exp(-gate))
            silu = gate * sigmoid
            hidden = (silu * up).astype(bf16)
            gate_grad = hidden_grad * up * sigmoid * (1.0 + gate * (1.0 - sigmoid))
            up_grad = hidden_grad * silu
            pair = jnp.concatenate([gate_grad.astype(bf16), up_grad.astype(bf16)], axis=1)
            hidden_all[span, :] = hidden
            pair_all[span, :] = pair
            out_sum[span, :] += dot_transposed(hidden, down)
            grad_sum[span, :] += dot_transposed(pair, pair_weights)
    weight_grads[:, : 2 * width] = dot(rows_turned[...], pair_all[...]).astype(bf16)
    weight_grads[:, 2 * width :] = dot(cotangent_turned[...], hidden_all[...]).astype(bf16)

    @pl.when(step == pl.num_programs(0) - 1)
    def _():
        for part in range(count):
            span = pl.ds(part * part_rows, part_rows)
            outs[part][...] = out_sum[span, :].astype(outs[part].dtype)
            grads[part][...] = grad_sum[span, :].astype(grads[part].dtype)


def hidden_width(units):
    for width in (256, 384, 128):
        if units % width == 0:
            return width
    return units


def feed_forward(rows_parts, cotangent_parts, weights, width):
    count = len(rows_parts)
    part_rows, model = rows_parts[0].shape
    length = count * part_rows
    steps = weights.shape[1] // (3 * width)
    whole = pl.BlockSpec((part_rows, model), lambda i: (0, 0))
    block = pl.BlockSpec((model, 3 * width), lambda i: (0, i))
    kinds = [f32] + [bf16] * (count - 1)
    shapes = [jax.ShapeDtypeStruct((part_rows, model), kind) for kind in kinds]
    results = pl.pallas_call(
        partial(ffn_body, count, width),
        grid=(steps,),
        in_specs=[whole] * (2 * count) + [block],
        out_specs=[whole] * (2 * count) + [block],
        out_shape=shapes + shapes + [jax.ShapeDtypeStruct(weights.shape, bf16)],
        scratch_shapes=[
            pltpu.VMEM((model, length), bf16),
            pltpu.VMEM((model, length), bf16),
            pltpu.VMEM((length, model), f32),
            pltpu.VMEM((length, model), f32),
            pltpu.VMEM((length, width), bf16),
            pltpu.VMEM((length, 2 * width), bf16),
        ],
        compiler_params=pltpu.CompilerParams(vmem_limit_bytes=56 * 1024 * 1024),
        name="feed_forward",
    )(*rows_parts, *cotangent_parts, weights)
    return results[:count], results[count : 2 * count], results[2 * count]


def block_scores(query_block, key_rows, row_start, finish):
    block_rows = query_block.shape[0]
    scores = jnp.einsum(
        "qkgd,skd->kgqs", query_block, key_rows[:finish], preferred_element_type=f32
    ) * HD ** (-0.5)
    causal = (row_start + jnp.arange(block_rows))[:, None] >= jnp.arange(finish)[None, :]
    return jnp.where(causal, scores, -1e30)


def attend(query_rows, key_rows, value_rows):
    length = query_rows.shape[0]
    heads_local = query_rows.shape[1]
    kv_local = key_rows.shape[1]
    grouped = query_rows.reshape(length, kv_local, heads_local // kv_local, HD)
    block_rows = min(512, length)
    outputs = []
    log_totals = []
    for block_index in range(length // block_rows):
        row_start = block_index * block_rows
        finish = row_start + block_rows
        scores = block_scores(grouped[row_start:finish], key_rows, row_start, finish)
        largest = jnp.max(scores, axis=-1, keepdims=True)
        exponent = jnp.exp(scores - largest)
        row_total = jnp.sum(exponent, axis=-1, keepdims=True)
        probability = (exponent / row_total).astype(bf16)
        attended = jnp.einsum(
            "kgqs,skd->qkgd", probability, value_rows[:finish], preferred_element_type=f32
        )
        outputs.append(attended.astype(bf16).reshape(block_rows, heads_local * HD))
        log_totals.append(largest + jnp.log(row_total))
    return (jnp.concatenate(outputs, axis=0), log_totals)


def attend_back(query_rows, key_rows, value_rows, log_totals, attended_grad):
    length = query_rows.shape[0]
    heads_local = query_rows.shape[1]
    kv_local = key_rows.shape[1]
    group_size = heads_local // kv_local
    grouped = query_rows.reshape(length, kv_local, group_size, HD)
    grad_grouped = attended_grad.reshape(length, kv_local, group_size, HD)
    block_rows = min(512, length)
    key_grad = jnp.zeros(key_rows.shape, f32)
    value_grad = jnp.zeros(value_rows.shape, f32)
    query_parts = []
    for block_index in range(length // block_rows):
        row_start = block_index * block_rows
        finish = row_start + block_rows
        query_block = grouped[row_start:finish]
        grad_block = grad_grouped[row_start:finish]
        scores = block_scores(query_block, key_rows, row_start, finish)
        probability = jnp.exp(scores - log_totals[block_index])
        prob_grad = jnp.einsum(
            "qkgd,skd->kgqs", grad_block, value_rows[:finish], preferred_element_type=f32
        )
        inner_sum = jnp.sum(probability * prob_grad, axis=-1, keepdims=True)
        score_grad = (probability * (prob_grad - inner_sum)).astype(bf16)
        query_parts.append(
            jnp.einsum("kgqs,skd->qkgd", score_grad, key_rows[:finish], preferred_element_type=f32)
            * HD ** (-0.5)
        )
        key_grad = key_grad.at[:finish].add(
            jnp.einsum("kgqs,qkgd->skd", score_grad, query_block, preferred_element_type=f32)
            * HD ** (-0.5)
        )
        value_grad = value_grad.at[:finish].add(
            jnp.einsum(
                "kgqs,qkgd->skd", probability.astype(bf16), grad_block, preferred_element_type=f32
            )
        )
    query_grad = jnp.concatenate(query_parts, axis=0).reshape(length, heads_local, HD)
    return (query_grad, key_grad, value_grad)


def on_device(
    tokens,
    out_cotangent,
    attn_gain,
    query_weight,
    key_weight,
    value_weight,
    query_gain,
    key_gain,
    out_weight,
    ffn_gain,
    gate_weight,
    up_weight,
    down_weight,
):
    shard, query_columns = query_weight.shape
    key_columns = key_weight.shape[1]
    qkv_columns = query_columns + 2 * key_columns
    units = gate_weight.shape[1]
    width = hidden_width(units)
    steps = units // width
    attn_shard = jnp.concatenate([query_weight, key_weight, value_weight, out_weight.T], axis=1)
    ffn_shard = jnp.stack(
        [
            gate_weight.reshape(shard, steps, width),
            up_weight.reshape(shard, steps, width),
            down_weight.T.reshape(shard, steps, width),
        ],
        axis=2,
    ).reshape(shard, 3 * units)
    attn_full = lax.all_gather(attn_shard, "fsdp", axis=0, tiled=True)
    qkv_full = attn_full[:, :qkv_columns]
    out_full = attn_full[:, qkv_columns:]
    ffn_full = lax.all_gather(ffn_shard, "fsdp", axis=0, tiled=True)

    residual = tokens.astype(f32)
    normed, attn_norm_pull = jax.vjp(rms_norm, residual, attn_gain)
    normed_rows = in_order(widen(normed.astype(bf16)))
    cotangent_parts = widen(out_cotangent)
    length = normed_rows.shape[0]
    cosine, sine_table = rotary_tables(length)
    qkv_raw = dot(normed_rows, qkv_full)
    query_raw = qkv_raw[:, :query_columns]
    key_raw = qkv_raw[:, query_columns : query_columns + key_columns]
    value_raw = qkv_raw[:, query_columns + key_columns :]
    (query_rows, key_rows), prepare_pull = jax.vjp(
        partial(prepare, cosine, sine_table), query_raw, key_raw, query_gain, key_gain
    )
    query_rows = query_rows.astype(bf16)
    key_rows = key_rows.astype(bf16)
    value_rows = value_raw.astype(bf16).reshape(length, -1, HD)
    attended, log_totals = attend(query_rows, key_rows, value_rows)
    branch = tuple(dot_transposed(part, out_full) for part in in_parts(attended))
    middle = residual + narrow(branch)
    normed_ffn, ffn_norm_pull = jax.vjp(rms_norm, middle, ffn_gain)
    ffn_parts = widen(normed_ffn.astype(bf16))
    out_parts, grad_parts, ffn_grads = feed_forward(ffn_parts, cotangent_parts, ffn_full, width)
    ffn_grads = lax.psum_scatter(ffn_grads, "fsdp", scatter_dimension=0, tiled=True)

    ffn_normed_grad = narrow(grad_parts)
    middle_piece, ffn_gain_local = ffn_norm_pull(ffn_normed_grad)
    middle_grad = out_cotangent.astype(f32) + middle_piece
    branch_rows = in_order(widen(middle_grad.astype(bf16)))
    output = (middle + narrow(out_parts)).astype(bf16)

    out_grad = dot_leading(branch_rows, attended)
    attended_grad = dot(branch_rows, out_full).astype(bf16)
    query_grad, key_grad, value_grad = attend_back(
        query_rows, key_rows, value_rows, log_totals, attended_grad
    )
    query_raw_grad, key_raw_grad, query_gain_local, key_gain_local = prepare_pull(
        (query_grad, key_grad)
    )
    qkv_grad = jnp.concatenate(
        [
            query_raw_grad.astype(bf16),
            key_raw_grad.astype(bf16),
            value_grad.reshape(length, -1).astype(bf16),
        ],
        axis=1,
    )
    normed_grad = narrow(tuple(dot_transposed(part, qkv_full) for part in in_parts(qkv_grad)))
    qkv_weight_grad = dot_leading(normed_rows, qkv_grad)
    attn_grads = jnp.concatenate([qkv_weight_grad.astype(bf16), out_grad.astype(bf16)], axis=1)
    attn_grads = lax.psum_scatter(attn_grads, "fsdp", scatter_dimension=0, tiled=True)
    tokens_piece, attn_gain_local = attn_norm_pull(normed_grad)
    tokens_grad = middle_grad + tokens_piece
    model = attn_gain.shape[0]
    gain_totals = sum_everywhere(
        jnp.concatenate([attn_gain_local, ffn_gain_local, query_gain_local, key_gain_local])
    )
    attn_grads = attn_grads.astype(f32)
    ffn_grads = ffn_grads.reshape(shard, steps, 3, width)
    gate_grad, up_grad, down_grad = (
        ffn_grads[:, :, at].reshape(shard, units).astype(f32) for at in range(3)
    )
    return (
        output,
        tokens_grad,
        gain_totals[:model],
        attn_grads[:, :query_columns],
        attn_grads[:, query_columns : query_columns + key_columns],
        attn_grads[:, query_columns + key_columns : qkv_columns],
        gain_totals[2 * model : 2 * model + HD],
        gain_totals[2 * model + HD :],
        attn_grads[:, qkv_columns:].T,
        gain_totals[model : 2 * model],
        gate_grad,
        up_grad,
        down_grad.T,
    )


def solution(mesh):
    placed = (
        P(("fsdp", "tp"), None),
        P(("fsdp", "tp"), None),
        P(),
        P("fsdp", "tp"),
        P("fsdp", "tp"),
        P("fsdp", "tp"),
        P(),
        P(),
        P("tp", "fsdp"),
        P(),
        P("fsdp", "tp"),
        P("fsdp", "tp"),
        P("tp", "fsdp"),
    )
    return jax.shard_map(
        on_device,
        mesh=mesh,
        in_specs=placed,
        out_specs=(
            P(("fsdp", "tp"), None),
            P(("fsdp", "tp"), None),
            P(),
            P("fsdp", "tp"),
            P("fsdp", "tp"),
            P("fsdp", "tp"),
            P(),
            P(),
            P("tp", "fsdp"),
            P(),
            P("fsdp", "tp"),
            P("fsdp", "tp"),
            P("tp", "fsdp"),
        ),
        check_vma=False,
    )
```

```python
from functools import partial

import jax
import jax.numpy as jnp
from jax import lax
from jax.experimental import pallas as pl
from jax.experimental.pallas import tpu as pltpu
from jax.sharding import PartitionSpec as P

HD = 64

eps = 1e-05
theta_base = 1000000.0
f32 = jnp.float32
bf16 = jnp.bfloat16


def rms_norm(values, gain):
    return values * lax.rsqrt(jnp.mean(values * values, axis=-1, keepdims=True) + eps) * gain


def rotary_tables(length):
    half_size = HD // 2
    frequency = theta_base ** (-jnp.arange(half_size, dtype=f32) * 2.0 / HD)
    angles = jnp.arange(length, dtype=f32)[:, None] * frequency[None, :]
    cosine = jnp.concatenate([jnp.cos(angles), jnp.cos(angles)], axis=-1)
    sine_table = jnp.concatenate([jnp.sin(angles), jnp.sin(angles)], axis=-1)
    return (cosine, sine_table)


def rotate(values, cosine, sine_table):
    half_size = values.shape[-1] // 2
    turned = jnp.concatenate([-values[..., half_size:], values[..., :half_size]], axis=-1)
    return values * cosine[:, None, :] + turned * sine_table[:, None, :]


def prepare(cosine, sine_table, query_raw, key_raw, query_gain, key_gain):
    length = query_raw.shape[0]
    query_rows = rotate(rms_norm(query_raw.reshape(length, -1, HD), query_gain), cosine, sine_table)
    key_rows = rotate(rms_norm(key_raw.reshape(length, -1, HD), key_gain), cosine, sine_table)
    return (query_rows, key_rows)


def dot(former, latter):
    return jnp.dot(former, latter, preferred_element_type=f32)


def dot_transposed(former, latter):
    return lax.dot_general(former, latter, (((1,), (1,)), ((), ())), preferred_element_type=f32)


def dot_leading(former, latter):
    return lax.dot_general(former, latter, (((0,), (0,)), ((), ())), preferred_element_type=f32)


def swap(values, axis_name, bit=1):
    count = lax.axis_size(axis_name)
    return lax.ppermute(values, axis_name, [(i, i ^ bit) for i in range(count)])


def widen(rows):
    if lax.axis_size("tp") == 2:
        return (rows, swap(rows, "tp"))
    return (lax.all_gather(rows, "tp", axis=0, tiled=True),)


def narrow(parts):
    if len(parts) == 2:
        return parts[0].astype(f32) + swap(parts[1].astype(bf16), "tp").astype(f32)
    return lax.psum_scatter(
        parts[0].astype(bf16), "tp", scatter_dimension=0, tiled=True
    ).astype(f32)


def in_order(parts):
    if len(parts) == 1:
        return parts[0]
    first = lax.axis_index("tp") == 0
    return jnp.concatenate(
        [jnp.where(first, parts[0], parts[1]), jnp.where(first, parts[1], parts[0])], axis=0
    )


def in_parts(rows):
    if lax.axis_size("tp") != 2:
        return (rows,)
    half = rows.shape[0] // 2
    index = lax.axis_index("tp")
    return (
        lax.dynamic_slice_in_dim(rows, index * half, half, 0),
        lax.dynamic_slice_in_dim(rows, (1 - index) * half, half, 0),
    )


def sum_everywhere(values):
    for axis_name in ("tp", "fsdp"):
        bit = 1
        while bit < lax.axis_size(axis_name):
            values = values + swap(values, axis_name, bit)
            bit *= 2
    return values


def ring_size():
    return lax.axis_size("fsdp") // 2


def chip_at(place):
    chips = ring_size()
    if isinstance(place, int):
        return 2 * place if place < chips // 2 else 2 * (chips - 1 - place) + 1
    return jnp.where(place < chips // 2, 2 * place, 2 * (chips - 1 - place) + 1)


def own_place():
    chip = lax.axis_index("fsdp") // 2
    return jnp.where(chip % 2 == 0, chip // 2, ring_size() - 1 - chip // 2)


def pass_on(values, direction):
    chips = ring_size()
    pairs = [
        (2 * chip_at(place) + core, 2 * chip_at((place + direction) % chips) + core)
        for place in range(chips)
        for core in range(2)
    ]
    return lax.ppermute(values, "fsdp", pairs)


def shard_table(ahead):
    core = lax.axis_index("fsdp") % 2
    chips = chip_at((own_place() + jnp.array(ahead, jnp.int32)) % ring_size())
    return jnp.concatenate([2 * chips + core, 2 * chips + 1 - core]).astype(jnp.int32)


def assemble_body(count, table, *refs):
    whole = refs[count]
    rows = refs[0].shape[0]
    for at in range(count):
        start = pl.multiple_of(table[at] * rows, rows)
        whole[pl.ds(start, rows), :] = refs[at][...]


def gather_ring(shard):
    chips = ring_size()
    ahead = [0]
    blocks = [shard]
    down = up = shard
    for step in range(1, chips // 2 + 1):
        down = pass_on(down, 1)
        ahead.append(chips - step)
        blocks.append(down)
        if step < chips // 2:
            up = pass_on(up, -1)
            ahead.append(step)
            blocks.append(up)
    blocks = blocks + [swap(block, "fsdp") for block in blocks]
    rows, columns = shard.shape
    count = len(blocks)
    vmem = pl.BlockSpec(memory_space=pltpu.VMEM)
    return pl.pallas_call(
        partial(assemble_body, count),
        in_specs=[pl.BlockSpec(memory_space=pltpu.SMEM)] + [vmem] * count,
        out_specs=vmem,
        out_shape=jax.ShapeDtypeStruct((count * rows, columns), shard.dtype),
        compiler_params=pltpu.CompilerParams(vmem_limit_bytes=48 * 1024 * 1024),
        name="assemble",
    )(shard_table(ahead), *blocks)


def ring_groups():
    chips = ring_size()
    middle = [[chips // 2 - step, chips // 2 + step] for step in range(1, chips // 2)]
    return [[chips // 2]] + middle + [[0]]


def weight_grad_body(parts, groups, rows, *refs):
    table = refs[0]
    first_in = refs[1 : 1 + parts]
    second_in = refs[1 + parts : 1 + 2 * parts]
    first_grads = refs[1 + 2 * parts : 1 + 3 * parts]
    second_grads = refs[1 + 3 * parts : 1 + 4 * parts]
    outs = refs[1 + 4 * parts : -3]
    first_turned, second_turned, total = refs[-3:]
    part_rows = first_in[0].shape[0]
    first_width = first_grads[0].shape[1]

    @pl.when(pl.program_id(0) == 0)
    def _():
        for part in range(parts):
            span = pl.ds(part * part_rows, part_rows)
            first_turned[:, span] = first_in[part][...].T
            second_turned[:, span] = second_in[part][...].T

    def joined(pieces):
        if parts == 1:
            return pieces[0][...]
        return jnp.concatenate([piece[...] for piece in pieces], axis=0)

    total[:, :first_width] = dot(first_turned[...], joined(first_grads)).astype(bf16)
    total[:, first_width:] = dot(second_turned[...], joined(second_grads)).astype(bf16)
    count = sum(len(group) for group in groups)
    at = 0
    for number, group in enumerate(groups):
        for member in range(len(group)):
            mine = pl.multiple_of(table[at] * rows, rows)
            outs[number][member] = total[pl.ds(mine, rows), :]
            near = pl.multiple_of(table[count + at] * rows, rows)
            outs[len(groups) + number][member] = total[pl.ds(near, rows), :]
            at += 1


def weight_grads(first, second, first_grads, second_grads, steps):
    parts = len(first)
    part_rows, model = first[0].shape
    length = parts * part_rows
    first_width = first_grads[0].shape[1] // steps
    second_width = second_grads[0].shape[1] // steps
    width = first_width + second_width
    groups = ring_groups()
    count = 2 * ring_size()
    rows = model // count
    table = shard_table([place for group in groups for place in group])
    whole = pl.BlockSpec((part_rows, model), lambda i: (0, 0))
    outs = [jax.ShapeDtypeStruct((len(group), rows, steps * width), bf16) for group in groups] * 2
    out_specs = [
        pl.BlockSpec((len(group), rows, width), lambda i: (0, 0, i)) for group in groups
    ] * 2
    results = pl.pallas_call(
        partial(weight_grad_body, parts, groups, rows),
        grid=(steps,),
        in_specs=[pl.BlockSpec(memory_space=pltpu.SMEM)]
        + [whole] * (2 * parts)
        + [pl.BlockSpec((part_rows, first_width), lambda i: (0, i))] * parts
        + [pl.BlockSpec((part_rows, second_width), lambda i: (0, i))] * parts,
        out_specs=out_specs,
        out_shape=outs,
        scratch_shapes=[
            pltpu.VMEM((model, length), bf16),
            pltpu.VMEM((model, length), bf16),
            pltpu.VMEM((model, width), bf16),
        ],
        compiler_params=pltpu.CompilerParams(vmem_limit_bytes=56 * 1024 * 1024),
        cost_estimate=pl.CostEstimate(
            flops=2 * length * model * steps * width,
            bytes_accessed=4 * model * steps * width,
            transcendentals=0,
        ),
        name="weight_grads",
    )(table, *first, *second, *first_grads, *second_grads)
    mine = results[: len(groups)]
    near = [swap(block, "fsdp") for block in results[len(groups) :]]
    half = steps * width // 2

    def share(group, member):
        return mine[group][member].astype(f32) + near[group][member].astype(f32)

    far = share(0, 0).astype(bf16)
    down = pass_on(far[:, :half], 1)
    up = pass_on(far[:, half:], -1)
    for step in range(1, ring_size() // 2):
        ahead, behind = share(step, 0), share(step, 1)
        if step == 1:
            ahead = jnp.concatenate([ahead[:, :half] + down.astype(f32), ahead[:, half:]], axis=1)
            behind = jnp.concatenate([behind[:, :half], behind[:, half:] + up.astype(f32)], axis=1)
        else:
            ahead = ahead + down.astype(f32)
            behind = behind + up.astype(f32)
        down = pass_on(ahead.astype(bf16), 1)
        up = pass_on(behind.astype(bf16), -1)
    return share(len(groups) - 1, 0) + down.astype(f32) + up.astype(f32)


def ffn_body(width, rows_in, cotangent_in, weights, out, grad, pairs, hiddens, out_sum, grad_sum):
    step = pl.program_id(0)
    length = rows_in.shape[0]

    @pl.when(step == 0)
    def _():
        out_sum[...] = jnp.zeros_like(out_sum)
        grad_sum[...] = jnp.zeros_like(grad_sum)

    pair_weights = weights[:, : 2 * width]
    down = weights[:, 2 * width :]
    chunk = min(256, length)
    for start in range(0, length, chunk):
        span = pl.ds(start, chunk)
        both = dot(rows_in[span, :], pair_weights)
        gate = both[:, :width]
        up = both[:, width:]
        hidden_grad = dot(cotangent_in[span, :], down)
        sigmoid = 1.0 / (1.0 + jnp.exp(-gate))
        silu = gate * sigmoid
        hidden = (silu * up).astype(bf16)
        gate_grad = hidden_grad * up * sigmoid * (1.0 + gate * (1.0 - sigmoid))
        up_grad = hidden_grad * silu
        pair = jnp.concatenate([gate_grad.astype(bf16), up_grad.astype(bf16)], axis=1)
        hiddens[span, :] = hidden
        pairs[span, :] = pair
        out_sum[span, :] += dot_transposed(hidden, down)
        grad_sum[span, :] += dot_transposed(pair, pair_weights)

    @pl.when(step == pl.num_programs(0) - 1)
    def _():
        out[...] = out_sum[...].astype(out.dtype)
        grad[...] = grad_sum[...].astype(grad.dtype)


def hidden_width(units):
    for width in (256, 384, 128):
        if units % width == 0:
            return width
    return units


def feed_forward(rows, cotangent, weights, width, kind):
    length, model = rows.shape
    steps = weights.shape[1] // (3 * width)
    whole = pl.BlockSpec((length, model), lambda i: (0, 0))
    sums = jax.ShapeDtypeStruct((length, model), kind)
    return pl.pallas_call(
        partial(ffn_body, width),
        grid=(steps,),
        in_specs=[whole, whole, pl.BlockSpec((model, 3 * width), lambda i: (0, i))],
        out_specs=[
            whole,
            whole,
            pl.BlockSpec((length, 2 * width), lambda i: (0, i)),
            pl.BlockSpec((length, width), lambda i: (0, i)),
        ],
        out_shape=[
            sums,
            sums,
            jax.ShapeDtypeStruct((length, steps * 2 * width), bf16),
            jax.ShapeDtypeStruct((length, steps * width), bf16),
        ],
        scratch_shapes=[
            pltpu.VMEM((length, model), f32),
            pltpu.VMEM((length, model), f32),
        ],
        compiler_params=pltpu.CompilerParams(vmem_limit_bytes=56 * 1024 * 1024),
        cost_estimate=pl.CostEstimate(
            flops=12 * length * model * steps * width,
            bytes_accessed=8 * model * steps * width,
            transcendentals=length * steps * width,
        ),
        name="feed_forward",
    )(rows, cotangent, weights)


def block_scores(query_block, key_rows, row_start, finish):
    block_rows = query_block.shape[0]
    scores = jnp.einsum(
        "qkgd,skd->kgqs", query_block, key_rows[:finish], preferred_element_type=f32
    ) * HD ** (-0.5)
    causal = (row_start + jnp.arange(block_rows))[:, None] >= jnp.arange(finish)[None, :]
    return jnp.where(causal, scores, -1e30)


def attend(query_rows, key_rows, value_rows):
    length = query_rows.shape[0]
    heads_local = query_rows.shape[1]
    kv_local = key_rows.shape[1]
    grouped = query_rows.reshape(length, kv_local, heads_local // kv_local, HD)
    block_rows = min(512, length)
    outputs = []
    log_totals = []
    for block_index in range(length // block_rows):
        row_start = block_index * block_rows
        finish = row_start + block_rows
        scores = block_scores(grouped[row_start:finish], key_rows, row_start, finish)
        largest = jnp.max(scores, axis=-1, keepdims=True)
        exponent = jnp.exp(scores - largest)
        row_total = jnp.sum(exponent, axis=-1, keepdims=True)
        probability = (exponent / row_total).astype(bf16)
        attended = jnp.einsum(
            "kgqs,skd->qkgd", probability, value_rows[:finish], preferred_element_type=f32
        )
        outputs.append(attended.astype(bf16).reshape(block_rows, heads_local * HD))
        log_totals.append(largest + jnp.log(row_total))
    return (jnp.concatenate(outputs, axis=0), log_totals)


def attend_back(query_rows, key_rows, value_rows, log_totals, attended_grad):
    length = query_rows.shape[0]
    heads_local = query_rows.shape[1]
    kv_local = key_rows.shape[1]
    group_size = heads_local // kv_local
    grouped = query_rows.reshape(length, kv_local, group_size, HD)
    grad_grouped = attended_grad.reshape(length, kv_local, group_size, HD)
    block_rows = min(512, length)
    key_grad = jnp.zeros(key_rows.shape, f32)
    value_grad = jnp.zeros(value_rows.shape, f32)
    query_parts = []
    for block_index in range(length // block_rows):
        row_start = block_index * block_rows
        finish = row_start + block_rows
        query_block = grouped[row_start:finish]
        grad_block = grad_grouped[row_start:finish]
        scores = block_scores(query_block, key_rows, row_start, finish)
        probability = jnp.exp(scores - log_totals[block_index])
        prob_grad = jnp.einsum(
            "qkgd,skd->kgqs", grad_block, value_rows[:finish], preferred_element_type=f32
        )
        inner_sum = jnp.sum(probability * prob_grad, axis=-1, keepdims=True)
        score_grad = (probability * (prob_grad - inner_sum)).astype(bf16)
        query_parts.append(
            jnp.einsum("kgqs,skd->qkgd", score_grad, key_rows[:finish], preferred_element_type=f32)
            * HD ** (-0.5)
        )
        key_grad = key_grad.at[:finish].add(
            jnp.einsum("kgqs,qkgd->skd", score_grad, query_block, preferred_element_type=f32)
            * HD ** (-0.5)
        )
        value_grad = value_grad.at[:finish].add(
            jnp.einsum(
                "kgqs,qkgd->skd", probability.astype(bf16), grad_block, preferred_element_type=f32
            )
        )
    query_grad = jnp.concatenate(query_parts, axis=0).reshape(length, heads_local, HD)
    return (query_grad, key_grad, value_grad)


def on_device(
    tokens,
    out_cotangent,
    attn_gain,
    query_weight,
    key_weight,
    value_weight,
    query_gain,
    key_gain,
    out_weight,
    ffn_gain,
    gate_weight,
    up_weight,
    down_weight,
):
    shard, query_columns = query_weight.shape
    key_columns = key_weight.shape[1]
    qkv_columns = query_columns + 2 * key_columns
    units = gate_weight.shape[1]
    width = hidden_width(units)
    steps = units // width
    attn_shard = jnp.concatenate([query_weight, key_weight, value_weight, out_weight.T], axis=1)
    ffn_shard = jnp.stack(
        [
            gate_weight.reshape(shard, steps, width),
            up_weight.reshape(shard, steps, width),
            down_weight.T.reshape(shard, steps, width),
        ],
        axis=2,
    ).reshape(shard, 3 * units)
    attn_full = gather_ring(attn_shard)
    qkv_full = attn_full[:, :qkv_columns]
    out_full = attn_full[:, qkv_columns:]
    ffn_full = lax.all_gather(ffn_shard, "fsdp", axis=0, tiled=True)

    residual = tokens.astype(f32)
    normed, attn_norm_pull = jax.vjp(rms_norm, residual, attn_gain)
    normed_rows = in_order(widen(normed.astype(bf16)))
    cotangent_parts = widen(out_cotangent)
    length = normed_rows.shape[0]
    cosine, sine_table = rotary_tables(length)
    qkv_raw = dot(normed_rows, qkv_full)
    query_raw = qkv_raw[:, :query_columns]
    key_raw = qkv_raw[:, query_columns : query_columns + key_columns]
    value_raw = qkv_raw[:, query_columns + key_columns :]
    (query_rows, key_rows), prepare_pull = jax.vjp(
        partial(prepare, cosine, sine_table), query_raw, key_raw, query_gain, key_gain
    )
    query_rows = query_rows.astype(bf16)
    key_rows = key_rows.astype(bf16)
    value_rows = value_raw.astype(bf16).reshape(length, -1, HD)
    attended, log_totals = attend(query_rows, key_rows, value_rows)
    branch = tuple(dot_transposed(part, out_full) for part in in_parts(attended))
    middle = residual + narrow(branch)
    normed_ffn, ffn_norm_pull = jax.vjp(rms_norm, middle, ffn_gain)
    ffn_parts = widen(normed_ffn.astype(bf16))
    results = [
        feed_forward(rows, cotangent, ffn_full, width, bf16 if at else f32)
        for at, (rows, cotangent) in reversed(list(enumerate(zip(ffn_parts, cotangent_parts))))
    ][::-1]
    out_parts, grad_parts, pairs, hiddens = zip(*results)
    ffn_normed_grad = narrow(grad_parts)
    middle_piece, ffn_gain_local = ffn_norm_pull(ffn_normed_grad)
    middle_grad = out_cotangent.astype(f32) + middle_piece
    branch_rows = in_order(widen(middle_grad.astype(bf16)))
    output = (middle + narrow(out_parts)).astype(bf16)
    ffn_grads = weight_grads(ffn_parts, cotangent_parts, pairs, hiddens, steps)

    attended_grad = dot(branch_rows, out_full).astype(bf16)
    query_grad, key_grad, value_grad = attend_back(
        query_rows, key_rows, value_rows, log_totals, attended_grad
    )
    query_raw_grad, key_raw_grad, query_gain_local, key_gain_local = prepare_pull(
        (query_grad, key_grad)
    )
    qkv_grad = jnp.concatenate(
        [
            query_raw_grad.astype(bf16),
            key_raw_grad.astype(bf16),
            value_grad.reshape(length, -1).astype(bf16),
        ],
        axis=1,
    )
    normed_grad = narrow(tuple(dot_transposed(part, qkv_full) for part in in_parts(qkv_grad)))
    attn_grads = weight_grads((normed_rows,), (branch_rows,), (qkv_grad,), (attended,), 1)
    tokens_piece, attn_gain_local = attn_norm_pull(normed_grad)
    tokens_grad = middle_grad + tokens_piece
    model = attn_gain.shape[0]
    gain_totals = sum_everywhere(
        jnp.concatenate([attn_gain_local, ffn_gain_local, query_gain_local, key_gain_local])
    )
    ffn_grads = ffn_grads.reshape(shard, steps, 3, width)
    gate_grad, up_grad, down_grad = (
        ffn_grads[:, :, at].reshape(shard, units) for at in range(3)
    )
    return (
        output,
        tokens_grad,
        gain_totals[:model],
        attn_grads[:, :query_columns],
        attn_grads[:, query_columns : query_columns + key_columns],
        attn_grads[:, query_columns + key_columns : qkv_columns],
        gain_totals[2 * model : 2 * model + HD],
        gain_totals[2 * model + HD :],
        attn_grads[:, qkv_columns:].T,
        gain_totals[model : 2 * model],
        gate_grad,
        up_grad,
        down_grad.T,
    )


def solution(mesh):
    placed = (
        P(("fsdp", "tp"), None),
        P(("fsdp", "tp"), None),
        P(),
        P("fsdp", "tp"),
        P("fsdp", "tp"),
        P("fsdp", "tp"),
        P(),
        P(),
        P("tp", "fsdp"),
        P(),
        P("fsdp", "tp"),
        P("fsdp", "tp"),
        P("tp", "fsdp"),
    )
    return jax.shard_map(
        on_device,
        mesh=mesh,
        in_specs=placed,
        out_specs=(
            P(("fsdp", "tp"), None),
            P(("fsdp", "tp"), None),
            P(),
            P("fsdp", "tp"),
            P("fsdp", "tp"),
            P("fsdp", "tp"),
            P(),
            P(),
            P("tp", "fsdp"),
            P(),
            P("fsdp", "tp"),
            P("fsdp", "tp"),
            P("tp", "fsdp"),
        ),
        check_vma=False,
    )
```

```python
from functools import partial

import jax
import jax.numpy as jnp
from jax import lax
from jax.experimental import pallas as pl
from jax.experimental.pallas import tpu as pltpu
from jax.sharding import PartitionSpec as P

HD = 64

eps = 1e-05
theta_base = 1000000.0
f32 = jnp.float32
bf16 = jnp.bfloat16


def rms_norm(values, gain):
    return values * lax.rsqrt(jnp.mean(values * values, axis=-1, keepdims=True) + eps) * gain


def rotary_tables(length):
    half_size = HD // 2
    frequency = theta_base ** (-jnp.arange(half_size, dtype=f32) * 2.0 / HD)
    angles = frequency[:, None] * jnp.arange(length, dtype=f32)[None, :]
    return (jnp.cos(angles), jnp.sin(angles))


def dot(former, latter):
    return jnp.dot(former, latter, preferred_element_type=f32)


def dot_transposed(former, latter):
    return lax.dot_general(former, latter, (((1,), (1,)), ((), ())), preferred_element_type=f32)


def dot_leading(former, latter):
    return lax.dot_general(former, latter, (((0,), (0,)), ((), ())), preferred_element_type=f32)


def swap(values, axis_name, bit=1):
    count = lax.axis_size(axis_name)
    return lax.ppermute(values, axis_name, [(i, i ^ bit) for i in range(count)])


def widen(rows):
    if lax.axis_size("tp") == 2:
        return (rows, swap(rows, "tp"))
    return (lax.all_gather(rows, "tp", axis=0, tiled=True),)


def narrow(parts):
    if len(parts) == 2:
        return parts[0].astype(f32) + swap(parts[1].astype(bf16), "tp").astype(f32)
    return lax.psum_scatter(
        parts[0].astype(bf16), "tp", scatter_dimension=0, tiled=True
    ).astype(f32)


def sum_everywhere(values):
    count, chips = lax.axis_size("tp"), ring_size()
    terms = [values]
    for step in range(1, count):
        terms.append(lax.ppermute(values, "tp", [(i, (i + step) % count) for i in range(count)]))
    values = sum(terms[1:], terms[0])
    values = values + swap(values, "fsdp")
    return sum([pass_on(values, step) for step in range(1, chips)], values)


def ring_size():
    return lax.axis_size("fsdp") // 2


def chip_at(place):
    chips = ring_size()
    if isinstance(place, int):
        return 2 * place if place < chips // 2 else 2 * (chips - 1 - place) + 1
    return jnp.where(place < chips // 2, 2 * place, 2 * (chips - 1 - place) + 1)


def own_place():
    chip = lax.axis_index("fsdp") // 2
    return jnp.where(chip % 2 == 0, chip // 2, ring_size() - 1 - chip // 2)


def pass_on(values, direction):
    chips = ring_size()
    pairs = [
        (2 * chip_at(place) + core, 2 * chip_at((place + direction) % chips) + core)
        for place in range(chips)
        for core in range(2)
    ]
    return lax.ppermute(values, "fsdp", pairs)


def shard_table(ahead):
    core = lax.axis_index("fsdp") % 2
    chips = chip_at((own_place() + jnp.array(ahead, jnp.int32)) % ring_size())
    return jnp.concatenate([2 * chips + core, 2 * chips + 1 - core]).astype(jnp.int32)


def assemble_body(count, table, *refs):
    whole = refs[count]
    rows = refs[0].shape[0]
    for at in range(count):
        start = pl.multiple_of(table[at] * rows, rows)
        whole[pl.ds(start, rows), :] = refs[at][...]


def gather_ring(shard):
    chips = ring_size()
    ahead = [0]
    blocks = [shard]
    down = up = shard
    for step in range(1, chips // 2 + 1):
        down = pass_on(down, 1)
        ahead.append(chips - step)
        blocks.append(down)
        if step < chips // 2:
            up = pass_on(up, -1)
            ahead.append(step)
            blocks.append(up)
    blocks = blocks + [swap(block, "fsdp") for block in blocks]
    rows, columns = shard.shape
    count = len(blocks)
    vmem = pl.BlockSpec(memory_space=pltpu.VMEM)
    return pl.pallas_call(
        partial(assemble_body, count),
        in_specs=[pl.BlockSpec(memory_space=pltpu.SMEM)] + [vmem] * count,
        out_specs=vmem,
        out_shape=jax.ShapeDtypeStruct((count * rows, columns), shard.dtype),
        compiler_params=pltpu.CompilerParams(vmem_limit_bytes=48 * 1024 * 1024),
        name="assemble",
    )(shard_table(ahead), *blocks)


def ring_groups():
    chips = ring_size()
    middle = [[chips // 2 - step, chips // 2 + step] for step in range(1, chips // 2)]
    return [[chips // 2]] + middle + [[0]]


def anywhere():
    return pl.BlockSpec(memory_space=pl.ANY)


def held(values, after):
    return pl.pallas_call(
        lambda *refs: None,
        in_specs=[anywhere()] * (1 + len(after)),
        out_specs=anywhere(),
        out_shape=jax.ShapeDtypeStruct(values.shape, values.dtype),
        input_output_aliases={0: 0},
        name="held",
    )(values, *after)


def weight_grad_body(parts, groups, rows, extra, *refs):
    table = refs[0]
    first_in = refs[1 : 1 + parts]
    second_in = refs[1 + parts : 1 + 2 * parts]
    first_grads = refs[1 + 2 * parts : 1 + 3 * parts]
    second_grads = refs[1 + 3 * parts : 1 + 4 * parts]
    outs = refs[1 + 4 * parts + extra : -3]
    first_turned, second_turned, total = refs[-3:]
    part_rows = first_in[0].shape[0]
    first_width = first_grads[0].shape[1]

    @pl.when(pl.program_id(0) == 0)
    def _():
        for part in range(parts):
            span = pl.ds(part * part_rows, part_rows)
            first_turned[:, span] = first_in[part][...].T
            second_turned[:, span] = second_in[part][...].T

    def joined(pieces):
        if parts == 1:
            return pieces[0][...]
        return jnp.concatenate([piece[...] for piece in pieces], axis=0)

    total[:, :first_width] = dot(first_turned[...], joined(first_grads)).astype(bf16)
    total[:, first_width:] = dot(second_turned[...], joined(second_grads)).astype(bf16)
    count = sum(len(group) for group in groups)
    at = 0
    for number, group in enumerate(groups):
        for member in range(len(group)):
            mine = pl.multiple_of(table[at] * rows, rows)
            outs[number][member] = total[pl.ds(mine, rows), :]
            near = pl.multiple_of(table[count + at] * rows, rows)
            outs[len(groups) + number][member] = total[pl.ds(near, rows), :]
            at += 1


def weight_grads(first, second, first_grads, second_grads, steps, after, before=()):
    parts = len(first)
    part_rows, model = first[0].shape
    length = parts * part_rows
    first_width = first_grads[0].shape[1] // steps
    second_width = second_grads[0].shape[1] // steps
    width = first_width + second_width
    groups = ring_groups()
    count = 2 * ring_size()
    rows = model // count
    table = shard_table([place for group in groups for place in group])
    whole = pl.BlockSpec((part_rows, model), lambda i: (0, 0))
    outs = [jax.ShapeDtypeStruct((len(group), rows, steps * width), bf16) for group in groups] * 2
    out_specs = [
        pl.BlockSpec((len(group), rows, width), lambda i: (0, 0, i)) for group in groups
    ] * 2
    results = pl.pallas_call(
        partial(weight_grad_body, parts, groups, rows, len(after)),
        grid=(steps,),
        in_specs=[pl.BlockSpec(memory_space=pltpu.SMEM)]
        + [whole] * (2 * parts)
        + [pl.BlockSpec((part_rows, first_width), lambda i: (0, i))] * parts
        + [pl.BlockSpec((part_rows, second_width), lambda i: (0, i))] * parts
        + [anywhere()] * len(after),
        out_specs=out_specs,
        out_shape=outs,
        scratch_shapes=[
            pltpu.VMEM((model, length), bf16),
            pltpu.VMEM((model, length), bf16),
            pltpu.VMEM((model, width), bf16),
        ],
        compiler_params=pltpu.CompilerParams(vmem_limit_bytes=56 * 1024 * 1024),
        cost_estimate=pl.CostEstimate(
            flops=2 * length * model * steps * width,
            bytes_accessed=4 * model * steps * width,
            transcendentals=0,
        ),
        name="weight_grads",
    )(table, *first, *second, *first_grads, *second_grads, *after)
    mine = results[: len(groups)]
    near = list(results[len(groups) :])
    if before:
        near[0] = held(near[0], before)
    near = [swap(block, "fsdp") for block in near]
    return mine, near


def ring_call(body, operands, outs, after, name):
    vmem = pl.BlockSpec(memory_space=pltpu.VMEM)
    return pl.pallas_call(
        body,
        in_specs=[vmem] * len(operands) + [anywhere()] * len(after),
        out_specs=[vmem] * len(outs),
        out_shape=outs,
        compiler_params=pltpu.CompilerParams(vmem_limit_bytes=48 * 1024 * 1024),
        name=name,
    )(*operands, *after)


def both_cores(mine, near, member):
    return mine[member].astype(f32) + near[member].astype(f32)


def open_body(cut, mine, near, *refs):
    low, high = refs[-2:]
    total = both_cores(mine, near, 0).astype(bf16)
    low[...] = total[:, :cut]
    high[...] = total[:, cut:]


def step_body(cut, mine, near, down, up, *refs):
    ahead, behind = refs[-2:]
    columns = ahead.shape[1]
    ahead_sum = both_cores(mine, near, 0)
    behind_sum = both_cores(mine, near, 1)
    if down.shape[1] == columns:
        ahead[...] = (ahead_sum + down[...].astype(f32)).astype(bf16)
        behind[...] = (behind_sum + up[...].astype(f32)).astype(bf16)
    else:
        ahead[:, :cut] = (ahead_sum[:, :cut] + down[...].astype(f32)).astype(bf16)
        ahead[:, cut:] = ahead_sum[:, cut:].astype(bf16)
        behind[:, :cut] = behind_sum[:, :cut].astype(bf16)
        behind[:, cut:] = (behind_sum[:, cut:] + up[...].astype(f32)).astype(bf16)


def close_body(pieces, mine, near, down, up, *outs):
    total = both_cores(mine, near, 0) + down[...].astype(f32) + up[...].astype(f32)
    for start, width, number, place, turn in pieces:
        values = total[:, start : start + width]
        if turn:
            outs[number][place : place + width, :] = values.T
        else:
            outs[number][:, place : place + width] = values


def ring_cut(columns):
    return columns // 2 // 128 * 128


def ring_pass(sums):
    return pass_on(sums[0], 1), pass_on(sums[1], -1)


def ring_open(blocks, after=()):
    mine, near = blocks
    rows, columns = mine[0].shape[1:]
    cut = ring_cut(columns)
    outs = [jax.ShapeDtypeStruct((rows, width), bf16) for width in (cut, columns - cut)]
    sums = ring_call(partial(open_body, cut), (mine[0], near[0]), outs, after, "ring_open")
    return ring_pass(sums), tuple(sums)


def ring_step(blocks, number, state, after=()):
    mine, near = blocks[0][number], blocks[1][number]
    rows, columns = mine.shape[1:]
    outs = [jax.ShapeDtypeStruct((rows, columns), bf16)] * 2
    body = partial(step_body, ring_cut(columns))
    sums = ring_call(body, (mine, near, *state), outs, after, "ring_step")
    return ring_pass(sums), tuple(sums)


def ring_close(blocks, state, pieces):
    mine, near = blocks[0][-1], blocks[1][-1]
    rows = mine.shape[1]
    in_kernel = all(width % 128 == 0 for _, width, _, _, turn in pieces if turn)
    sizes, turns = {}, {}
    for _, width, number, place, turn in pieces:
        sizes[number] = max(sizes.get(number, 0), place + width)
        turns[number] = turn
    if not in_kernel:
        pieces = [piece[:4] + (False,) for piece in pieces]
    outs = [
        jax.ShapeDtypeStruct(
            (sizes[number], rows) if turns[number] and in_kernel else (rows, sizes[number]), f32
        )
        for number in range(len(sizes))
    ]
    results = ring_call(
        partial(close_body, pieces), (mine, near, *state), outs, (), "ring_close"
    )
    return [
        result.T if turns[number] and not in_kernel else result
        for number, result in enumerate(results)
    ]


def ffn_body(width, extra, *refs):
    rows_in, cotangent_in, weights = refs[:3]
    out, grad, pairs, hiddens, out_sum, grad_sum = refs[3 + extra :]
    step = pl.program_id(0)
    length = rows_in.shape[0]

    @pl.when(step == 0)
    def _():
        out_sum[...] = jnp.zeros_like(out_sum)
        grad_sum[...] = jnp.zeros_like(grad_sum)

    pair_weights = weights[:, : 2 * width]
    down = weights[:, 2 * width :]
    chunk = min(256, length)
    for start in range(0, length, chunk):
        span = pl.ds(start, chunk)
        both = dot(rows_in[span, :], pair_weights)
        gate = both[:, :width]
        up = both[:, width:]
        hidden_grad = dot(cotangent_in[span, :], down)
        sigmoid = 1.0 / (1.0 + jnp.exp(-gate))
        silu = gate * sigmoid
        hidden = (silu * up).astype(bf16)
        gate_grad = hidden_grad * up * sigmoid * (1.0 + gate * (1.0 - sigmoid))
        up_grad = hidden_grad * silu
        pair = jnp.concatenate([gate_grad.astype(bf16), up_grad.astype(bf16)], axis=1)
        hiddens[span, :] = hidden
        pairs[span, :] = pair
        out_sum[span, :] += dot_transposed(hidden, down)
        grad_sum[span, :] += dot_transposed(pair, pair_weights)

    @pl.when(step == pl.num_programs(0) - 1)
    def _():
        out[...] = out_sum[...].astype(out.dtype)
        grad[...] = grad_sum[...].astype(grad.dtype)


def hidden_width(units):
    for width in (256, 384, 128):
        if units % width == 0:
            return width
    return units


def feed_forward(rows, cotangent, weights, width, kind, after):
    length, model = rows.shape
    steps = weights.shape[1] // (3 * width)
    whole = pl.BlockSpec((length, model), lambda i: (0, 0))
    sums = jax.ShapeDtypeStruct((length, model), kind)
    return pl.pallas_call(
        partial(ffn_body, width, len(after)),
        grid=(steps,),
        in_specs=[whole, whole, pl.BlockSpec((model, 3 * width), lambda i: (0, i))]
        + [anywhere()] * len(after),
        out_specs=[
            whole,
            whole,
            pl.BlockSpec((length, 2 * width), lambda i: (0, i)),
            pl.BlockSpec((length, width), lambda i: (0, i)),
        ],
        out_shape=[
            sums,
            sums,
            jax.ShapeDtypeStruct((length, steps * 2 * width), bf16),
            jax.ShapeDtypeStruct((length, steps * width), bf16),
        ],
        scratch_shapes=[
            pltpu.VMEM((length, model), f32),
            pltpu.VMEM((length, model), f32),
        ],
        compiler_params=pltpu.CompilerParams(vmem_limit_bytes=56 * 1024 * 1024),
        cost_estimate=pl.CostEstimate(
            flops=12 * length * model * steps * width,
            bytes_accessed=8 * model * steps * width,
            transcendentals=length * steps * width,
        ),
        name="feed_forward",
    )(rows, cotangent, weights, *after)


def lines(start, size):
    if isinstance(start, int):
        return pl.ds(start, size)
    return pl.ds(pl.multiple_of(start, size), size)


def part_starts(place, count, part_rows):
    if count == 1:
        return [0]
    return [place[0] * part_rows, (1 - place[0]) * part_rows]


def causal_block(size):
    keys = lax.broadcasted_iota(jnp.int32, (size, size), 0)
    queries = lax.broadcasted_iota(jnp.int32, (size, size), 1)
    return keys <= queries


def attend_body(count, *refs):
    place, weights, query_gain, key_gain, cosine, sine = refs[:6]
    rows_in = refs[6 : 6 + count]
    branches = refs[6 + count : 6 + 2 * count]
    attended_out = refs[6 + 2 * count : 6 + 3 * count]
    raw, query_rows, key_rows, value_rows, attended, log_totals = refs[6 + 3 * count : 12 + 3 * count]
    rows, turned = refs[12 + 3 * count :]
    part_rows = rows_in[0].shape[0]
    length = rows.shape[0]
    heads = query_rows.shape[0] // HD
    kv_heads = key_rows.shape[0] // HD
    group_size = heads // kv_heads
    columns = (heads + 2 * kv_heads) * HD
    half = HD // 2
    starts = part_starts(place, count, part_rows)
    for part in range(count):
        rows[lines(starts[part], part_rows), :] = rows_in[part][...]

    chunk = min(256, columns)
    for first in range(0, columns, chunk):
        product = dot_transposed(weights[:, first : first + chunk].T, rows[...])
        for at in range(0, chunk, HD):
            head = (first + at) // HD
            values = product[at : at + HD]
            if head >= heads + kv_heads:
                start = (head - heads - kv_heads) * HD
                value_rows[start : start + HD, :] = values.astype(bf16)
                continue
            raw[first + at : first + at + HD, :] = values
            gain = query_gain if head < heads else key_gain
            scale = lax.rsqrt(jnp.mean(values * values, axis=0, keepdims=True) + eps)
            normed = values * scale * gain[...]
            top, bottom = normed[:half], normed[half:]
            top, bottom = (
                top * cosine[...] - bottom * sine[...],
                bottom * cosine[...] + top * sine[...],
            )
            if head < heads:
                target, start = query_rows, head * HD
                top = top.astype(bf16).astype(f32) * HD**-0.5
                bottom = bottom.astype(bf16).astype(f32) * HD**-0.5
            else:
                target, start = key_rows, (head - heads) * HD
            target[start : start + half, :] = top.astype(bf16)
            target[start + half : start + HD, :] = bottom.astype(bf16)

    block = min(256, length)
    causal = causal_block(block)

    def one_group(kv_head, carry):
        span = lines(kv_head * HD, HD)
        keys = key_rows[span, :].T
        values = value_rows[span, :]
        for member in range(group_size):
            head = kv_head * group_size + member
            for start in range(0, length, block):
                here = slice(start, start + block)
                query = query_rows[lines(head * HD, HD), here]
                weight = jnp.where(causal, jnp.exp(dot(keys[here], query)), 0.0)
                total = jnp.sum(weight, axis=0, keepdims=True)
                result = dot(values[:, here], weight.astype(bf16))
                if start:
                    weight = jnp.exp(dot(keys[:start], query))
                    total = total + jnp.sum(weight, axis=0, keepdims=True)
                    result = result + dot(values[:, :start], weight.astype(bf16))
                attended[lines(head * HD, HD), here] = (result * (1.0 / total)).astype(bf16)
                log_totals[head, :, here] = jnp.log(total)
        return carry

    lax.fori_loop(0, kv_heads, one_group, 0)
    turned[...] = attended[...].T
    for part in range(count):
        mine = turned[lines(starts[part], part_rows), :]
        attended_out[part][...] = mine
        branches[part][...] = dot_transposed(mine, weights[:, columns:]).astype(branches[part].dtype)


def attend(place, weights, query_gain, key_gain, cosine, sine, parts, query_columns, key_columns):
    count = len(parts)
    part_rows, model = parts[0].shape
    length = count * part_rows
    heads = query_columns // HD
    shape = jax.ShapeDtypeStruct
    kinds = [f32] + [bf16] * (count - 1)
    vmem = pl.BlockSpec(memory_space=pltpu.VMEM)
    outs = (
        [shape((part_rows, model), kind) for kind in kinds]
        + [shape((part_rows, query_columns), bf16)] * count
        + [
            shape((query_columns + key_columns, length), f32),
            shape((query_columns, length), bf16),
            shape((key_columns, length), bf16),
            shape((key_columns, length), bf16),
            shape((query_columns, length), bf16),
            shape((heads, 1, length), f32),
        ]
    )
    results = pl.pallas_call(
        partial(attend_body, count),
        in_specs=[pl.BlockSpec(memory_space=pltpu.SMEM)] + [vmem] * (5 + count),
        out_specs=[vmem] * len(outs),
        out_shape=outs,
        scratch_shapes=[
            pltpu.VMEM((length, model), bf16),
            pltpu.VMEM((length, query_columns), bf16),
        ],
        compiler_params=pltpu.CompilerParams(vmem_limit_bytes=56 * 1024 * 1024),
        cost_estimate=pl.CostEstimate(
            flops=2 * length * model * (2 * query_columns + 2 * key_columns)
            + 8 * length * length * query_columns,
            bytes_accessed=16 * length * model,
            transcendentals=heads * length * length,
        ),
        name="attend",
    )(place, weights, query_gain, key_gain, cosine, sine, *parts)
    return results[:count], results[count : 2 * count], results[2 * count :]


def attend_back_body(count, stage, stages, extra, *refs):
    place, weights, query_gain, key_gain, cosine, sine = refs[:6]
    raw, query_rows, key_rows, value_rows, attended, log_totals = refs[6:12]
    branch_in = refs[12 : 12 + count]
    refs = refs[12 + count :]
    if stage:
        earlier = refs[:3]
        refs = refs[3:]
    refs = refs[extra:]
    last = stage == stages - 1
    if last:
        grads, raw_grads, refs = refs[:count], refs[count : 2 * count], refs[2 * count :]
        query_gain_grad, key_gain_grad, turned_grads = refs[:3]
        rows, attended_grad, key_sum, value_sum, straight = refs[3:]
    else:
        turned_grads, query_gain_grad, key_gain_grad = refs[:3]
        rows, attended_grad, key_sum, value_sum = refs[3:]
    part_rows = branch_in[0].shape[0]
    length = rows.shape[0]
    heads = query_rows.shape[0] // HD
    kv_heads = key_rows.shape[0] // HD
    group_size = heads // kv_heads
    columns = (heads + 2 * kv_heads) * HD
    half = HD // 2
    starts = part_starts(place, count, part_rows)
    for part in range(count):
        rows[lines(starts[part], part_rows), :] = branch_in[part][...]
    groups_here = kv_heads // stages
    stage_rows = groups_here * group_size * HD
    chunk = min(256, stage_rows)
    for first in range(stage * stage_rows, (stage + 1) * stage_rows, chunk):
        piece = weights[:, columns + first : columns + first + chunk].T
        attended_grad[first : first + chunk, :] = dot_transposed(piece, rows[...]).astype(bf16)
    if stage:
        turned_grads[...] = earlier[0][...]
        query_gain_grad[...] = earlier[1][...]
        key_gain_grad[...] = earlier[2][...]
    else:
        turned_grads[...] = jnp.zeros_like(turned_grads)
        query_gain_grad[...] = jnp.zeros_like(query_gain_grad)
        key_gain_grad[...] = jnp.zeros_like(key_gain_grad)
    block = min(256, length)
    causal = causal_block(block)

    def unprepare(grad, values, gain, gain_grad):
        top, bottom = grad[:half], grad[half:]
        grad = jnp.concatenate(
            [
                top * cosine[...] + bottom * sine[...],
                bottom * cosine[...] - top * sine[...],
            ],
            axis=0,
        )
        scale = lax.rsqrt(jnp.mean(values * values, axis=0, keepdims=True) + eps)
        normed = values * scale
        gain_grad[...] += jnp.sum(grad * normed, axis=1, keepdims=True)
        grad = grad * gain[...]
        inner = jnp.mean(grad * normed, axis=0, keepdims=True)
        return (scale * (grad - normed * inner)).astype(bf16)

    def one_group(kv_head, carry):
        span = lines(kv_head * HD, HD)
        keys_turned = key_rows[span, :]
        keys = keys_turned.T
        values = value_rows[span, :].T
        key_sum[...] = jnp.zeros_like(key_sum)
        value_sum[...] = jnp.zeros_like(value_sum)
        for member in range(group_size):
            head = kv_head * group_size + member
            head_span = lines(head * HD, HD)
            query_parts = []
            for start in range(0, length, block):
                here = slice(start, start + block)
                query = query_rows[head_span, here]
                grad = attended_grad[head_span, here]
                inner = jnp.sum(
                    grad.astype(f32) * attended[head_span, here].astype(f32), axis=0, keepdims=True
                )
                log_total = log_totals[head, :, here]
                query_grad = None
                for low, high in [(start, start + block)] + ([(0, start)] if start else []):
                    prob = jnp.exp(dot(keys[low:high], query) - log_total)
                    if low == start:
                        prob = jnp.where(causal, prob, 0.0)
                    prob_grad = dot(values[low:high], grad)
                    score_grad = (prob * (prob_grad - inner)).astype(bf16)
                    piece = dot(keys_turned[:, low:high], score_grad)
                    query_grad = piece if query_grad is None else query_grad + piece
                    key_sum[:, low:high] += dot_transposed(query, score_grad)
                    value_sum[:, low:high] += dot_transposed(grad, prob.astype(bf16))
                query_parts.append(query_grad * HD**-0.5)
            turned_grads[head_span, :] = unprepare(
                jnp.concatenate(query_parts, axis=1), raw[head_span, :], query_gain, query_gain_grad
            )
        key_span = lines((heads + kv_head) * HD, HD)
        turned_grads[key_span, :] = unprepare(
            key_sum[...], raw[key_span, :], key_gain, key_gain_grad
        )
        turned_grads[lines((heads + kv_heads + kv_head) * HD, HD), :] = value_sum[...].astype(bf16)
        return carry

    lax.fori_loop(stage * groups_here, (stage + 1) * groups_here, one_group, 0)
    if last:
        straight[...] = turned_grads[...].T
        for part in range(count):
            mine = straight[lines(starts[part], part_rows), :]
            raw_grads[part][...] = mine
            grads[part][...] = dot_transposed(mine, weights[:, :columns]).astype(grads[part].dtype)


def back_stages(kept):
    return 2 if kept[2].shape[0] // HD % 2 == 0 else 1


def attend_back(fixed, kept, parts, stage, earlier, after):
    count = len(parts)
    stages = back_stages(kept)
    part_rows, model = parts[0].shape
    length = count * part_rows
    query_columns = kept[1].shape[0]
    columns = query_columns + 2 * kept[2].shape[0]
    shape = jax.ShapeDtypeStruct
    vmem = pl.BlockSpec(memory_space=pltpu.VMEM)
    last = stage == stages - 1
    gains = [shape((HD, 1), f32)] * 2
    turned = shape((columns, length), bf16)
    scratch = [
        pltpu.VMEM((length, model), bf16),
        pltpu.VMEM((query_columns, length), bf16),
        pltpu.VMEM((HD, length), f32),
        pltpu.VMEM((HD, length), f32),
    ]
    if last:
        outs = (
            [shape((part_rows, model), kind) for kind in [f32] + [bf16] * (count - 1)]
            + [shape((part_rows, columns), bf16)] * count
            + gains
        )
        scratch = [pltpu.VMEM(turned.shape, bf16)] + scratch + [pltpu.VMEM((length, columns), bf16)]
    else:
        outs = [turned] + gains
    results = pl.pallas_call(
        partial(attend_back_body, count, stage, stages, len(after)),
        in_specs=[pl.BlockSpec(memory_space=pltpu.SMEM)]
        + [vmem] * (11 + count + len(earlier))
        + [anywhere()] * len(after),
        out_specs=[vmem] * len(outs),
        out_shape=outs,
        scratch_shapes=scratch,
        compiler_params=pltpu.CompilerParams(vmem_limit_bytes=56 * 1024 * 1024),
        cost_estimate=pl.CostEstimate(
            flops=(
                2 * length * model * (query_columns + columns)
                + 20 * length * length * query_columns
            )
            // stages,
            bytes_accessed=16 * length * model,
            transcendentals=query_columns // HD * length * length // stages,
        ),
        name="attend_back",
    )(*fixed, *kept, *parts, *earlier, *after)
    if not last:
        return results
    return results[:count], results[count : 2 * count], results[2 * count], results[2 * count + 1]


def on_device(
    tokens,
    out_cotangent,
    attn_gain,
    query_weight,
    key_weight,
    value_weight,
    query_gain,
    key_gain,
    out_weight,
    ffn_gain,
    gate_weight,
    up_weight,
    down_weight,
):
    shard, query_columns = query_weight.shape
    key_columns = key_weight.shape[1]
    qkv_columns = query_columns + 2 * key_columns
    units = gate_weight.shape[1]
    width = hidden_width(units)
    steps = units // width
    attn_shard = jnp.concatenate([query_weight, key_weight, value_weight, out_weight.T], axis=1)
    ffn_shard = jnp.stack(
        [
            gate_weight.reshape(shard, steps, width),
            up_weight.reshape(shard, steps, width),
            down_weight.T.reshape(shard, steps, width),
        ],
        axis=2,
    ).reshape(shard, 3 * units)
    attn_full = gather_ring(attn_shard)
    ffn_full = lax.all_gather(ffn_shard, "fsdp", axis=0, tiled=True)

    residual = tokens.astype(f32)
    normed, attn_norm_pull = jax.vjp(rms_norm, residual, attn_gain)
    normed_parts = widen(normed.astype(bf16))
    cotangent_parts = widen(out_cotangent)
    length = len(normed_parts) * normed_parts[0].shape[0]
    cosine, sine = rotary_tables(length)
    place = lax.axis_index("tp").astype(jnp.int32).reshape(1)
    fixed = (place, attn_full, query_gain[:, None], key_gain[:, None], cosine, sine)
    branch, attended, kept = attend(*fixed, normed_parts, query_columns, key_columns)
    middle = residual + narrow(branch)
    normed_ffn, ffn_norm_pull = jax.vjp(rms_norm, middle, ffn_gain)
    ffn_parts = widen(normed_ffn.astype(bf16))
    results = []
    for at in reversed(range(len(ffn_parts))):
        after = [results[-1][1]] if results else []
        results.append(
            feed_forward(
                ffn_parts[at], cotangent_parts[at], ffn_full, width, bf16 if at else f32, after
            )
        )
    out_parts, grad_parts, pairs, hiddens = (list(item) for item in zip(*results[::-1]))
    ffn_normed_grad = narrow(grad_parts)
    middle_piece, ffn_gain_local = ffn_norm_pull(ffn_normed_grad)
    middle_grad = out_cotangent.astype(f32) + middle_piece
    branch_parts = widen(middle_grad.astype(bf16))

    ffn_blocks = weight_grads(
        ffn_parts,
        cotangent_parts,
        pairs,
        hiddens,
        steps,
        (branch_parts[0],),
        branch_parts[1:],
    )
    ffn_state, sent = ring_open(ffn_blocks)
    ffn_next, attn_next, last = 1, 1, ring_size() // 2
    stages = back_stages(kept)
    back = ()
    for stage in range(stages):
        back = attend_back(fixed, kept, branch_parts, stage, back, sent)
        done = back[1] if stage < stages - 1 else back[2]
        if stage == 0:
            out_parts[-1] = held(out_parts[-1], (done,))
        if ffn_next < last:
            ffn_state, sent = ring_step(ffn_blocks, ffn_next, ffn_state, (done,))
            ffn_next += 1
    output = (middle + narrow(out_parts)).astype(bf16)
    normed_grad, qkv_grad, query_gain_local, key_gain_local = back
    normed_grad = narrow([*normed_grad[:-1], held(normed_grad[-1], sent)])
    attn_blocks = weight_grads(normed_parts, branch_parts, qkv_grad, attended, 1, sent)
    attn_state, sent = ring_open(attn_blocks)
    while ffn_next < last or attn_next < last:
        if attn_next < last:
            attn_state, sent = ring_step(attn_blocks, attn_next, attn_state, sent)
            attn_next += 1
        if ffn_next < last:
            ffn_state, sent = ring_step(ffn_blocks, ffn_next, ffn_state, sent)
            ffn_next += 1
    ffn_pieces = [
        (step * 3 * width + number * width, width, number, step * width, number == 2)
        for step in range(steps)
        for number in range(3)
    ]
    gate_grad, up_grad, down_grad = ring_close(ffn_blocks, ffn_state, ffn_pieces)
    attn_pieces = [
        (0, query_columns, 0, 0, False),
        (query_columns, key_columns, 1, 0, False),
        (query_columns + key_columns, key_columns, 2, 0, False),
        (qkv_columns, query_columns, 3, 0, True),
    ]
    query_grad, key_grad, value_grad, out_grad = ring_close(attn_blocks, attn_state, attn_pieces)
    tokens_piece, attn_gain_local = attn_norm_pull(normed_grad)
    tokens_grad = middle_grad + tokens_piece
    model = attn_gain.shape[0]
    gain_totals = sum_everywhere(
        jnp.concatenate([attn_gain_local, ffn_gain_local, query_gain_local[:, 0], key_gain_local[:, 0]])
    )
    return (
        output,
        tokens_grad,
        gain_totals[:model],
        query_grad,
        key_grad,
        value_grad,
        gain_totals[2 * model : 2 * model + HD],
        gain_totals[2 * model + HD :],
        out_grad,
        gain_totals[model : 2 * model],
        gate_grad,
        up_grad,
        down_grad,
    )


def solution(mesh):
    placed = (
        P(("fsdp", "tp"), None),
        P(("fsdp", "tp"), None),
        P(),
        P("fsdp", "tp"),
        P("fsdp", "tp"),
        P("fsdp", "tp"),
        P(),
        P(),
        P("tp", "fsdp"),
        P(),
        P("fsdp", "tp"),
        P("fsdp", "tp"),
        P("tp", "fsdp"),
    )
    return jax.shard_map(
        on_device,
        mesh=mesh,
        in_specs=placed,
        out_specs=(
            P(("fsdp", "tp"), None),
            P(("fsdp", "tp"), None),
            P(),
            P("fsdp", "tp"),
            P("fsdp", "tp"),
            P("fsdp", "tp"),
            P(),
            P(),
            P("tp", "fsdp"),
            P(),
            P("fsdp", "tp"),
            P("fsdp", "tp"),
            P("tp", "fsdp"),
        ),
        check_vma=False,
    )
```

```python
from functools import partial

import jax
import jax.numpy as jnp
from jax import lax
from jax.experimental import pallas as pl
from jax.experimental.pallas import tpu as pltpu
from jax.sharding import PartitionSpec as P

HD = 64

eps = 1e-05
theta_base = 1000000.0
f32 = jnp.float32
bf16 = jnp.bfloat16


def rms_norm(values, gain):
    return values * lax.rsqrt(jnp.mean(values * values, axis=-1, keepdims=True) + eps) * gain


def rotary_tables(length):
    half_size = HD // 2
    frequency = theta_base ** (-jnp.arange(half_size, dtype=f32) * 2.0 / HD)
    angles = frequency[:, None] * jnp.arange(length, dtype=f32)[None, :]
    return (jnp.cos(angles), jnp.sin(angles))


def dot(former, latter):
    return jnp.dot(former, latter, preferred_element_type=f32)


def dot_transposed(former, latter):
    return lax.dot_general(former, latter, (((1,), (1,)), ((), ())), preferred_element_type=f32)


def dot_leading(former, latter):
    return lax.dot_general(former, latter, (((0,), (0,)), ((), ())), preferred_element_type=f32)


def swap(values, axis_name, bit=1):
    count = lax.axis_size(axis_name)
    return lax.ppermute(values, axis_name, [(i, i ^ bit) for i in range(count)])


def widen(rows):
    if lax.axis_size("tp") == 2:
        return (rows, swap(rows, "tp"))
    return (lax.all_gather(rows, "tp", axis=0, tiled=True),)


def narrow_send(part):
    return swap(part.astype(bf16), "tp")


def narrow(parts):
    if len(parts) == 2:
        return parts[0].astype(f32) + narrow_send(parts[1]).astype(f32)
    return lax.psum_scatter(
        parts[0].astype(bf16), "tp", scatter_dimension=0, tiled=True
    ).astype(f32)


def sum_everywhere(values):
    count, chips = lax.axis_size("tp"), ring_size()
    terms = [values]
    for step in range(1, count):
        terms.append(lax.ppermute(values, "tp", [(i, (i + step) % count) for i in range(count)]))
    values = sum(terms[1:], terms[0])
    values = values + swap(values, "fsdp")
    return sum([pass_on(values, step) for step in range(1, chips)], values)


def ring_size():
    return lax.axis_size("fsdp") // 2


def chip_at(place):
    chips = ring_size()
    if isinstance(place, int):
        return 2 * place if place < chips // 2 else 2 * (chips - 1 - place) + 1
    return jnp.where(place < chips // 2, 2 * place, 2 * (chips - 1 - place) + 1)


def own_place():
    chip = lax.axis_index("fsdp") // 2
    return jnp.where(chip % 2 == 0, chip // 2, ring_size() - 1 - chip // 2)


def pass_on(values, direction):
    chips = ring_size()
    pairs = [
        (2 * chip_at(place) + core, 2 * chip_at((place + direction) % chips) + core)
        for place in range(chips)
        for core in range(2)
    ]
    return lax.ppermute(values, "fsdp", pairs)


def shard_table(ahead):
    core = lax.axis_index("fsdp") % 2
    chips = chip_at((own_place() + jnp.array(ahead, jnp.int32)) % ring_size())
    return jnp.concatenate([2 * chips + core, 2 * chips + 1 - core]).astype(jnp.int32)


def assemble_body(count, table, *refs):
    whole = refs[count]
    rows = refs[0].shape[0]
    for at in range(count):
        start = pl.multiple_of(table[at] * rows, rows)
        whole[pl.ds(start, rows), :] = refs[at][...]


def gather_ring(shard):
    chips = ring_size()
    ahead = [0]
    blocks = [shard]
    down = up = shard
    for step in range(1, chips // 2 + 1):
        down = pass_on(down, 1)
        ahead.append(chips - step)
        blocks.append(down)
        if step < chips // 2:
            up = pass_on(up, -1)
            ahead.append(step)
            blocks.append(up)
    blocks = blocks + [swap(block, "fsdp") for block in blocks]
    rows, columns = shard.shape
    count = len(blocks)
    vmem = pl.BlockSpec(memory_space=pltpu.VMEM)
    return pl.pallas_call(
        partial(assemble_body, count),
        in_specs=[pl.BlockSpec(memory_space=pltpu.SMEM)] + [vmem] * count,
        out_specs=vmem,
        out_shape=jax.ShapeDtypeStruct((count * rows, columns), shard.dtype),
        compiler_params=pltpu.CompilerParams(vmem_limit_bytes=48 * 1024 * 1024),
        name="assemble",
    )(shard_table(ahead), *blocks)


def ring_groups():
    chips = ring_size()
    middle = [[chips // 2 - step, chips // 2 + step] for step in range(1, chips // 2)]
    return [[chips // 2]] + middle + [[0]]


def anywhere():
    return pl.BlockSpec(memory_space=pl.ANY)


def held(values, after):
    return pl.pallas_call(
        lambda *refs: None,
        in_specs=[anywhere()] * (1 + len(after)),
        out_specs=anywhere(),
        out_shape=jax.ShapeDtypeStruct(values.shape, values.dtype),
        input_output_aliases={0: 0},
        name="held",
    )(values, *after)


def weight_grad_body(parts, groups, rows, extra, *refs):
    table = refs[0]
    first_in = refs[1 : 1 + parts]
    second_in = refs[1 + parts : 1 + 2 * parts]
    first_grads = refs[1 + 2 * parts : 1 + 3 * parts]
    second_grads = refs[1 + 3 * parts : 1 + 4 * parts]
    outs = refs[1 + 4 * parts + extra : -3]
    first_turned, second_turned, total = refs[-3:]
    part_rows = first_in[0].shape[0]
    first_width = first_grads[0].shape[1]

    @pl.when(pl.program_id(0) == 0)
    def _():
        for part in range(parts):
            span = pl.ds(part * part_rows, part_rows)
            first_turned[:, span] = first_in[part][...].T
            second_turned[:, span] = second_in[part][...].T

    def joined(pieces):
        if parts == 1:
            return pieces[0][...]
        return jnp.concatenate([piece[...] for piece in pieces], axis=0)

    total[:, :first_width] = dot(first_turned[...], joined(first_grads)).astype(bf16)
    total[:, first_width:] = dot(second_turned[...], joined(second_grads)).astype(bf16)
    count = sum(len(group) for group in groups)
    at = 0
    for number, group in enumerate(groups):
        for member in range(len(group)):
            mine = pl.multiple_of(table[at] * rows, rows)
            outs[number][member] = total[pl.ds(mine, rows), :]
            near = pl.multiple_of(table[count + at] * rows, rows)
            outs[len(groups) + number][member] = total[pl.ds(near, rows), :]
            at += 1


def weight_grads(first, second, first_grads, second_grads, steps, after, before=()):
    parts = len(first)
    part_rows, model = first[0].shape
    length = parts * part_rows
    first_width = first_grads[0].shape[1] // steps
    second_width = second_grads[0].shape[1] // steps
    width = first_width + second_width
    groups = ring_groups()
    count = 2 * ring_size()
    rows = model // count
    table = shard_table([place for group in groups for place in group])
    whole = pl.BlockSpec((part_rows, model), lambda i: (0, 0))
    outs = [jax.ShapeDtypeStruct((len(group), rows, steps * width), bf16) for group in groups] * 2
    out_specs = [
        pl.BlockSpec((len(group), rows, width), lambda i: (0, 0, i)) for group in groups
    ] * 2
    results = pl.pallas_call(
        partial(weight_grad_body, parts, groups, rows, len(after)),
        grid=(steps,),
        in_specs=[pl.BlockSpec(memory_space=pltpu.SMEM)]
        + [whole] * (2 * parts)
        + [pl.BlockSpec((part_rows, first_width), lambda i: (0, i))] * parts
        + [pl.BlockSpec((part_rows, second_width), lambda i: (0, i))] * parts
        + [anywhere()] * len(after),
        out_specs=out_specs,
        out_shape=outs,
        scratch_shapes=[
            pltpu.VMEM((model, length), bf16),
            pltpu.VMEM((model, length), bf16),
            pltpu.VMEM((model, width), bf16),
        ],
        compiler_params=pltpu.CompilerParams(vmem_limit_bytes=56 * 1024 * 1024),
        cost_estimate=pl.CostEstimate(
            flops=2 * length * model * steps * width,
            bytes_accessed=4 * model * steps * width,
            transcendentals=0,
        ),
        name="weight_grads",
    )(table, *first, *second, *first_grads, *second_grads, *after)
    mine = results[: len(groups)]
    near = list(results[len(groups) :])
    if before:
        near[0] = held(near[0], before)
    near = [swap(block, "fsdp") for block in near]
    return mine, near


def ring_call(body, operands, outs, after, name):
    vmem = pl.BlockSpec(memory_space=pltpu.VMEM)
    return pl.pallas_call(
        body,
        in_specs=[vmem] * len(operands) + [anywhere()] * len(after),
        out_specs=[vmem] * len(outs),
        out_shape=outs,
        compiler_params=pltpu.CompilerParams(vmem_limit_bytes=48 * 1024 * 1024),
        name=name,
    )(*operands, *after)


def both_cores(mine, near, member):
    return mine[member].astype(f32) + near[member].astype(f32)


def open_body(cut, mine, near, *refs):
    low, high = refs[-2:]
    total = both_cores(mine, near, 0).astype(bf16)
    low[...] = total[:, :cut]
    high[...] = total[:, cut:]


def step_body(cut, mine, near, down, up, *refs):
    ahead, behind = refs[-2:]
    columns = ahead.shape[1]
    ahead_sum = both_cores(mine, near, 0)
    behind_sum = both_cores(mine, near, 1)
    if down.shape[1] == columns:
        ahead[...] = (ahead_sum + down[...].astype(f32)).astype(bf16)
        behind[...] = (behind_sum + up[...].astype(f32)).astype(bf16)
    else:
        ahead[:, :cut] = (ahead_sum[:, :cut] + down[...].astype(f32)).astype(bf16)
        ahead[:, cut:] = ahead_sum[:, cut:].astype(bf16)
        behind[:, :cut] = behind_sum[:, :cut].astype(bf16)
        behind[:, cut:] = (behind_sum[:, cut:] + up[...].astype(f32)).astype(bf16)


def close_body(pieces, mine, near, down, up, *outs):
    total = both_cores(mine, near, 0) + down[...].astype(f32) + up[...].astype(f32)
    for start, width, number, place, turn in pieces:
        values = total[:, start : start + width]
        if turn:
            outs[number][place : place + width, :] = values.T
        else:
            outs[number][:, place : place + width] = values


def ring_cut(columns):
    return columns // 2 // 128 * 128


def ring_pass(sums):
    return pass_on(sums[0], 1), pass_on(sums[1], -1)


def ring_open(blocks, after=()):
    mine, near = blocks
    rows, columns = mine[0].shape[1:]
    cut = ring_cut(columns)
    outs = [jax.ShapeDtypeStruct((rows, width), bf16) for width in (cut, columns - cut)]
    sums = ring_call(partial(open_body, cut), (mine[0], near[0]), outs, after, "ring_open")
    return ring_pass(sums), tuple(sums)


def ring_step(blocks, number, state, after=()):
    mine, near = blocks[0][number], blocks[1][number]
    rows, columns = mine.shape[1:]
    outs = [jax.ShapeDtypeStruct((rows, columns), bf16)] * 2
    body = partial(step_body, ring_cut(columns))
    sums = ring_call(body, (mine, near, *state), outs, after, "ring_step")
    return ring_pass(sums), tuple(sums)


def ring_close(blocks, state, pieces):
    mine, near = blocks[0][-1], blocks[1][-1]
    rows = mine.shape[1]
    in_kernel = all(width % 128 == 0 for _, width, _, _, turn in pieces if turn)
    sizes, turns = {}, {}
    for _, width, number, place, turn in pieces:
        sizes[number] = max(sizes.get(number, 0), place + width)
        turns[number] = turn
    if not in_kernel:
        pieces = [piece[:4] + (False,) for piece in pieces]
    outs = [
        jax.ShapeDtypeStruct(
            (sizes[number], rows) if turns[number] and in_kernel else (rows, sizes[number]), f32
        )
        for number in range(len(sizes))
    ]
    results = ring_call(
        partial(close_body, pieces), (mine, near, *state), outs, (), "ring_close"
    )
    return [
        result.T if turns[number] and not in_kernel else result
        for number, result in enumerate(results)
    ]


def ffn_body(width, extra, *refs):
    rows_in, cotangent_in, weights = refs[:3]
    out, grad, pairs, hiddens, out_sum, grad_sum = refs[3 + extra :]
    step = pl.program_id(0)
    length = rows_in.shape[0]

    @pl.when(step == 0)
    def _():
        out_sum[...] = jnp.zeros_like(out_sum)
        grad_sum[...] = jnp.zeros_like(grad_sum)

    pair_weights = weights[:, : 2 * width]
    down = weights[:, 2 * width :]
    chunk = min(256, length)
    for start in range(0, length, chunk):
        span = pl.ds(start, chunk)
        both = dot(rows_in[span, :], pair_weights)
        gate = both[:, :width]
        up = both[:, width:]
        hidden_grad = dot(cotangent_in[span, :], down)
        sigmoid = 1.0 / (1.0 + jnp.exp(-gate))
        silu = gate * sigmoid
        hidden = (silu * up).astype(bf16)
        gate_grad = hidden_grad * up * sigmoid * (1.0 + gate * (1.0 - sigmoid))
        up_grad = hidden_grad * silu
        pair = jnp.concatenate([gate_grad.astype(bf16), up_grad.astype(bf16)], axis=1)
        hiddens[span, :] = hidden
        pairs[span, :] = pair
        out_sum[span, :] += dot_transposed(hidden, down)
        grad_sum[span, :] += dot_transposed(pair, pair_weights)

    @pl.when(step == pl.num_programs(0) - 1)
    def _():
        out[...] = out_sum[...].astype(out.dtype)
        grad[...] = grad_sum[...].astype(grad.dtype)


def hidden_width(units):
    for width in (768, 256, 384, 128):
        if units % width == 0:
            return width
    return units


def feed_forward(rows, cotangent, weights, width, kind, after):
    length, model = rows.shape
    steps = weights.shape[1] // (3 * width)
    whole = pl.BlockSpec((length, model), lambda i: (0, 0))
    sums = jax.ShapeDtypeStruct((length, model), kind)
    return pl.pallas_call(
        partial(ffn_body, width, len(after)),
        grid=(steps,),
        in_specs=[whole, whole, pl.BlockSpec((model, 3 * width), lambda i: (0, i))]
        + [anywhere()] * len(after),
        out_specs=[
            whole,
            whole,
            pl.BlockSpec((length, 2 * width), lambda i: (0, i)),
            pl.BlockSpec((length, width), lambda i: (0, i)),
        ],
        out_shape=[
            sums,
            sums,
            jax.ShapeDtypeStruct((length, steps * 2 * width), bf16),
            jax.ShapeDtypeStruct((length, steps * width), bf16),
        ],
        scratch_shapes=[
            pltpu.VMEM((length, model), f32),
            pltpu.VMEM((length, model), f32),
        ],
        compiler_params=pltpu.CompilerParams(vmem_limit_bytes=56 * 1024 * 1024),
        cost_estimate=pl.CostEstimate(
            flops=12 * length * model * steps * width,
            bytes_accessed=8 * model * steps * width,
            transcendentals=length * steps * width,
        ),
        name="feed_forward",
    )(rows, cotangent, weights, *after)


def lines(start, size):
    if isinstance(start, int):
        return pl.ds(start, size)
    return pl.ds(pl.multiple_of(start, size), size)


def part_starts(place, count, part_rows):
    if count == 1:
        return [0]
    return [place[0] * part_rows, (1 - place[0]) * part_rows]


def causal_block(size):
    keys = lax.broadcasted_iota(jnp.int32, (size, size), 0)
    queries = lax.broadcasted_iota(jnp.int32, (size, size), 1)
    return keys <= queries


def attend_body(count, *refs):
    place, weights, query_gain, key_gain, cosine, sine = refs[:6]
    rows_in = refs[6 : 6 + count]
    branches = refs[6 + count : 6 + 2 * count]
    attended_out = refs[6 + 2 * count : 6 + 3 * count]
    raw, query_rows, key_rows, value_rows, attended, log_totals = refs[6 + 3 * count : 12 + 3 * count]
    rows, turned = refs[12 + 3 * count :]
    part_rows = rows_in[0].shape[0]
    length = rows.shape[0]
    heads = query_rows.shape[0] // HD
    kv_heads = key_rows.shape[0] // HD
    group_size = heads // kv_heads
    columns = (heads + 2 * kv_heads) * HD
    half = HD // 2
    starts = part_starts(place, count, part_rows)
    for part in range(count):
        rows[lines(starts[part], part_rows), :] = rows_in[part][...]

    chunk = min(256, columns)
    for first in range(0, columns, chunk):
        product = dot_transposed(weights[:, first : first + chunk].T, rows[...])
        for at in range(0, chunk, HD):
            head = (first + at) // HD
            values = product[at : at + HD]
            if head >= heads + kv_heads:
                start = (head - heads - kv_heads) * HD
                value_rows[start : start + HD, :] = values.astype(bf16)
                continue
            raw[first + at : first + at + HD, :] = values
            gain = query_gain if head < heads else key_gain
            scale = lax.rsqrt(jnp.mean(values * values, axis=0, keepdims=True) + eps)
            normed = values * scale * gain[...]
            top, bottom = normed[:half], normed[half:]
            top, bottom = (
                top * cosine[...] - bottom * sine[...],
                bottom * cosine[...] + top * sine[...],
            )
            if head < heads:
                target, start = query_rows, head * HD
                top = top.astype(bf16).astype(f32) * HD**-0.5
                bottom = bottom.astype(bf16).astype(f32) * HD**-0.5
            else:
                target, start = key_rows, (head - heads) * HD
            target[start : start + half, :] = top.astype(bf16)
            target[start + half : start + HD, :] = bottom.astype(bf16)

    block = min(256, length)
    causal = causal_block(block)

    def one_group(kv_head, carry):
        span = lines(kv_head * HD, HD)
        keys = key_rows[span, :].T
        values = value_rows[span, :]
        for member in range(group_size):
            head = kv_head * group_size + member
            for start in range(0, length, block):
                here = slice(start, start + block)
                query = query_rows[lines(head * HD, HD), here]
                weight = jnp.where(causal, jnp.exp(dot(keys[here], query)), 0.0)
                total = jnp.sum(weight, axis=0, keepdims=True)
                result = dot(values[:, here], weight.astype(bf16))
                if start:
                    weight = jnp.exp(dot(keys[:start], query))
                    total = total + jnp.sum(weight, axis=0, keepdims=True)
                    result = result + dot(values[:, :start], weight.astype(bf16))
                attended[lines(head * HD, HD), here] = (result * (1.0 / total)).astype(bf16)
                log_totals[head, :, here] = jnp.log(total)
        return carry

    lax.fori_loop(0, kv_heads, one_group, 0)
    turned[...] = attended[...].T
    for part in range(count):
        mine = turned[lines(starts[part], part_rows), :]
        attended_out[part][...] = mine
        branches[part][...] = dot_transposed(mine, weights[:, columns:]).astype(branches[part].dtype)


def attend(place, weights, query_gain, key_gain, cosine, sine, parts, query_columns, key_columns):
    count = len(parts)
    part_rows, model = parts[0].shape
    length = count * part_rows
    heads = query_columns // HD
    shape = jax.ShapeDtypeStruct
    kinds = [f32] + [bf16] * (count - 1)
    vmem = pl.BlockSpec(memory_space=pltpu.VMEM)
    outs = (
        [shape((part_rows, model), kind) for kind in kinds]
        + [shape((part_rows, query_columns), bf16)] * count
        + [
            shape((query_columns + key_columns, length), f32),
            shape((query_columns, length), bf16),
            shape((key_columns, length), bf16),
            shape((key_columns, length), bf16),
            shape((query_columns, length), bf16),
            shape((heads, 1, length), f32),
        ]
    )
    results = pl.pallas_call(
        partial(attend_body, count),
        in_specs=[pl.BlockSpec(memory_space=pltpu.SMEM)] + [vmem] * (5 + count),
        out_specs=[vmem] * len(outs),
        out_shape=outs,
        scratch_shapes=[
            pltpu.VMEM((length, model), bf16),
            pltpu.VMEM((length, query_columns), bf16),
        ],
        compiler_params=pltpu.CompilerParams(vmem_limit_bytes=56 * 1024 * 1024),
        cost_estimate=pl.CostEstimate(
            flops=2 * length * model * (2 * query_columns + 2 * key_columns)
            + 8 * length * length * query_columns,
            bytes_accessed=16 * length * model,
            transcendentals=heads * length * length,
        ),
        name="attend",
    )(place, weights, query_gain, key_gain, cosine, sine, *parts)
    return results[:count], results[count : 2 * count], results[2 * count :]


def attend_back_body(count, first_group, last_group, extra, *refs):
    place, weights, query_gain, key_gain, cosine, sine = refs[:6]
    raw, query_rows, key_rows, value_rows, attended, log_totals = refs[6:12]
    branch_in = refs[12 : 12 + count]
    refs = refs[12 + count :]
    if first_group:
        earlier = refs[:3]
        refs = refs[3:]
    refs = refs[extra:]
    last = last_group * HD == key_rows.shape[0]
    if last:
        grads, raw_grads, refs = refs[:count], refs[count : 2 * count], refs[2 * count :]
        query_gain_grad, key_gain_grad, turned_grads = refs[:3]
        rows, attended_grad, key_sum, value_sum, straight = refs[3:]
    else:
        turned_grads, query_gain_grad, key_gain_grad = refs[:3]
        rows, attended_grad, key_sum, value_sum = refs[3:]
    part_rows = branch_in[0].shape[0]
    length = rows.shape[0]
    heads = query_rows.shape[0] // HD
    kv_heads = key_rows.shape[0] // HD
    group_size = heads // kv_heads
    columns = (heads + 2 * kv_heads) * HD
    half = HD // 2
    starts = part_starts(place, count, part_rows)
    for part in range(count):
        rows[lines(starts[part], part_rows), :] = branch_in[part][...]
    stage_rows = (last_group - first_group) * group_size * HD
    chunk = min(256, stage_rows)
    begin = first_group * group_size * HD
    for first in range(begin, begin + stage_rows, chunk):
        piece = weights[:, columns + first : columns + first + chunk].T
        attended_grad[first : first + chunk, :] = dot_transposed(piece, rows[...]).astype(bf16)
    if first_group:
        turned_grads[...] = earlier[0][...]
        query_gain_grad[...] = earlier[1][...]
        key_gain_grad[...] = earlier[2][...]
    else:
        turned_grads[...] = jnp.zeros_like(turned_grads)
        query_gain_grad[...] = jnp.zeros_like(query_gain_grad)
        key_gain_grad[...] = jnp.zeros_like(key_gain_grad)
    block = min(256, length)
    causal = causal_block(block)

    def unprepare(grad, values, gain, gain_grad):
        top, bottom = grad[:half], grad[half:]
        grad = jnp.concatenate(
            [
                top * cosine[...] + bottom * sine[...],
                bottom * cosine[...] - top * sine[...],
            ],
            axis=0,
        )
        scale = lax.rsqrt(jnp.mean(values * values, axis=0, keepdims=True) + eps)
        normed = values * scale
        gain_grad[...] += jnp.sum(grad * normed, axis=1, keepdims=True)
        grad = grad * gain[...]
        inner = jnp.mean(grad * normed, axis=0, keepdims=True)
        return (scale * (grad - normed * inner)).astype(bf16)

    def one_group(kv_head, carry):
        span = lines(kv_head * HD, HD)
        keys_turned = key_rows[span, :]
        keys = keys_turned.T
        values = value_rows[span, :].T
        key_sum[...] = jnp.zeros_like(key_sum)
        value_sum[...] = jnp.zeros_like(value_sum)
        for member in range(group_size):
            head = kv_head * group_size + member
            head_span = lines(head * HD, HD)
            query_parts = []
            for start in range(0, length, block):
                here = slice(start, start + block)
                query = query_rows[head_span, here]
                grad = attended_grad[head_span, here]
                inner = jnp.sum(
                    grad.astype(f32) * attended[head_span, here].astype(f32), axis=0, keepdims=True
                )
                log_total = log_totals[head, :, here]
                query_grad = None
                for low, high in [(start, start + block)] + ([(0, start)] if start else []):
                    prob = jnp.exp(dot(keys[low:high], query) - log_total)
                    if low == start:
                        prob = jnp.where(causal, prob, 0.0)
                    prob_grad = dot(values[low:high], grad)
                    score_grad = (prob * (prob_grad - inner)).astype(bf16)
                    piece = dot(keys_turned[:, low:high], score_grad)
                    query_grad = piece if query_grad is None else query_grad + piece
                    key_sum[:, low:high] += dot_transposed(query, score_grad)
                    value_sum[:, low:high] += dot_transposed(grad, prob.astype(bf16))
                query_parts.append(query_grad * HD**-0.5)
            turned_grads[head_span, :] = unprepare(
                jnp.concatenate(query_parts, axis=1), raw[head_span, :], query_gain, query_gain_grad
            )
        key_span = lines((heads + kv_head) * HD, HD)
        turned_grads[key_span, :] = unprepare(
            key_sum[...], raw[key_span, :], key_gain, key_gain_grad
        )
        turned_grads[lines((heads + kv_heads + kv_head) * HD, HD), :] = value_sum[...].astype(bf16)
        return carry

    lax.fori_loop(first_group, last_group, one_group, 0)
    if last:
        straight[...] = turned_grads[...].T
        for part in range(count):
            mine = straight[lines(starts[part], part_rows), :]
            raw_grads[part][...] = mine
            grads[part][...] = dot_transposed(mine, weights[:, :columns]).astype(grads[part].dtype)


def back_stages(kept):
    kv_heads = kept[2].shape[0] // HD
    if kv_heads % 4:
        return [(0, kv_heads)]
    quarter = kv_heads // 4
    return [(0, quarter), (quarter, 3 * quarter), (3 * quarter, kv_heads)]


def attend_back(fixed, kept, parts, stage, earlier, after):
    count = len(parts)
    first_group, last_group = stage
    kv_heads = kept[2].shape[0] // HD
    part_rows, model = parts[0].shape
    length = count * part_rows
    query_columns = kept[1].shape[0]
    columns = query_columns + 2 * kept[2].shape[0]
    shape = jax.ShapeDtypeStruct
    vmem = pl.BlockSpec(memory_space=pltpu.VMEM)
    last = last_group == kv_heads
    share = kv_heads // (last_group - first_group)
    gains = [shape((HD, 1), f32)] * 2
    turned = shape((columns, length), bf16)
    scratch = [
        pltpu.VMEM((length, model), bf16),
        pltpu.VMEM((query_columns, length), bf16),
        pltpu.VMEM((HD, length), f32),
        pltpu.VMEM((HD, length), f32),
    ]
    if last:
        outs = (
            [shape((part_rows, model), kind) for kind in [f32] + [bf16] * (count - 1)]
            + [shape((part_rows, columns), bf16)] * count
            + gains
        )
        scratch = [pltpu.VMEM(turned.shape, bf16)] + scratch + [pltpu.VMEM((length, columns), bf16)]
    else:
        outs = [turned] + gains
    results = pl.pallas_call(
        partial(attend_back_body, count, first_group, last_group, len(after)),
        in_specs=[pl.BlockSpec(memory_space=pltpu.SMEM)]
        + [vmem] * (11 + count + len(earlier))
        + [anywhere()] * len(after),
        out_specs=[vmem] * len(outs),
        out_shape=outs,
        scratch_shapes=scratch,
        compiler_params=pltpu.CompilerParams(vmem_limit_bytes=56 * 1024 * 1024),
        cost_estimate=pl.CostEstimate(
            flops=(
                2 * length * model * (query_columns + columns)
                + 20 * length * length * query_columns
            )
            // share,
            bytes_accessed=16 * length * model,
            transcendentals=query_columns // HD * length * length // share,
        ),
        name="attend_back",
    )(*fixed, *kept, *parts, *earlier, *after)
    if not last:
        return results
    return results[:count], results[count : 2 * count], results[2 * count], results[2 * count + 1]


def on_device(
    tokens,
    out_cotangent,
    attn_gain,
    query_weight,
    key_weight,
    value_weight,
    query_gain,
    key_gain,
    out_weight,
    ffn_gain,
    gate_weight,
    up_weight,
    down_weight,
):
    shard, query_columns = query_weight.shape
    key_columns = key_weight.shape[1]
    qkv_columns = query_columns + 2 * key_columns
    units = gate_weight.shape[1]
    width = hidden_width(units)
    steps = units // width
    attn_shard = jnp.concatenate([query_weight, key_weight, value_weight, out_weight.T], axis=1)
    ffn_shard = jnp.stack(
        [
            gate_weight.reshape(shard, steps, width),
            up_weight.reshape(shard, steps, width),
            down_weight.T.reshape(shard, steps, width),
        ],
        axis=2,
    ).reshape(shard, 3 * units)
    attn_full = gather_ring(attn_shard)
    ffn_full = lax.all_gather(ffn_shard, "fsdp", axis=0, tiled=True)

    residual = tokens.astype(f32)
    normed, attn_norm_pull = jax.vjp(rms_norm, residual, attn_gain)
    normed_parts = widen(normed.astype(bf16))
    if len(normed_parts) == 2:
        cotangent_parts = widen(held(out_cotangent, normed_parts[1:]))
    else:
        cotangent_parts = widen(out_cotangent)
    length = len(normed_parts) * normed_parts[0].shape[0]
    cosine, sine = rotary_tables(length)
    place = lax.axis_index("tp").astype(jnp.int32).reshape(1)
    fixed = (place, attn_full, query_gain[:, None], key_gain[:, None], cosine, sine)
    branch, attended, kept = attend(*fixed, normed_parts, query_columns, key_columns)
    middle = residual + narrow([*branch[:-1], held(branch[-1], cotangent_parts[1:])])
    normed_ffn, ffn_norm_pull = jax.vjp(rms_norm, middle, ffn_gain)
    ffn_parts = widen(normed_ffn.astype(bf16))
    results = []
    for at in reversed(range(len(ffn_parts))):
        after = [results[-1][1]] if results else []
        results.append(
            feed_forward(
                ffn_parts[at], cotangent_parts[at], ffn_full, width, bf16 if at else f32, after
            )
        )
    out_parts, grad_parts, pairs, hiddens = (list(item) for item in zip(*results[::-1]))
    ffn_normed_grad = narrow(grad_parts)
    middle_piece, ffn_gain_local = ffn_norm_pull(ffn_normed_grad)
    middle_grad = out_cotangent.astype(f32) + middle_piece
    branch_parts = widen(middle_grad.astype(bf16))

    ffn_blocks = weight_grads(
        ffn_parts,
        cotangent_parts,
        pairs,
        hiddens,
        steps,
        (branch_parts[0],),
        branch_parts[1:],
    )
    ffn_state, sent = ring_open(ffn_blocks)
    ffn_next, attn_next, last = 1, 1, ring_size() // 2
    out_other = [narrow_send(held(out_parts[-1], branch_parts[1:]))] if len(out_parts) == 2 else []
    back = ()
    for stage in back_stages(kept):
        back = attend_back(fixed, kept, branch_parts, stage, back, sent)
        done = back[1] if len(back) == 3 else back[2]
        if ffn_next < last:
            after = (done, *out_other) if ffn_next == 2 else (done,)
            ffn_state, sent = ring_step(ffn_blocks, ffn_next, ffn_state, after)
            ffn_next += 1
    if out_other:
        output = middle + out_parts[0] + out_other[0].astype(f32)
    else:
        output = middle + narrow(out_parts)
    output = output.astype(bf16)
    normed_grad, qkv_grad, query_gain_local, key_gain_local = back
    normed_grad = narrow([*normed_grad[:-1], held(normed_grad[-1], sent)])
    attn_blocks = weight_grads(normed_parts, branch_parts, qkv_grad, attended, 1, sent)
    attn_state, sent = ring_open(attn_blocks)
    while ffn_next < last or attn_next < last:
        if ffn_next < last:
            ffn_state, sent = ring_step(ffn_blocks, ffn_next, ffn_state)
            ffn_next += 1
        if attn_next < last:
            attn_state, sent = ring_step(attn_blocks, attn_next, attn_state, sent)
            attn_next += 1
    ffn_pieces = [
        (step * 3 * width + number * width, width, number, step * width, number == 2)
        for step in range(steps)
        for number in range(3)
    ]
    gate_grad, up_grad, down_grad = ring_close(ffn_blocks, ffn_state, ffn_pieces)
    attn_pieces = [
        (0, query_columns, 0, 0, False),
        (query_columns, key_columns, 1, 0, False),
        (query_columns + key_columns, key_columns, 2, 0, False),
        (qkv_columns, query_columns, 3, 0, True),
    ]
    query_grad, key_grad, value_grad, out_grad = ring_close(attn_blocks, attn_state, attn_pieces)
    tokens_piece, attn_gain_local = attn_norm_pull(normed_grad)
    tokens_grad = middle_grad + tokens_piece
    model = attn_gain.shape[0]
    gain_totals = sum_everywhere(
        jnp.concatenate([attn_gain_local, ffn_gain_local, query_gain_local[:, 0], key_gain_local[:, 0]])
    )
    return (
        output,
        tokens_grad,
        gain_totals[:model],
        query_grad,
        key_grad,
        value_grad,
        gain_totals[2 * model : 2 * model + HD],
        gain_totals[2 * model + HD :],
        out_grad,
        gain_totals[model : 2 * model],
        gate_grad,
        up_grad,
        down_grad,
    )


def solution(mesh):
    placed = (
        P(("fsdp", "tp"), None),
        P(("fsdp", "tp"), None),
        P(),
        P("fsdp", "tp"),
        P("fsdp", "tp"),
        P("fsdp", "tp"),
        P(),
        P(),
        P("tp", "fsdp"),
        P(),
        P("fsdp", "tp"),
        P("fsdp", "tp"),
        P("tp", "fsdp"),
    )
    return jax.shard_map(
        on_device,
        mesh=mesh,
        in_specs=placed,
        out_specs=(
            P(("fsdp", "tp"), None),
            P(("fsdp", "tp"), None),
            P(),
            P("fsdp", "tp"),
            P("fsdp", "tp"),
            P("fsdp", "tp"),
            P(),
            P(),
            P("tp", "fsdp"),
            P(),
            P("fsdp", "tp"),
            P("fsdp", "tp"),
            P("tp", "fsdp"),
        ),
        check_vma=False,
    )
```

```python
from functools import partial

import jax
import jax.numpy as jnp
from jax import lax
from jax.experimental import pallas as pl
from jax.experimental.pallas import tpu as pltpu
from jax.sharding import PartitionSpec as P

HD = 64

eps = 1e-05
theta_base = 1000000.0
f32 = jnp.float32
bf16 = jnp.bfloat16


def rms_norm(values, gain):
    return values * lax.rsqrt(jnp.mean(values * values, axis=-1, keepdims=True) + eps) * gain


def rotary_tables(length):
    half_size = HD // 2
    frequency = theta_base ** (-jnp.arange(half_size, dtype=f32) * 2.0 / HD)
    angles = frequency[:, None] * jnp.arange(length, dtype=f32)[None, :]
    return (jnp.cos(angles), jnp.sin(angles))


def dot(former, latter):
    return jnp.dot(former, latter, preferred_element_type=f32)


def dot_transposed(former, latter):
    return lax.dot_general(former, latter, (((1,), (1,)), ((), ())), preferred_element_type=f32)


def dot_leading(former, latter):
    return lax.dot_general(former, latter, (((0,), (0,)), ((), ())), preferred_element_type=f32)


def swap(values, axis_name, bit=1):
    count = lax.axis_size(axis_name)
    return lax.ppermute(values, axis_name, [(i, i ^ bit) for i in range(count)])


def widen(rows):
    if lax.axis_size("tp") == 2:
        return (rows, swap(rows, "tp"))
    return (lax.all_gather(rows, "tp", axis=0, tiled=True),)


def narrow_send(part):
    return swap(part.astype(bf16), "tp")


def narrow(parts):
    if len(parts) == 2:
        return parts[0].astype(f32) + narrow_send(parts[1]).astype(f32)
    return lax.psum_scatter(
        parts[0].astype(bf16), "tp", scatter_dimension=0, tiled=True
    ).astype(f32)


def sum_everywhere(values):
    count, chips = lax.axis_size("tp"), ring_size()
    terms = [values]
    for step in range(1, count):
        terms.append(lax.ppermute(values, "tp", [(i, (i + step) % count) for i in range(count)]))
    values = sum(terms[1:], terms[0])
    values = values + swap(values, "fsdp")
    return sum([pass_on(values, step) for step in range(1, chips)], values)


def ring_size():
    return lax.axis_size("fsdp") // 2


def chip_at(place):
    chips = ring_size()
    if isinstance(place, int):
        return 2 * place if place < chips // 2 else 2 * (chips - 1 - place) + 1
    return jnp.where(place < chips // 2, 2 * place, 2 * (chips - 1 - place) + 1)


def own_place():
    chip = lax.axis_index("fsdp") // 2
    return jnp.where(chip % 2 == 0, chip // 2, ring_size() - 1 - chip // 2)


def pass_on(values, direction):
    chips = ring_size()
    pairs = [
        (2 * chip_at(place) + core, 2 * chip_at((place + direction) % chips) + core)
        for place in range(chips)
        for core in range(2)
    ]
    return lax.ppermute(values, "fsdp", pairs)


def shard_table(ahead):
    core = lax.axis_index("fsdp") % 2
    chips = chip_at((own_place() + jnp.array(ahead, jnp.int32)) % ring_size())
    return jnp.concatenate([2 * chips + core, 2 * chips + 1 - core]).astype(jnp.int32)


def gather_ring(shard, ready):
    rows = shard.shape[0]
    half = rows // 2
    chips = ring_size()
    blocks, ahead, offset, arrived = [shard], [0], [0], []
    down = up = shard
    for step in range(1, chips // 2 + 1):
        if step in ready:
            down = held(down, ready[step])
            up = held(up, ready[step]) if step > 1 else down
        if step == chips // 2:
            down, up = down[:half], up[half:]
        down, up = pass_on(down, 1), pass_on(up, -1)
        arrived.append((down, up))
        blocks += [down, up]
        ahead += [chips - step, step]
        offset += [0, half if step == chips // 2 else 0]
    blocks = blocks + [swap(block, "fsdp") for block in blocks]
    starts = shard_table(ahead) * rows + jnp.array(offset * 2, jnp.int32)
    return starts, blocks, arrived


def place_rows(whole, starts, blocks):
    for at, block in enumerate(blocks):
        whole[pl.ds(pl.multiple_of(starts[at], 16), block.shape[0]), :] = block[...]


def assemble_body(starts, *refs):
    place_rows(refs[-1], starts, refs[:-1])


def assemble(starts, blocks, rows):
    vmem = pl.BlockSpec(memory_space=pltpu.VMEM)
    return pl.pallas_call(
        assemble_body,
        in_specs=[pl.BlockSpec(memory_space=pltpu.SMEM)] + [vmem] * len(blocks),
        out_specs=vmem,
        out_shape=jax.ShapeDtypeStruct((rows, blocks[0].shape[1]), bf16),
        compiler_params=pltpu.CompilerParams(vmem_limit_bytes=48 * 1024 * 1024),
        name="assemble",
    )(starts, *blocks)


def pack_body(steps, width, *refs):
    query, key, value, out, gate, up, down, attn, ffn = refs
    start = 0
    for piece in (query, key, value):
        attn[:, start : start + piece.shape[1]] = piece[...]
        start += piece.shape[1]
    attn[:, start:] = out[...].T
    for step in range(steps):
        here = slice(step * width, (step + 1) * width)
        start = 3 * step * width
        ffn[:, start : start + width] = gate[:, here]
        ffn[:, start + width : start + 2 * width] = up[:, here]
        ffn[:, start + 2 * width : start + 3 * width] = down[here, :].T


def pack(query, key, value, out, gate, up, down, width):
    shard, units = gate.shape
    steps = units // width
    if width % 128 or out.shape[0] % 128:
        attn = jnp.concatenate([query, key, value, out.T], axis=1)
        blocks = [piece.reshape(shard, steps, width) for piece in (gate, up, down.T)]
        return attn, jnp.stack(blocks, axis=2).reshape(shard, 3 * units)
    vmem = pl.BlockSpec(memory_space=pltpu.VMEM)
    columns = query.shape[1] + 2 * key.shape[1] + out.shape[0]
    return pl.pallas_call(
        partial(pack_body, steps, width),
        in_specs=[vmem] * 7,
        out_specs=[vmem] * 2,
        out_shape=[
            jax.ShapeDtypeStruct((shard, columns), bf16),
            jax.ShapeDtypeStruct((shard, 3 * units), bf16),
        ],
        compiler_params=pltpu.CompilerParams(vmem_limit_bytes=32 * 1024 * 1024),
        name="pack",
    )(query, key, value, out, gate, up, down)


def ring_groups():
    chips = ring_size()
    middle = [[chips // 2 - step, chips // 2 + step] for step in range(1, chips // 2)]
    return [[chips // 2]] + middle + [[0]]


def anywhere():
    return pl.BlockSpec(memory_space=pl.ANY)


def held(values, after):
    return pl.pallas_call(
        lambda *refs: None,
        in_specs=[anywhere()] * (1 + len(after)),
        out_specs=anywhere(),
        out_shape=jax.ShapeDtypeStruct(values.shape, values.dtype),
        input_output_aliases={0: 0},
        name="held",
    )(values, *after)


def weight_grad_body(parts, groups, rows, extra, *refs):
    table = refs[0]
    first_in = refs[1 : 1 + parts]
    second_in = refs[1 + parts : 1 + 2 * parts]
    first_grads = refs[1 + 2 * parts : 1 + 3 * parts]
    second_grads = refs[1 + 3 * parts : 1 + 4 * parts]
    outs = refs[1 + 4 * parts + extra : -3]
    first_turned, second_turned, total = refs[-3:]
    part_rows = first_in[0].shape[0]
    first_width = first_grads[0].shape[1]

    @pl.when(pl.program_id(0) == 0)
    def _():
        for part in range(parts):
            span = pl.ds(part * part_rows, part_rows)
            first_turned[:, span] = first_in[part][...].T
            second_turned[:, span] = second_in[part][...].T

    def joined(pieces):
        if parts == 1:
            return pieces[0][...]
        return jnp.concatenate([piece[...] for piece in pieces], axis=0)

    total[:, :first_width] = dot(first_turned[...], joined(first_grads)).astype(bf16)
    total[:, first_width:] = dot(second_turned[...], joined(second_grads)).astype(bf16)
    count = sum(len(group) for group in groups)
    at = 0
    for number, group in enumerate(groups):
        for member in range(len(group)):
            mine = pl.multiple_of(table[at] * rows, rows)
            outs[number][member] = total[pl.ds(mine, rows), :]
            near = pl.multiple_of(table[count + at] * rows, rows)
            outs[len(groups) + number][member] = total[pl.ds(near, rows), :]
            at += 1


def weight_grads(first, second, first_grads, second_grads, steps, after, before=()):
    parts = len(first)
    part_rows, model = first[0].shape
    length = parts * part_rows
    first_width = first_grads[0].shape[1] // steps
    second_width = second_grads[0].shape[1] // steps
    width = first_width + second_width
    groups = ring_groups()
    count = 2 * ring_size()
    rows = model // count
    table = shard_table([place for group in groups for place in group])
    whole = pl.BlockSpec((part_rows, model), lambda i: (0, 0))
    outs = [jax.ShapeDtypeStruct((len(group), rows, steps * width), bf16) for group in groups] * 2
    out_specs = [
        pl.BlockSpec((len(group), rows, width), lambda i: (0, 0, i)) for group in groups
    ] * 2
    results = pl.pallas_call(
        partial(weight_grad_body, parts, groups, rows, len(after)),
        grid=(steps,),
        in_specs=[pl.BlockSpec(memory_space=pltpu.SMEM)]
        + [whole] * (2 * parts)
        + [pl.BlockSpec((part_rows, first_width), lambda i: (0, i))] * parts
        + [pl.BlockSpec((part_rows, second_width), lambda i: (0, i))] * parts
        + [anywhere()] * len(after),
        out_specs=out_specs,
        out_shape=outs,
        scratch_shapes=[
            pltpu.VMEM((model, length), bf16),
            pltpu.VMEM((model, length), bf16),
            pltpu.VMEM((model, width), bf16),
        ],
        compiler_params=pltpu.CompilerParams(vmem_limit_bytes=56 * 1024 * 1024),
        cost_estimate=pl.CostEstimate(
            flops=2 * length * model * steps * width,
            bytes_accessed=4 * model * steps * width,
            transcendentals=0,
        ),
        name="weight_grads",
    )(table, *first, *second, *first_grads, *second_grads, *after)
    mine = results[: len(groups)]
    near = list(results[len(groups) :])
    if before:
        near[0] = held(near[0], before)
    near = [swap(block, "fsdp") for block in near]
    return mine, near


def ring_call(body, operands, outs, after, name):
    vmem = pl.BlockSpec(memory_space=pltpu.VMEM)
    return pl.pallas_call(
        body,
        in_specs=[vmem] * len(operands) + [anywhere()] * len(after),
        out_specs=[vmem] * len(outs),
        out_shape=outs,
        compiler_params=pltpu.CompilerParams(vmem_limit_bytes=48 * 1024 * 1024),
        name=name,
    )(*operands, *after)


def both_cores(mine, near, member):
    return mine[member].astype(f32) + near[member].astype(f32)


def open_body(cut, mine, near, *refs):
    low, high = refs[-2:]
    total = both_cores(mine, near, 0).astype(bf16)
    low[...] = total[:, :cut]
    high[...] = total[:, cut:]


def step_body(cut, mine, near, down, up, *refs):
    ahead, behind = refs[-2:]
    columns = ahead.shape[1]
    ahead_sum = both_cores(mine, near, 0)
    behind_sum = both_cores(mine, near, 1)
    if down.shape[1] == columns:
        ahead[...] = (ahead_sum + down[...].astype(f32)).astype(bf16)
        behind[...] = (behind_sum + up[...].astype(f32)).astype(bf16)
    else:
        ahead[:, :cut] = (ahead_sum[:, :cut] + down[...].astype(f32)).astype(bf16)
        ahead[:, cut:] = ahead_sum[:, cut:].astype(bf16)
        behind[:, :cut] = behind_sum[:, :cut].astype(bf16)
        behind[:, cut:] = (behind_sum[:, cut:] + up[...].astype(f32)).astype(bf16)


def close_body(pieces, mine, near, down, up, *outs):
    total = both_cores(mine, near, 0) + down[...].astype(f32) + up[...].astype(f32)
    for start, width, number, place, turn in pieces:
        values = total[:, start : start + width]
        if turn:
            outs[number][place : place + width, :] = values.T
        else:
            outs[number][:, place : place + width] = values


def ring_cut(columns):
    return columns // 2 // 128 * 128


def ring_pass(sums):
    return pass_on(sums[0], 1), pass_on(sums[1], -1)


def ring_open(blocks, after=()):
    mine, near = blocks
    rows, columns = mine[0].shape[1:]
    cut = ring_cut(columns)
    outs = [jax.ShapeDtypeStruct((rows, width), bf16) for width in (cut, columns - cut)]
    sums = ring_call(partial(open_body, cut), (mine[0], near[0]), outs, after, "ring_open")
    return ring_pass(sums), tuple(sums)


def ring_step(blocks, number, state, after=()):
    mine, near = blocks[0][number], blocks[1][number]
    rows, columns = mine.shape[1:]
    outs = [jax.ShapeDtypeStruct((rows, columns), bf16)] * 2
    body = partial(step_body, ring_cut(columns))
    sums = ring_call(body, (mine, near, *state), outs, after, "ring_step")
    return ring_pass(sums), tuple(sums)


def ring_close(blocks, state, pieces):
    mine, near = blocks[0][-1], blocks[1][-1]
    rows = mine.shape[1]
    in_kernel = all(width % 128 == 0 for _, width, _, _, turn in pieces if turn)
    sizes, turns = {}, {}
    for _, width, number, place, turn in pieces:
        sizes[number] = max(sizes.get(number, 0), place + width)
        turns[number] = turn
    if not in_kernel:
        pieces = [piece[:4] + (False,) for piece in pieces]
    outs = [
        jax.ShapeDtypeStruct(
            (sizes[number], rows) if turns[number] and in_kernel else (rows, sizes[number]), f32
        )
        for number in range(len(sizes))
    ]
    results = ring_call(
        partial(close_body, pieces), (mine, near, *state), outs, (), "ring_close"
    )
    return [
        result.T if turns[number] and not in_kernel else result
        for number, result in enumerate(results)
    ]


def ffn_body(width, count, extra, *refs):
    starts, rows_in, cotangent_in = refs[:3]
    blocks = refs[3 : 3 + count]
    out, grad, pairs, hiddens, out_sum, grad_sum, weights = refs[3 + count + extra :]
    step = pl.program_id(0)
    length = rows_in.shape[0]

    @pl.when(step == 0)
    def _():
        out_sum[...] = jnp.zeros_like(out_sum)
        grad_sum[...] = jnp.zeros_like(grad_sum)

    place_rows(weights, starts, blocks)
    pair_weights = weights[:, : 2 * width]
    down = weights[:, 2 * width :]
    chunk = min(256, length)
    for start in range(0, length, chunk):
        span = pl.ds(start, chunk)
        both = dot(rows_in[span, :], pair_weights)
        gate = both[:, :width]
        up = both[:, width:]
        hidden_grad = dot(cotangent_in[span, :], down)
        sigmoid = 1.0 / (1.0 + jnp.exp(-gate))
        silu = gate * sigmoid
        hidden = (silu * up).astype(bf16)
        gate_grad = hidden_grad * up * sigmoid * (1.0 + gate * (1.0 - sigmoid))
        up_grad = hidden_grad * silu
        pair = jnp.concatenate([gate_grad.astype(bf16), up_grad.astype(bf16)], axis=1)
        hiddens[span, :] = hidden
        pairs[span, :] = pair
        out_sum[span, :] += dot_transposed(hidden, down)
        grad_sum[span, :] += dot_transposed(pair, pair_weights)

    @pl.when(step == pl.num_programs(0) - 1)
    def _():
        out[...] = out_sum[...].astype(out.dtype)
        grad[...] = grad_sum[...].astype(grad.dtype)


def hidden_width(units):
    for width in (768, 256, 384, 128):
        if units % width == 0:
            return width
    return units


def feed_forward(rows, cotangent, starts, blocks, width, kind, after):
    length, model = rows.shape
    steps = blocks[0].shape[1] // (3 * width)
    whole = pl.BlockSpec((length, model), lambda i: (0, 0))
    sums = jax.ShapeDtypeStruct((length, model), kind)
    return pl.pallas_call(
        partial(ffn_body, width, len(blocks), len(after)),
        grid=(steps,),
        in_specs=[pl.BlockSpec(memory_space=pltpu.SMEM), whole, whole]
        + [pl.BlockSpec((block.shape[0], 3 * width), lambda i: (0, i)) for block in blocks]
        + [anywhere()] * len(after),
        out_specs=[
            whole,
            whole,
            pl.BlockSpec((length, 2 * width), lambda i: (0, i)),
            pl.BlockSpec((length, width), lambda i: (0, i)),
        ],
        out_shape=[
            sums,
            sums,
            jax.ShapeDtypeStruct((length, steps * 2 * width), bf16),
            jax.ShapeDtypeStruct((length, steps * width), bf16),
        ],
        scratch_shapes=[
            pltpu.VMEM((length, model), f32),
            pltpu.VMEM((length, model), f32),
            pltpu.VMEM((model, 3 * width), bf16),
        ],
        compiler_params=pltpu.CompilerParams(vmem_limit_bytes=56 * 1024 * 1024),
        cost_estimate=pl.CostEstimate(
            flops=12 * length * model * steps * width,
            bytes_accessed=8 * model * steps * width,
            transcendentals=length * steps * width,
        ),
        name="feed_forward",
    )(starts, rows, cotangent, *blocks, *after)


def lines(start, size):
    if isinstance(start, int):
        return pl.ds(start, size)
    return pl.ds(pl.multiple_of(start, size), size)


def part_starts(place, count, part_rows):
    if count == 1:
        return [0]
    return [place[0] * part_rows, (1 - place[0]) * part_rows]


def causal_block(size):
    keys = lax.broadcasted_iota(jnp.int32, (size, size), 0)
    queries = lax.broadcasted_iota(jnp.int32, (size, size), 1)
    return keys <= queries


def attend_body(count, *refs):
    place, weights, query_gain, key_gain, cosine, sine = refs[:6]
    rows_in = refs[6 : 6 + count]
    branches = refs[6 + count : 6 + 2 * count]
    attended_out = refs[6 + 2 * count : 6 + 3 * count]
    raw, query_rows, key_rows, value_rows, attended, log_totals = refs[6 + 3 * count : 12 + 3 * count]
    rows, turned = refs[12 + 3 * count :]
    part_rows = rows_in[0].shape[0]
    length = rows.shape[0]
    heads = query_rows.shape[0] // HD
    kv_heads = key_rows.shape[0] // HD
    group_size = heads // kv_heads
    columns = (heads + 2 * kv_heads) * HD
    half = HD // 2
    starts = part_starts(place, count, part_rows)
    for part in range(count):
        rows[lines(starts[part], part_rows), :] = rows_in[part][...]

    chunk = min(256, columns)
    for first in range(0, columns, chunk):
        product = dot_transposed(weights[:, first : first + chunk].T, rows[...])
        for at in range(0, chunk, HD):
            head = (first + at) // HD
            values = product[at : at + HD]
            if head >= heads + kv_heads:
                start = (head - heads - kv_heads) * HD
                value_rows[start : start + HD, :] = values.astype(bf16)
                continue
            raw[first + at : first + at + HD, :] = values
            gain = query_gain if head < heads else key_gain
            scale = lax.rsqrt(jnp.mean(values * values, axis=0, keepdims=True) + eps)
            normed = values * scale * gain[...]
            top, bottom = normed[:half], normed[half:]
            top, bottom = (
                top * cosine[...] - bottom * sine[...],
                bottom * cosine[...] + top * sine[...],
            )
            if head < heads:
                target, start = query_rows, head * HD
                top = top.astype(bf16).astype(f32) * HD**-0.5
                bottom = bottom.astype(bf16).astype(f32) * HD**-0.5
            else:
                target, start = key_rows, (head - heads) * HD
            target[start : start + half, :] = top.astype(bf16)
            target[start + half : start + HD, :] = bottom.astype(bf16)

    block = min(256, length)
    causal = causal_block(block)

    def one_group(kv_head, carry):
        span = lines(kv_head * HD, HD)
        keys = key_rows[span, :].T
        values = value_rows[span, :]
        for member in range(group_size):
            head = kv_head * group_size + member
            for start in range(0, length, block):
                here = slice(start, start + block)
                query = query_rows[lines(head * HD, HD), here]
                weight = jnp.where(causal, jnp.exp(dot(keys[here], query)), 0.0)
                total = jnp.sum(weight, axis=0, keepdims=True)
                result = dot(values[:, here], weight.astype(bf16))
                if start:
                    weight = jnp.exp(dot(keys[:start], query))
                    total = total + jnp.sum(weight, axis=0, keepdims=True)
                    result = result + dot(values[:, :start], weight.astype(bf16))
                attended[lines(head * HD, HD), here] = (result * (1.0 / total)).astype(bf16)
                log_totals[head, :, here] = jnp.log(total)
        return carry

    lax.fori_loop(0, kv_heads, one_group, 0)
    turned[...] = attended[...].T
    for part in range(count):
        mine = turned[lines(starts[part], part_rows), :]
        attended_out[part][...] = mine
        branches[part][...] = dot_transposed(mine, weights[:, columns:]).astype(branches[part].dtype)


def attend(place, weights, query_gain, key_gain, cosine, sine, parts, query_columns, key_columns):
    count = len(parts)
    part_rows, model = parts[0].shape
    length = count * part_rows
    heads = query_columns // HD
    shape = jax.ShapeDtypeStruct
    kinds = [f32] + [bf16] * (count - 1)
    vmem = pl.BlockSpec(memory_space=pltpu.VMEM)
    outs = (
        [shape((part_rows, model), kind) for kind in kinds]
        + [shape((part_rows, query_columns), bf16)] * count
        + [
            shape((query_columns + key_columns, length), f32),
            shape((query_columns, length), bf16),
            shape((key_columns, length), bf16),
            shape((key_columns, length), bf16),
            shape((query_columns, length), bf16),
            shape((heads, 1, length), f32),
        ]
    )
    results = pl.pallas_call(
        partial(attend_body, count),
        in_specs=[pl.BlockSpec(memory_space=pltpu.SMEM)] + [vmem] * (5 + count),
        out_specs=[vmem] * len(outs),
        out_shape=outs,
        scratch_shapes=[
            pltpu.VMEM((length, model), bf16),
            pltpu.VMEM((length, query_columns), bf16),
        ],
        compiler_params=pltpu.CompilerParams(vmem_limit_bytes=56 * 1024 * 1024),
        cost_estimate=pl.CostEstimate(
            flops=2 * length * model * (2 * query_columns + 2 * key_columns)
            + 8 * length * length * query_columns,
            bytes_accessed=16 * length * model,
            transcendentals=heads * length * length,
        ),
        name="attend",
    )(place, weights, query_gain, key_gain, cosine, sine, *parts)
    return results[:count], results[count : 2 * count], results[2 * count :]


def attend_back_body(count, first_group, last_group, extra, *refs):
    place, weights, query_gain, key_gain, cosine, sine = refs[:6]
    raw, query_rows, key_rows, value_rows, attended, log_totals = refs[6:12]
    branch_in = refs[12 : 12 + count]
    refs = refs[12 + count :]
    if first_group:
        earlier = refs[:3]
        refs = refs[3:]
    refs = refs[extra:]
    last = last_group * HD == key_rows.shape[0]
    if last:
        grads, raw_grads, refs = refs[:count], refs[count : 2 * count], refs[2 * count :]
        query_gain_grad, key_gain_grad, turned_grads = refs[:3]
        rows, attended_grad, key_sum, value_sum, straight = refs[3:]
    else:
        turned_grads, query_gain_grad, key_gain_grad = refs[:3]
        rows, attended_grad, key_sum, value_sum = refs[3:]
    part_rows = branch_in[0].shape[0]
    length = rows.shape[0]
    heads = query_rows.shape[0] // HD
    kv_heads = key_rows.shape[0] // HD
    group_size = heads // kv_heads
    columns = (heads + 2 * kv_heads) * HD
    half = HD // 2
    starts = part_starts(place, count, part_rows)
    for part in range(count):
        rows[lines(starts[part], part_rows), :] = branch_in[part][...]
    stage_rows = (last_group - first_group) * group_size * HD
    chunk = min(256, stage_rows)
    begin = first_group * group_size * HD
    for first in range(begin, begin + stage_rows, chunk):
        piece = weights[:, columns + first : columns + first + chunk].T
        attended_grad[first : first + chunk, :] = dot_transposed(piece, rows[...]).astype(bf16)
    if first_group:
        turned_grads[...] = earlier[0][...]
        query_gain_grad[...] = earlier[1][...]
        key_gain_grad[...] = earlier[2][...]
    else:
        turned_grads[...] = jnp.zeros_like(turned_grads)
        query_gain_grad[...] = jnp.zeros_like(query_gain_grad)
        key_gain_grad[...] = jnp.zeros_like(key_gain_grad)
    block = min(256, length)
    causal = causal_block(block)

    def unprepare(grad, values, gain, gain_grad):
        top, bottom = grad[:half], grad[half:]
        grad = jnp.concatenate(
            [
                top * cosine[...] + bottom * sine[...],
                bottom * cosine[...] - top * sine[...],
            ],
            axis=0,
        )
        scale = lax.rsqrt(jnp.mean(values * values, axis=0, keepdims=True) + eps)
        normed = values * scale
        gain_grad[...] += jnp.sum(grad * normed, axis=1, keepdims=True)
        grad = grad * gain[...]
        inner = jnp.mean(grad * normed, axis=0, keepdims=True)
        return (scale * (grad - normed * inner)).astype(bf16)

    def one_group(kv_head, carry):
        span = lines(kv_head * HD, HD)
        keys_turned = key_rows[span, :]
        keys = keys_turned.T
        values = value_rows[span, :].T
        key_sum[...] = jnp.zeros_like(key_sum)
        value_sum[...] = jnp.zeros_like(value_sum)
        for member in range(group_size):
            head = kv_head * group_size + member
            head_span = lines(head * HD, HD)
            query_parts = []
            for start in range(0, length, block):
                here = slice(start, start + block)
                query = query_rows[head_span, here]
                grad = attended_grad[head_span, here]
                inner = jnp.sum(
                    grad.astype(f32) * attended[head_span, here].astype(f32), axis=0, keepdims=True
                )
                log_total = log_totals[head, :, here]
                query_grad = None
                for low, high in [(start, start + block)] + ([(0, start)] if start else []):
                    prob = jnp.exp(dot(keys[low:high], query) - log_total)
                    if low == start:
                        prob = jnp.where(causal, prob, 0.0)
                    prob_grad = dot(values[low:high], grad)
                    score_grad = (prob * (prob_grad - inner)).astype(bf16)
                    piece = dot(keys_turned[:, low:high], score_grad)
                    query_grad = piece if query_grad is None else query_grad + piece
                    key_sum[:, low:high] += dot_transposed(query, score_grad)
                    value_sum[:, low:high] += dot_transposed(grad, prob.astype(bf16))
                query_parts.append(query_grad * HD**-0.5)
            turned_grads[head_span, :] = unprepare(
                jnp.concatenate(query_parts, axis=1), raw[head_span, :], query_gain, query_gain_grad
            )
        key_span = lines((heads + kv_head) * HD, HD)
        turned_grads[key_span, :] = unprepare(
            key_sum[...], raw[key_span, :], key_gain, key_gain_grad
        )
        turned_grads[lines((heads + kv_heads + kv_head) * HD, HD), :] = value_sum[...].astype(bf16)
        return carry

    lax.fori_loop(first_group, last_group, one_group, 0)
    if last:
        straight[...] = turned_grads[...].T
        for part in range(count):
            mine = straight[lines(starts[part], part_rows), :]
            raw_grads[part][...] = mine
            grads[part][...] = dot_transposed(mine, weights[:, :columns]).astype(grads[part].dtype)


def back_stages(kept):
    kv_heads = kept[2].shape[0] // HD
    if kv_heads % 4:
        return [(0, kv_heads)]
    quarter = kv_heads // 4
    return [(0, quarter), (quarter, 3 * quarter), (3 * quarter, kv_heads)]


def attend_back(fixed, kept, parts, stage, earlier, after):
    count = len(parts)
    first_group, last_group = stage
    kv_heads = kept[2].shape[0] // HD
    part_rows, model = parts[0].shape
    length = count * part_rows
    query_columns = kept[1].shape[0]
    columns = query_columns + 2 * kept[2].shape[0]
    shape = jax.ShapeDtypeStruct
    vmem = pl.BlockSpec(memory_space=pltpu.VMEM)
    last = last_group == kv_heads
    share = kv_heads // (last_group - first_group)
    gains = [shape((HD, 1), f32)] * 2
    turned = shape((columns, length), bf16)
    scratch = [
        pltpu.VMEM((length, model), bf16),
        pltpu.VMEM((query_columns, length), bf16),
        pltpu.VMEM((HD, length), f32),
        pltpu.VMEM((HD, length), f32),
    ]
    if last:
        outs = (
            [shape((part_rows, model), kind) for kind in [f32] + [bf16] * (count - 1)]
            + [shape((part_rows, columns), bf16)] * count
            + gains
        )
        scratch = [pltpu.VMEM(turned.shape, bf16)] + scratch + [pltpu.VMEM((length, columns), bf16)]
    else:
        outs = [turned] + gains
    results = pl.pallas_call(
        partial(attend_back_body, count, first_group, last_group, len(after)),
        in_specs=[pl.BlockSpec(memory_space=pltpu.SMEM)]
        + [vmem] * (11 + count + len(earlier))
        + [anywhere()] * len(after),
        out_specs=[vmem] * len(outs),
        out_shape=outs,
        scratch_shapes=scratch,
        compiler_params=pltpu.CompilerParams(vmem_limit_bytes=56 * 1024 * 1024),
        cost_estimate=pl.CostEstimate(
            flops=(
                2 * length * model * (query_columns + columns)
                + 20 * length * length * query_columns
            )
            // share,
            bytes_accessed=16 * length * model,
            transcendentals=query_columns // HD * length * length // share,
        ),
        name="attend_back",
    )(*fixed, *kept, *parts, *earlier, *after)
    if not last:
        return results
    return results[:count], results[count : 2 * count], results[2 * count], results[2 * count + 1]


def on_device(
    tokens,
    out_cotangent,
    attn_gain,
    query_weight,
    key_weight,
    value_weight,
    query_gain,
    key_gain,
    out_weight,
    ffn_gain,
    gate_weight,
    up_weight,
    down_weight,
):
    shard, query_columns = query_weight.shape
    key_columns = key_weight.shape[1]
    qkv_columns = query_columns + 2 * key_columns
    units = gate_weight.shape[1]
    width = hidden_width(units)
    steps = units // width
    attn_shard, ffn_shard = pack(
        query_weight, key_weight, value_weight, out_weight, gate_weight, up_weight, down_weight, width
    )
    attn_starts, attn_pieces, attn_arrived = gather_ring(attn_shard, {})
    attn_full = assemble(attn_starts, attn_pieces, query_weight.shape[0] * lax.axis_size("fsdp"))

    residual = tokens.astype(f32)
    normed, attn_norm_pull = jax.vjp(rms_norm, residual, attn_gain)
    normed_parts = widen(normed.astype(bf16))
    if len(normed_parts) == 2:
        cotangent_parts = widen(held(out_cotangent, normed_parts[1:]))
    else:
        cotangent_parts = widen(out_cotangent)
    length = len(normed_parts) * normed_parts[0].shape[0]
    cosine, sine = rotary_tables(length)
    place = lax.axis_index("tp").astype(jnp.int32).reshape(1)
    fixed = (place, attn_full, query_gain[:, None], key_gain[:, None], cosine, sine)
    branch, attended, kept = attend(*fixed, normed_parts, query_columns, key_columns)
    ffn_starts, ffn_pieces, ffn_arrived = gather_ring(
        ffn_shard, {1: attn_arrived[-2], 2: (branch[0],)}
    )
    branch = [*branch[:-1], held(branch[-1], (*cotangent_parts[1:], *ffn_arrived[0]))]
    middle = residual + narrow(branch)
    normed_ffn, ffn_norm_pull = jax.vjp(rms_norm, middle, ffn_gain)
    ffn_parts = widen(normed_ffn.astype(bf16))
    results = []
    for at in reversed(range(len(ffn_parts))):
        after = [results[-1][1]] if results else []
        results.append(
            feed_forward(
                ffn_parts[at],
                cotangent_parts[at],
                ffn_starts,
                ffn_pieces,
                width,
                bf16 if at else f32,
                after,
            )
        )
    out_parts, grad_parts, pairs, hiddens = (list(item) for item in zip(*results[::-1]))
    ffn_normed_grad = narrow(grad_parts)
    middle_piece, ffn_gain_local = ffn_norm_pull(ffn_normed_grad)
    middle_grad = out_cotangent.astype(f32) + middle_piece
    branch_parts = widen(middle_grad.astype(bf16))

    ffn_blocks = weight_grads(
        ffn_parts,
        cotangent_parts,
        pairs,
        hiddens,
        steps,
        (branch_parts[0],),
        branch_parts[1:],
    )
    ffn_state, sent = ring_open(ffn_blocks)
    ffn_next, attn_next, last = 1, 1, ring_size() // 2
    out_other = [narrow_send(held(out_parts[-1], branch_parts[1:]))] if len(out_parts) == 2 else []
    back = ()
    for stage in back_stages(kept):
        back = attend_back(fixed, kept, branch_parts, stage, back, sent)
        done = back[1] if len(back) == 3 else back[2]
        if ffn_next < last:
            after = (done, *out_other) if ffn_next == 2 else (done,)
            ffn_state, sent = ring_step(ffn_blocks, ffn_next, ffn_state, after)
            ffn_next += 1
    if out_other:
        output = middle + out_parts[0] + out_other[0].astype(f32)
    else:
        output = middle + narrow(out_parts)
    output = output.astype(bf16)
    normed_grad, qkv_grad, query_gain_local, key_gain_local = back
    normed_grad = narrow([*normed_grad[:-1], held(normed_grad[-1], sent)])
    attn_blocks = weight_grads(normed_parts, branch_parts, qkv_grad, attended, 1, sent)
    attn_state, sent = ring_open(attn_blocks)
    while ffn_next < last or attn_next < last:
        if ffn_next < last:
            ffn_state, sent = ring_step(ffn_blocks, ffn_next, ffn_state)
            ffn_next += 1
        if attn_next < last:
            attn_state, sent = ring_step(attn_blocks, attn_next, attn_state, sent)
            attn_next += 1
    ffn_places = [
        (step * 3 * width + number * width, width, number, step * width, number == 2)
        for step in range(steps)
        for number in range(3)
    ]
    gate_grad, up_grad, down_grad = ring_close(ffn_blocks, ffn_state, ffn_places)
    attn_places = [
        (0, query_columns, 0, 0, False),
        (query_columns, key_columns, 1, 0, False),
        (query_columns + key_columns, key_columns, 2, 0, False),
        (qkv_columns, query_columns, 3, 0, True),
    ]
    query_grad, key_grad, value_grad, out_grad = ring_close(attn_blocks, attn_state, attn_places)
    tokens_piece, attn_gain_local = attn_norm_pull(normed_grad)
    tokens_grad = middle_grad + tokens_piece
    model = attn_gain.shape[0]
    gain_totals = sum_everywhere(
        jnp.concatenate([attn_gain_local, ffn_gain_local, query_gain_local[:, 0], key_gain_local[:, 0]])
    )
    return (
        output,
        tokens_grad,
        gain_totals[:model],
        query_grad,
        key_grad,
        value_grad,
        gain_totals[2 * model : 2 * model + HD],
        gain_totals[2 * model + HD :],
        out_grad,
        gain_totals[model : 2 * model],
        gate_grad,
        up_grad,
        down_grad,
    )


def solution(mesh):
    placed = (
        P(("fsdp", "tp"), None),
        P(("fsdp", "tp"), None),
        P(),
        P("fsdp", "tp"),
        P("fsdp", "tp"),
        P("fsdp", "tp"),
        P(),
        P(),
        P("tp", "fsdp"),
        P(),
        P("fsdp", "tp"),
        P("fsdp", "tp"),
        P("tp", "fsdp"),
    )
    return jax.shard_map(
        on_device,
        mesh=mesh,
        in_specs=placed,
        out_specs=(
            P(("fsdp", "tp"), None),
            P(("fsdp", "tp"), None),
            P(),
            P("fsdp", "tp"),
            P("fsdp", "tp"),
            P("fsdp", "tp"),
            P(),
            P(),
            P("tp", "fsdp"),
            P(),
            P("fsdp", "tp"),
            P("fsdp", "tp"),
            P("tp", "fsdp"),
        ),
        check_vma=False,
    )
```

```python
from functools import partial

import jax
import jax.numpy as jnp
from jax import lax
from jax.experimental import pallas as pl
from jax.experimental.pallas import tpu as pltpu
from jax.sharding import PartitionSpec as P

HD = 64

eps = 1e-05
theta_base = 1000000.0
f32 = jnp.float32
bf16 = jnp.bfloat16


def rms_norm(values, gain):
    return values * lax.rsqrt(jnp.mean(values * values, axis=-1, keepdims=True) + eps) * gain


def rotary_tables(length):
    half_size = HD // 2
    frequency = theta_base ** (-jnp.arange(half_size, dtype=f32) * 2.0 / HD)
    angles = frequency[:, None] * jnp.arange(length, dtype=f32)[None, :]
    return (jnp.cos(angles), jnp.sin(angles))


def dot(former, latter):
    return jnp.dot(former, latter, preferred_element_type=f32)


def dot_transposed(former, latter):
    return lax.dot_general(former, latter, (((1,), (1,)), ((), ())), preferred_element_type=f32)


def dot_leading(former, latter):
    return lax.dot_general(former, latter, (((0,), (0,)), ((), ())), preferred_element_type=f32)


def swap(values, axis_name, bit=1):
    count = lax.axis_size(axis_name)
    return lax.ppermute(values, axis_name, [(i, i ^ bit) for i in range(count)])


def anywhere():
    return pl.BlockSpec(memory_space=pl.ANY)


def entire(arrays):
    return [pl.BlockSpec(array.shape, lambda i, rank=array.ndim: (0,) * rank) for array in arrays]


def held_all(arrays, after):
    count = len(arrays)
    return pl.pallas_call(
        lambda *refs: None,
        in_specs=[anywhere()] * (count + len(after)),
        out_specs=[anywhere()] * count,
        out_shape=[jax.ShapeDtypeStruct(array.shape, array.dtype) for array in arrays],
        input_output_aliases={at: at for at in range(count)},
        name="held",
    )(*arrays, *after)


def held(values, after):
    return held_all([values], after)[0]


def widen(rows):
    if lax.axis_size("tp") == 2:
        return (rows, swap(rows, "tp"))
    return (lax.all_gather(rows, "tp", axis=0, tiled=True),)


def narrow_send(part):
    return swap(part.astype(bf16), "tp")


def narrow(parts):
    if len(parts) == 2:
        return parts[0].astype(f32) + narrow_send(parts[1]).astype(f32)
    return lax.psum_scatter(
        parts[0].astype(bf16), "tp", scatter_dimension=0, tiled=True
    ).astype(f32)


def sum_rounds():
    return [
        (axis_name, 1 << bit)
        for axis_name in ("tp", "fsdp")
        for bit in range(lax.axis_size(axis_name).bit_length() - 1)
    ]


def ring_size():
    return lax.axis_size("fsdp") // 2


def chip_at(place):
    chips = ring_size()
    if isinstance(place, int):
        return 2 * place if place < chips // 2 else 2 * (chips - 1 - place) + 1
    return jnp.where(place < chips // 2, 2 * place, 2 * (chips - 1 - place) + 1)


def own_place():
    chip = lax.axis_index("fsdp") // 2
    return jnp.where(chip % 2 == 0, chip // 2, ring_size() - 1 - chip // 2)


def pass_on(values, direction):
    chips = ring_size()
    pairs = [
        (2 * chip_at(place) + core, 2 * chip_at((place + direction) % chips) + core)
        for place in range(chips)
        for core in range(2)
    ]
    return lax.ppermute(values, "fsdp", pairs)


def shard_table(ahead):
    core = lax.axis_index("fsdp") % 2
    chips = chip_at((own_place() + jnp.array(ahead, jnp.int32)) % ring_size())
    return jnp.concatenate([2 * chips + core, 2 * chips + 1 - core]).astype(jnp.int32)


def gather_ring(shard, ready):
    rows = shard.shape[0]
    half = rows // 2
    chips = ring_size()
    blocks, ahead, offset, arrived = [], [0], [0], []
    sent = [shard]
    for step in range(1, chips // 2 + 1):
        if step in ready:
            sent = held_all(sent, ready[step])
        blocks += sent
        down, up = sent[0], sent[-1]
        if step == chips // 2:
            down, up = down[:half], up[half:]
        sent = [pass_on(down, 1), pass_on(up, -1)]
        arrived.append(sent)
        ahead += [chips - step, step]
        offset += [0, half if step == chips // 2 else 0]
    blocks += sent
    starts = shard_table(ahead) * rows + jnp.array(offset * 2, jnp.int32)
    return starts, blocks, arrived


def gather_near(blocks, ready=()):
    ends = held_all(blocks[-2:], ready) if ready else blocks[-2:]
    blocks = [*blocks[:-2], *ends]
    return blocks + [swap(block, "fsdp") for block in blocks]


def place_rows(whole, starts, blocks):
    for at, block in enumerate(blocks):
        whole[pl.ds(pl.multiple_of(starts[at], 16), block.shape[0]), :] = block[...]


def assemble_body(starts, *refs):
    place_rows(refs[-1], starts, refs[:-1])


def assemble(starts, blocks, rows):
    out = jax.ShapeDtypeStruct((rows, blocks[0].shape[1]), bf16)
    return pl.pallas_call(
        assemble_body,
        grid=(1,),
        in_specs=[pl.BlockSpec(memory_space=pltpu.SMEM)] + entire(blocks),
        out_specs=entire([out])[0],
        out_shape=out,
        compiler_params=pltpu.CompilerParams(vmem_limit_bytes=48 * 1024 * 1024),
        name="assemble",
    )(starts, *blocks)


def pack_body(places, *refs):
    whole = refs[-1]
    for number, source, start, width in places:
        whole[:, start : start + width] = refs[number][:, source : source + width]


def pack(arrays, places, after):
    columns = max(start + width for _, _, start, width in places)
    out = jax.ShapeDtypeStruct((arrays[0].shape[0], columns), bf16)
    return pl.pallas_call(
        partial(pack_body, places),
        grid=(1,),
        in_specs=entire(arrays) + [anywhere()] * len(after),
        out_specs=entire([out])[0],
        out_shape=out,
        compiler_params=pltpu.CompilerParams(vmem_limit_bytes=32 * 1024 * 1024),
        name="pack",
    )(*arrays, *after)


def ring_groups():
    chips = ring_size()
    middle = [[chips // 2 - step, chips // 2 + step] for step in range(1, chips // 2)]
    return [[chips // 2]] + middle + [[0]]


def weight_grad_body(parts, groups, rows, extra, *refs):
    table = refs[0]
    first_in = refs[1 : 1 + parts]
    second_in = refs[1 + parts : 1 + 2 * parts]
    first_grads = refs[1 + 2 * parts : 1 + 3 * parts]
    second_grads = refs[1 + 3 * parts : 1 + 4 * parts]
    outs = refs[1 + 4 * parts + extra : -3]
    first_turned, second_turned, total = refs[-3:]
    part_rows = first_in[0].shape[0]
    first_width = first_grads[0].shape[1]

    @pl.when(pl.program_id(0) == 0)
    def _():
        for part in range(parts):
            span = pl.ds(part * part_rows, part_rows)
            first_turned[:, span] = first_in[part][...].T
            second_turned[:, span] = second_in[part][...].T

    def joined(pieces):
        if parts == 1:
            return pieces[0][...]
        return jnp.concatenate([piece[...] for piece in pieces], axis=0)

    total[:, :first_width] = dot(first_turned[...], joined(first_grads)).astype(bf16)
    total[:, first_width:] = dot(second_turned[...], joined(second_grads)).astype(bf16)
    count = sum(len(group) for group in groups)
    at = 0
    for number, group in enumerate(groups):
        for member in range(len(group)):
            mine = pl.multiple_of(table[at] * rows, rows)
            outs[number][member] = total[pl.ds(mine, rows), :]
            near = pl.multiple_of(table[count + at] * rows, rows)
            outs[len(groups) + number][member] = total[pl.ds(near, rows), :]
            at += 1


def weight_grads(first, second, first_grads, second_grads, steps, after, before=()):
    parts = len(first)
    part_rows, model = first[0].shape
    length = parts * part_rows
    first_width = first_grads[0].shape[1] // steps
    second_width = second_grads[0].shape[1] // steps
    width = first_width + second_width
    groups = ring_groups()
    count = 2 * ring_size()
    rows = model // count
    table = shard_table([place for group in groups for place in group])
    whole = pl.BlockSpec((part_rows, model), lambda i: (0, 0))
    outs = [jax.ShapeDtypeStruct((len(group), rows, steps * width), bf16) for group in groups] * 2
    out_specs = [
        pl.BlockSpec((len(group), rows, width), lambda i: (0, 0, i)) for group in groups
    ] * 2
    results = pl.pallas_call(
        partial(weight_grad_body, parts, groups, rows, len(after)),
        grid=(steps,),
        in_specs=[pl.BlockSpec(memory_space=pltpu.SMEM)]
        + [whole] * (2 * parts)
        + [pl.BlockSpec((part_rows, first_width), lambda i: (0, i))] * parts
        + [pl.BlockSpec((part_rows, second_width), lambda i: (0, i))] * parts
        + [anywhere()] * len(after),
        out_specs=out_specs,
        out_shape=outs,
        scratch_shapes=[
            pltpu.VMEM((model, length), bf16),
            pltpu.VMEM((model, length), bf16),
            pltpu.VMEM((model, width), bf16),
        ],
        compiler_params=pltpu.CompilerParams(vmem_limit_bytes=56 * 1024 * 1024),
        cost_estimate=pl.CostEstimate(
            flops=2 * length * model * steps * width,
            bytes_accessed=4 * model * steps * width,
            transcendentals=0,
        ),
        name="weight_grads",
    )(table, *first, *second, *first_grads, *second_grads, *after)
    mine = results[: len(groups)]
    near = list(results[len(groups) :])
    if before:
        near[0] = held(near[0], before)
    near = [swap(block, "fsdp") for block in near]
    return mine, near


def ring_call(body, operands, outs, after, name):
    return pl.pallas_call(
        body,
        grid=(1,),
        in_specs=entire(operands) + [anywhere()] * len(after),
        out_specs=entire(outs),
        out_shape=outs,
        compiler_params=pltpu.CompilerParams(vmem_limit_bytes=48 * 1024 * 1024),
        name=name,
    )(*operands, *after)


def both_cores(mine, near, member):
    return mine[member].astype(f32) + near[member].astype(f32)


def open_body(cut, mine, near, *refs):
    low, high = refs[-2:]
    total = both_cores(mine, near, 0).astype(bf16)
    low[...] = total[:, :cut]
    high[...] = total[:, cut:]


def step_body(cut, mine, near, down, up, *refs):
    ahead, behind = refs[-2:]
    columns = ahead.shape[1]
    ahead_sum = both_cores(mine, near, 0)
    behind_sum = both_cores(mine, near, 1)
    if down.shape[1] == columns:
        ahead[...] = (ahead_sum + down[...].astype(f32)).astype(bf16)
        behind[...] = (behind_sum + up[...].astype(f32)).astype(bf16)
    else:
        ahead[:, :cut] = (ahead_sum[:, :cut] + down[...].astype(f32)).astype(bf16)
        ahead[:, cut:] = ahead_sum[:, cut:].astype(bf16)
        behind[:, :cut] = behind_sum[:, :cut].astype(bf16)
        behind[:, cut:] = (behind_sum[:, cut:] + up[...].astype(f32)).astype(bf16)


def close_body(pieces, mine, near, down, up, *outs):
    total = both_cores(mine, near, 0) + down[...].astype(f32) + up[...].astype(f32)
    for start, width, number, place in pieces:
        outs[number][:, place : place + width] = total[:, start : start + width]


def ring_cut(columns):
    return columns // 2 // 128 * 128


def ring_pass(sums):
    return pass_on(sums[0], 1), pass_on(sums[1], -1)


def ring_open(blocks, after=()):
    mine, near = blocks
    rows, columns = mine[0].shape[1:]
    cut = ring_cut(columns)
    outs = [jax.ShapeDtypeStruct((rows, width), bf16) for width in (cut, columns - cut)]
    sums = ring_call(partial(open_body, cut), (mine[0], near[0]), outs, after, "ring_open")
    return ring_pass(sums), tuple(sums)


def ring_step(blocks, number, state, after=()):
    mine, near = blocks[0][number], blocks[1][number]
    rows, columns = mine.shape[1:]
    outs = [jax.ShapeDtypeStruct((rows, columns), bf16)] * 2
    body = partial(step_body, ring_cut(columns))
    sums = ring_call(body, (mine, near, *state), outs, after, "ring_step")
    return ring_pass(sums), tuple(sums)


def ring_close(blocks, state, pieces):
    mine, near = blocks[0][-1], blocks[1][-1]
    rows = mine.shape[1]
    sizes = {}
    for _, width, number, place in pieces:
        sizes[number] = max(sizes.get(number, 0), place + width)
    outs = [jax.ShapeDtypeStruct((rows, sizes[number]), f32) for number in range(len(sizes))]
    return ring_call(partial(close_body, pieces), (mine, near, *state), outs, (), "ring_close")


def ffn_body(width, count, extra, *refs):
    starts, rows_in, cotangent_in = refs[:3]
    blocks = refs[3 : 3 + count]
    out, grad, pairs, hiddens, out_sum, grad_sum, weights = refs[3 + count + extra :]
    step = pl.program_id(0)
    length = rows_in.shape[0]

    @pl.when(step == 0)
    def _():
        out_sum[...] = jnp.zeros_like(out_sum)
        grad_sum[...] = jnp.zeros_like(grad_sum)

    place_rows(weights, starts, blocks)
    pair_weights = weights[:, : 2 * width]
    down = weights[:, 2 * width :]
    chunk = min(256, length)
    for start in range(0, length, chunk):
        span = pl.ds(start, chunk)
        both = dot(rows_in[span, :], pair_weights)
        gate = both[:, :width]
        up = both[:, width:]
        hidden_grad = dot(cotangent_in[span, :], down)
        sigmoid = 1.0 / (1.0 + jnp.exp(-gate))
        silu = gate * sigmoid
        hidden = (silu * up).astype(bf16)
        gate_grad = hidden_grad * up * sigmoid * (1.0 + gate * (1.0 - sigmoid))
        up_grad = hidden_grad * silu
        pair = jnp.concatenate([gate_grad.astype(bf16), up_grad.astype(bf16)], axis=1)
        hiddens[span, :] = hidden
        pairs[span, :] = pair
        out_sum[span, :] += dot_transposed(hidden, down)
        grad_sum[span, :] += dot_transposed(pair, pair_weights)

    @pl.when(step == pl.num_programs(0) - 1)
    def _():
        out[...] = out_sum[...].astype(out.dtype)
        grad[...] = grad_sum[...].astype(grad.dtype)


def hidden_width(units):
    for width in (768, 256, 384, 128):
        if units % width == 0:
            return width
    return units


def feed_forward(rows, cotangent, starts, blocks, width, kind, after):
    length, model = rows.shape
    steps = blocks[0].shape[1] // (3 * width)
    whole = pl.BlockSpec((length, model), lambda i: (0, 0))
    sums = jax.ShapeDtypeStruct((length, model), kind)
    return pl.pallas_call(
        partial(ffn_body, width, len(blocks), len(after)),
        grid=(steps,),
        in_specs=[pl.BlockSpec(memory_space=pltpu.SMEM), whole, whole]
        + [pl.BlockSpec((block.shape[0], 3 * width), lambda i: (0, i)) for block in blocks]
        + [anywhere()] * len(after),
        out_specs=[
            whole,
            whole,
            pl.BlockSpec((length, 2 * width), lambda i: (0, i)),
            pl.BlockSpec((length, width), lambda i: (0, i)),
        ],
        out_shape=[
            sums,
            sums,
            jax.ShapeDtypeStruct((length, steps * 2 * width), bf16),
            jax.ShapeDtypeStruct((length, steps * width), bf16),
        ],
        scratch_shapes=[
            pltpu.VMEM((length, model), f32),
            pltpu.VMEM((length, model), f32),
            pltpu.VMEM((model, 3 * width), bf16),
        ],
        compiler_params=pltpu.CompilerParams(vmem_limit_bytes=56 * 1024 * 1024),
        cost_estimate=pl.CostEstimate(
            flops=12 * length * model * steps * width,
            bytes_accessed=8 * model * steps * width,
            transcendentals=length * steps * width,
        ),
        name="feed_forward",
    )(starts, rows, cotangent, *blocks, *after)


def lines(start, size):
    if isinstance(start, int):
        return pl.ds(start, size)
    return pl.ds(pl.multiple_of(start, size), size)


def part_starts(place, count, part_rows):
    if count == 1:
        return [0]
    return [place[0] * part_rows, (1 - place[0]) * part_rows]


def causal_block(size):
    keys = lax.broadcasted_iota(jnp.int32, (size, size), 0)
    queries = lax.broadcasted_iota(jnp.int32, (size, size), 1)
    return keys <= queries


def attend_body(count, *refs):
    place, weights, query_gain, key_gain, cosine, sine = refs[:6]
    rows_in = refs[6 : 6 + count]
    branches = refs[6 + count : 6 + 2 * count]
    attended_out = refs[6 + 2 * count : 6 + 3 * count]
    raw, query_rows, key_rows, value_rows, attended, log_totals = refs[6 + 3 * count : 12 + 3 * count]
    rows, turned = refs[12 + 3 * count :]
    part_rows = rows_in[0].shape[0]
    length = rows.shape[0]
    heads = query_rows.shape[0] // HD
    kv_heads = key_rows.shape[0] // HD
    group_size = heads // kv_heads
    columns = (heads + 2 * kv_heads) * HD
    half = HD // 2
    starts = part_starts(place, count, part_rows)
    for part in range(count):
        rows[lines(starts[part], part_rows), :] = rows_in[part][...]

    chunk = min(256, columns)
    for first in range(0, columns, chunk):
        product = dot_transposed(weights[:, first : first + chunk].T, rows[...])
        for at in range(0, chunk, HD):
            head = (first + at) // HD
            values = product[at : at + HD]
            if head >= heads + kv_heads:
                start = (head - heads - kv_heads) * HD
                value_rows[start : start + HD, :] = values.astype(bf16)
                continue
            raw[first + at : first + at + HD, :] = values
            gain = query_gain if head < heads else key_gain
            scale = lax.rsqrt(jnp.mean(values * values, axis=0, keepdims=True) + eps)
            normed = values * scale * gain[...]
            top, bottom = normed[:half], normed[half:]
            top, bottom = (
                top * cosine[...] - bottom * sine[...],
                bottom * cosine[...] + top * sine[...],
            )
            if head < heads:
                target, start = query_rows, head * HD
                top = top.astype(bf16).astype(f32) * HD**-0.5
                bottom = bottom.astype(bf16).astype(f32) * HD**-0.5
            else:
                target, start = key_rows, (head - heads) * HD
            target[start : start + half, :] = top.astype(bf16)
            target[start + half : start + HD, :] = bottom.astype(bf16)

    block = min(256, length)
    causal = causal_block(block)

    def one_group(kv_head, carry):
        span = lines(kv_head * HD, HD)
        keys = key_rows[span, :].T
        values = value_rows[span, :]
        for member in range(group_size):
            head = kv_head * group_size + member
            for start in range(0, length, block):
                here = slice(start, start + block)
                query = query_rows[lines(head * HD, HD), here]
                weight = jnp.where(causal, jnp.exp(dot(keys[here], query)), 0.0)
                total = jnp.sum(weight, axis=0, keepdims=True)
                result = dot(values[:, here], weight.astype(bf16))
                if start:
                    weight = jnp.exp(dot(keys[:start], query))
                    total = total + jnp.sum(weight, axis=0, keepdims=True)
                    result = result + dot(values[:, :start], weight.astype(bf16))
                attended[lines(head * HD, HD), here] = (result * (1.0 / total)).astype(bf16)
                log_totals[head, :, here] = jnp.log(total)
        return carry

    lax.fori_loop(0, kv_heads, one_group, 0)
    turned[...] = attended[...].T
    for part in range(count):
        mine = turned[lines(starts[part], part_rows), :]
        attended_out[part][...] = mine
        branches[part][...] = dot_transposed(mine, weights[:, columns:]).astype(branches[part].dtype)


def attend(place, weights, query_gain, key_gain, cosine, sine, parts, query_columns, key_columns):
    count = len(parts)
    part_rows, model = parts[0].shape
    length = count * part_rows
    heads = query_columns // HD
    shape = jax.ShapeDtypeStruct
    kinds = [f32] + [bf16] * (count - 1)
    outs = (
        [shape((part_rows, model), kind) for kind in kinds]
        + [shape((part_rows, query_columns), bf16)] * count
        + [
            shape((query_columns + key_columns, length), f32),
            shape((query_columns, length), bf16),
            shape((key_columns, length), bf16),
            shape((key_columns, length), bf16),
            shape((query_columns, length), bf16),
            shape((heads, 1, length), f32),
        ]
    )
    results = pl.pallas_call(
        partial(attend_body, count),
        grid=(1,),
        in_specs=[pl.BlockSpec(memory_space=pltpu.SMEM)]
        + entire([weights, query_gain, key_gain, cosine, sine, *parts]),
        out_specs=entire(outs),
        out_shape=outs,
        scratch_shapes=[
            pltpu.VMEM((length, model), bf16),
            pltpu.VMEM((length, query_columns), bf16),
        ],
        compiler_params=pltpu.CompilerParams(vmem_limit_bytes=56 * 1024 * 1024),
        cost_estimate=pl.CostEstimate(
            flops=2 * length * model * (2 * query_columns + 2 * key_columns)
            + 8 * length * length * query_columns,
            bytes_accessed=16 * length * model,
            transcendentals=heads * length * length,
        ),
        name="attend",
    )(place, weights, query_gain, key_gain, cosine, sine, *parts)
    return results[:count], results[count : 2 * count], results[2 * count :]


def attend_back_body(count, first_group, last_group, extra, *refs):
    place, weights, query_gain, key_gain, cosine, sine = refs[:6]
    raw, query_rows, key_rows, value_rows, attended, log_totals = refs[6:12]
    branch_in = refs[12 : 12 + count]
    refs = refs[12 + count :]
    if first_group:
        earlier = refs[:3]
        refs = refs[3:]
    if last_group * HD == key_rows.shape[0]:
        normed_in = refs[:count]
        refs = refs[count:]
    refs = refs[extra:]
    last = last_group * HD == key_rows.shape[0]
    if last:
        grads, raw_grads, refs = refs[:count], refs[count : 2 * count], refs[2 * count :]
        attn_gain_grad, refs = refs[0], refs[1:]
        query_gain_grad, key_gain_grad, turned_grads = refs[:3]
        rows, attended_grad, key_sum, value_sum, straight = refs[3:]
    else:
        turned_grads, query_gain_grad, key_gain_grad = refs[:3]
        rows, attended_grad, key_sum, value_sum = refs[3:]
    part_rows = branch_in[0].shape[0]
    length = rows.shape[0]
    heads = query_rows.shape[0] // HD
    kv_heads = key_rows.shape[0] // HD
    group_size = heads // kv_heads
    columns = (heads + 2 * kv_heads) * HD
    half = HD // 2
    starts = part_starts(place, count, part_rows)
    for part in range(count):
        rows[lines(starts[part], part_rows), :] = branch_in[part][...]
    stage_rows = (last_group - first_group) * group_size * HD
    chunk = min(256, stage_rows)
    begin = first_group * group_size * HD
    for first in range(begin, begin + stage_rows, chunk):
        piece = weights[:, columns + first : columns + first + chunk].T
        attended_grad[first : first + chunk, :] = dot_transposed(piece, rows[...]).astype(bf16)
    if first_group:
        turned_grads[...] = earlier[0][...]
        query_gain_grad[...] = earlier[1][...]
        key_gain_grad[...] = earlier[2][...]
    else:
        turned_grads[...] = jnp.zeros_like(turned_grads)
        query_gain_grad[...] = jnp.zeros_like(query_gain_grad)
        key_gain_grad[...] = jnp.zeros_like(key_gain_grad)
    block = min(256, length)
    causal = causal_block(block)

    def unprepare(grad, values, gain, gain_grad):
        top, bottom = grad[:half], grad[half:]
        grad = jnp.concatenate(
            [
                top * cosine[...] + bottom * sine[...],
                bottom * cosine[...] - top * sine[...],
            ],
            axis=0,
        )
        scale = lax.rsqrt(jnp.mean(values * values, axis=0, keepdims=True) + eps)
        normed = values * scale
        gain_grad[...] += jnp.sum(grad * normed, axis=1, keepdims=True)
        grad = grad * gain[...]
        inner = jnp.mean(grad * normed, axis=0, keepdims=True)
        return (scale * (grad - normed * inner)).astype(bf16)

    def one_group(kv_head, carry):
        span = lines(kv_head * HD, HD)
        keys_turned = key_rows[span, :]
        keys = keys_turned.T
        values = value_rows[span, :].T
        key_sum[...] = jnp.zeros_like(key_sum)
        value_sum[...] = jnp.zeros_like(value_sum)
        for member in range(group_size):
            head = kv_head * group_size + member
            head_span = lines(head * HD, HD)
            query_parts = []
            for start in range(0, length, block):
                here = slice(start, start + block)
                query = query_rows[head_span, here]
                grad = attended_grad[head_span, here]
                inner = jnp.sum(
                    grad.astype(f32) * attended[head_span, here].astype(f32), axis=0, keepdims=True
                )
                log_total = log_totals[head, :, here]
                query_grad = None
                for low, high in [(start, start + block)] + ([(0, start)] if start else []):
                    prob = jnp.exp(dot(keys[low:high], query) - log_total)
                    if low == start:
                        prob = jnp.where(causal, prob, 0.0)
                    prob_grad = dot(values[low:high], grad)
                    score_grad = (prob * (prob_grad - inner)).astype(bf16)
                    piece = dot(keys_turned[:, low:high], score_grad)
                    query_grad = piece if query_grad is None else query_grad + piece
                    key_sum[:, low:high] += dot_transposed(query, score_grad)
                    value_sum[:, low:high] += dot_transposed(grad, prob.astype(bf16))
                query_parts.append(query_grad * HD**-0.5)
            turned_grads[head_span, :] = unprepare(
                jnp.concatenate(query_parts, axis=1), raw[head_span, :], query_gain, query_gain_grad
            )
        key_span = lines((heads + kv_head) * HD, HD)
        turned_grads[key_span, :] = unprepare(
            key_sum[...], raw[key_span, :], key_gain, key_gain_grad
        )
        turned_grads[lines((heads + kv_heads + kv_head) * HD, HD), :] = value_sum[...].astype(bf16)
        return carry

    lax.fori_loop(first_group, last_group, one_group, 0)
    if last:
        straight[...] = turned_grads[...].T
        for part in range(count):
            mine = straight[lines(starts[part], part_rows), :]
            raw_grads[part][...] = mine
            grad = dot_transposed(mine, weights[:, :columns])
            grads[part][...] = grad.astype(grads[part].dtype)
            gain_sum = jnp.sum(grad * normed_in[part][...].astype(f32), axis=0, keepdims=True)
            attn_gain_grad[...] = attn_gain_grad[...] + gain_sum if part else gain_sum


def back_stages(kept):
    kv_heads = kept[2].shape[0] // HD
    if kv_heads % 4:
        return [(0, kv_heads)]
    quarter = kv_heads // 4
    return [(0, quarter), (quarter, 3 * quarter), (3 * quarter, kv_heads)]


def attend_back(fixed, kept, parts, normed, stage, earlier, after):
    count = len(parts)
    first_group, last_group = stage
    kv_heads = kept[2].shape[0] // HD
    part_rows, model = parts[0].shape
    length = count * part_rows
    query_columns = kept[1].shape[0]
    columns = query_columns + 2 * kept[2].shape[0]
    shape = jax.ShapeDtypeStruct
    last = last_group == kv_heads
    normed = normed if last else ()
    share = kv_heads // (last_group - first_group)
    gains = [shape((HD, 1), f32)] * 2
    turned = shape((columns, length), bf16)
    scratch = [
        pltpu.VMEM((length, model), bf16),
        pltpu.VMEM((query_columns, length), bf16),
        pltpu.VMEM((HD, length), f32),
        pltpu.VMEM((HD, length), f32),
    ]
    if last:
        outs = (
            [shape((part_rows, model), kind) for kind in [f32] + [bf16] * (count - 1)]
            + [shape((part_rows, columns), bf16)] * count
            + [shape((1, model), f32)]
            + gains
        )
        scratch = [pltpu.VMEM(turned.shape, bf16)] + scratch + [pltpu.VMEM((length, columns), bf16)]
    else:
        outs = [turned] + gains
    results = pl.pallas_call(
        partial(attend_back_body, count, first_group, last_group, len(after)),
        grid=(1,),
        in_specs=[pl.BlockSpec(memory_space=pltpu.SMEM)]
        + entire([*fixed[1:], *kept, *parts, *earlier, *normed])
        + [anywhere()] * len(after),
        out_specs=entire(outs),
        out_shape=outs,
        scratch_shapes=scratch,
        compiler_params=pltpu.CompilerParams(vmem_limit_bytes=56 * 1024 * 1024),
        cost_estimate=pl.CostEstimate(
            flops=(
                2 * length * model * (query_columns + columns)
                + 20 * length * length * query_columns
            )
            // share,
            bytes_accessed=16 * length * model,
            transcendentals=query_columns // HD * length * length // share,
        ),
        name="attend_back",
    )(*fixed, *kept, *parts, *earlier, *normed, *after)
    if not last:
        return results
    return results[:count], results[count : 2 * count], *results[2 * count :]


def on_device(
    tokens,
    out_cotangent,
    attn_gain,
    query_weight,
    key_weight,
    value_weight,
    query_gain,
    key_gain,
    out_weight,
    ffn_gain,
    gate_weight,
    up_weight,
    down_weight,
):
    shard, query_columns = query_weight.shape
    key_columns = key_weight.shape[1]
    qkv_columns = query_columns + 2 * key_columns
    units = gate_weight.shape[1]
    width = hidden_width(units)
    steps = units // width
    pieces = (query_weight, key_weight, value_weight, out_weight.T)
    firsts = [0, query_columns, query_columns + key_columns, qkv_columns]
    places = [(at, 0, firsts[at], piece.shape[1]) for at, piece in enumerate(pieces)]
    attn_starts, attn_blocks, attn_arrived = gather_ring(pack(pieces, places, ()), {})
    rows_in_all = shard * lax.axis_size("fsdp")
    attn_full = assemble(attn_starts, gather_near(attn_blocks), rows_in_all)
    pieces = (gate_weight, up_weight, down_weight.T)
    places = [
        (at, step * width, (3 * step + at) * width, width)
        for step in range(steps)
        for at in range(3)
    ]
    ffn_shard = pack(pieces, places, attn_arrived[-2])

    residual = tokens.astype(f32)
    normed, attn_norm_pull = jax.vjp(rms_norm, residual, attn_gain)
    normed_parts = widen(normed.astype(bf16))
    if len(normed_parts) == 2:
        cotangent_parts = widen(held(out_cotangent, normed_parts[1:]))
    else:
        cotangent_parts = widen(out_cotangent)
    length = len(normed_parts) * normed_parts[0].shape[0]
    cosine, sine = rotary_tables(length)
    place = lax.axis_index("tp").astype(jnp.int32).reshape(1)
    fixed = (place, attn_full, query_gain[:, None], key_gain[:, None], cosine, sine)
    branch, attended, kept = attend(*fixed, normed_parts, query_columns, key_columns)
    ready = {2: [branch[0]]}
    ffn_starts, ffn_pieces, ffn_arrived = gather_ring(ffn_shard, ready)
    branch = [*branch[:-1], held(branch[-1], (*cotangent_parts[1:], *ffn_arrived[0]))]
    middle = residual + narrow(branch)
    normed_ffn, ffn_norm_pull = jax.vjp(rms_norm, middle, ffn_gain)
    ffn_parts = widen(normed_ffn.astype(bf16))
    ffn_pieces = gather_near(ffn_pieces, ffn_parts[1:])
    results = []
    for at in reversed(range(len(ffn_parts))):
        after = [results[-1][1]] if results else []
        results.append(
            feed_forward(
                ffn_parts[at],
                cotangent_parts[at],
                ffn_starts,
                ffn_pieces,
                width,
                bf16 if at else f32,
                after,
            )
        )
    out_parts, grad_parts, pairs, hiddens = (list(item) for item in zip(*results[::-1]))
    ffn_normed_grad = narrow(grad_parts)
    middle_piece, ffn_gain_local = ffn_norm_pull(ffn_normed_grad)
    middle_grad = out_cotangent.astype(f32) + middle_piece
    branch_parts = widen(middle_grad.astype(bf16))

    ffn_blocks = weight_grads(
        ffn_parts,
        cotangent_parts,
        pairs,
        hiddens,
        steps,
        (branch_parts[0],),
        branch_parts[1:],
    )
    ffn_state, sent = ring_open(ffn_blocks)
    ffn_next, attn_next, last = 1, 1, ring_size() // 2
    out_other = [narrow_send(held(out_parts[-1], branch_parts[1:]))] if len(out_parts) == 2 else []
    back = ()
    for stage in back_stages(kept):
        back = attend_back(fixed, kept, branch_parts, normed_parts, stage, back, sent)
        done = back[1] if len(back) == 3 else back[2]
        if ffn_next < last:
            after = (done, *out_other) if ffn_next == 2 else (done,)
            ffn_state, sent = ring_step(ffn_blocks, ffn_next, ffn_state, after)
            ffn_next += 1
    if out_other:
        output = middle + out_parts[0] + out_other[0].astype(f32)
    else:
        output = middle + narrow(out_parts)
    output = output.astype(bf16)
    normed_grad, qkv_grad, attn_gain_local, query_gain_local, key_gain_local = back
    gains = jnp.concatenate(
        [
            attn_gain_local[0] / attn_gain,
            ffn_gain_local,
            query_gain_local[:, 0],
            key_gain_local[:, 0],
        ]
    )
    rounds = sum_rounds()
    grad_other = ()
    if len(normed_grad) == 2:
        grad_other = (narrow_send(held(normed_grad[1], sent)),)
        normed_grad = normed_grad[0] + grad_other[0].astype(f32)
    else:
        normed_grad = narrow(normed_grad)
    attn_blocks = weight_grads(normed_parts, branch_parts, qkv_grad, attended, 1, sent)
    while rounds and (rounds[0][0] == "tp" or rounds[0][1] == 1):
        gains = gains + swap(gains, *rounds.pop(0))
    attn_state, sent = ring_open(attn_blocks, (gains,))
    while ffn_next < last or attn_next < last:
        if ffn_next < last:
            ffn_state, sent = ring_step(ffn_blocks, ffn_next, ffn_state)
            ffn_next += 1
        if attn_next < last:
            if rounds:
                gains = gains + swap(held(gains, sent), *rounds.pop(0))
            after = (*sent, gains) if attn_next < 2 else (*sent, gains, *grad_other)
            attn_state, sent = ring_step(attn_blocks, attn_next, attn_state, after)
            attn_next += 1
    for axis_name, bit in rounds:
        gains = gains + swap(gains, axis_name, bit)
    ffn_places = [
        (step * 3 * width + number * width, width, number, step * width)
        for step in range(steps)
        for number in range(3)
    ]
    gate_grad, up_grad, down_grad = ring_close(ffn_blocks, ffn_state, ffn_places)
    attn_places = [
        (0, query_columns, 0, 0),
        (query_columns, key_columns, 1, 0),
        (query_columns + key_columns, key_columns, 2, 0),
        (qkv_columns, query_columns, 3, 0),
    ]
    query_grad, key_grad, value_grad, out_grad = ring_close(attn_blocks, attn_state, attn_places)
    tokens_piece, _ = attn_norm_pull(normed_grad)
    tokens_grad = middle_grad + tokens_piece
    model = attn_gain.shape[0]
    return (
        output,
        tokens_grad,
        gains[:model],
        query_grad,
        key_grad,
        value_grad,
        gains[2 * model : 2 * model + HD],
        gains[2 * model + HD :],
        out_grad.T,
        gains[model : 2 * model],
        gate_grad,
        up_grad,
        down_grad.T,
    )


def solution(mesh):
    placed = (
        P(("fsdp", "tp"), None),
        P(("fsdp", "tp"), None),
        P(),
        P("fsdp", "tp"),
        P("fsdp", "tp"),
        P("fsdp", "tp"),
        P(),
        P(),
        P("tp", "fsdp"),
        P(),
        P("fsdp", "tp"),
        P("fsdp", "tp"),
        P("tp", "fsdp"),
    )
    return jax.shard_map(
        on_device,
        mesh=mesh,
        in_specs=placed,
        out_specs=(
            P(("fsdp", "tp"), None),
            P(("fsdp", "tp"), None),
            P(),
            P("fsdp", "tp"),
            P("fsdp", "tp"),
            P("fsdp", "tp"),
            P(),
            P(),
            P("tp", "fsdp"),
            P(),
            P("fsdp", "tp"),
            P("fsdp", "tp"),
            P("tp", "fsdp"),
        ),
        check_vma=False,
    )
```

```python
from functools import partial

import jax
import jax.numpy as jnp
from jax import lax
from jax.experimental import pallas as pl
from jax.experimental.pallas import tpu as pltpu
from jax.sharding import PartitionSpec as P

HD = 64

eps = 1e-05
theta_base = 1000000.0
f32 = jnp.float32
bf16 = jnp.bfloat16


def rms_norm(values, gain):
    return values * lax.rsqrt(jnp.mean(values * values, axis=-1, keepdims=True) + eps) * gain


def rotary_tables(length):
    half_size = HD // 2
    frequency = theta_base ** (-jnp.arange(half_size, dtype=f32) * 2.0 / HD)
    angles = frequency[:, None] * jnp.arange(length, dtype=f32)[None, :]
    return (jnp.cos(angles), jnp.sin(angles))


def dot(former, latter):
    return jnp.dot(former, latter, preferred_element_type=f32)


def dot_transposed(former, latter):
    return lax.dot_general(former, latter, (((1,), (1,)), ((), ())), preferred_element_type=f32)


def dot_leading(former, latter):
    return lax.dot_general(former, latter, (((0,), (0,)), ((), ())), preferred_element_type=f32)


def swap(values, axis_name, bit=1):
    count = lax.axis_size(axis_name)
    return lax.ppermute(values, axis_name, [(i, i ^ bit) for i in range(count)])


def anywhere():
    return pl.BlockSpec(memory_space=pl.ANY)


def entire(arrays):
    return [pl.BlockSpec(array.shape, lambda i, rank=array.ndim: (0,) * rank) for array in arrays]


def held_all(arrays, after):
    count = len(arrays)
    return pl.pallas_call(
        lambda *refs: None,
        in_specs=[anywhere()] * (count + len(after)),
        out_specs=[anywhere()] * count,
        out_shape=[jax.ShapeDtypeStruct(array.shape, array.dtype) for array in arrays],
        input_output_aliases={at: at for at in range(count)},
        name="held",
    )(*arrays, *after)


def held(values, after):
    return held_all([values], after)[0]


def widen(rows):
    if lax.axis_size("tp") == 2:
        return (rows, swap(rows, "tp"))
    return (lax.all_gather(rows, "tp", axis=0, tiled=True),)


def narrow_send(part):
    return swap(part.astype(bf16), "tp")


def narrow(parts):
    if len(parts) == 2:
        return parts[0].astype(f32) + narrow_send(parts[1]).astype(f32)
    return lax.psum_scatter(
        parts[0].astype(bf16), "tp", scatter_dimension=0, tiled=True
    ).astype(f32)


def sum_rounds():
    return [
        (axis_name, 1 << bit)
        for axis_name in ("tp", "fsdp")
        for bit in range(lax.axis_size(axis_name).bit_length() - 1)
    ]


def ring_size():
    return lax.axis_size("fsdp") // 2


def chip_at(place):
    chips = ring_size()
    if isinstance(place, int):
        return 2 * place if place < chips // 2 else 2 * (chips - 1 - place) + 1
    return jnp.where(place < chips // 2, 2 * place, 2 * (chips - 1 - place) + 1)


def own_place():
    chip = lax.axis_index("fsdp") // 2
    return jnp.where(chip % 2 == 0, chip // 2, ring_size() - 1 - chip // 2)


def pass_on(values, direction):
    chips = ring_size()
    pairs = [
        (2 * chip_at(place) + core, 2 * chip_at((place + direction) % chips) + core)
        for place in range(chips)
        for core in range(2)
    ]
    return lax.ppermute(values, "fsdp", pairs)


def shard_table(ahead):
    core = lax.axis_index("fsdp") % 2
    chips = chip_at((own_place() + jnp.array(ahead, jnp.int32)) % ring_size())
    return jnp.concatenate([2 * chips + core, 2 * chips + 1 - core]).astype(jnp.int32)


def gather_ring(shard, ready):
    rows = shard.shape[0]
    half = rows // 2
    chips = ring_size()
    blocks, ahead, offset, arrived = [], [0], [0], []
    sent = [shard]
    for step in range(1, chips // 2 + 1):
        if step in ready:
            sent = held_all(sent, ready[step])
        blocks += sent
        down, up = sent[0], sent[-1]
        if step == chips // 2:
            down, up = down[:half], up[half:]
        sent = [pass_on(down, 1), pass_on(up, -1)]
        arrived.append(sent)
        ahead += [chips - step, step]
        offset += [0, half if step == chips // 2 else 0]
    blocks += sent
    starts = shard_table(ahead) * rows + jnp.array(offset * 2, jnp.int32)
    return starts, blocks, arrived


def gather_near(blocks, ready=()):
    ends = held_all(blocks[-2:], ready) if ready else blocks[-2:]
    blocks = [*blocks[:-2], *ends]
    return blocks + [swap(block, "fsdp") for block in blocks]


def place_rows(whole, starts, blocks):
    for at, block in enumerate(blocks):
        whole[pl.ds(pl.multiple_of(starts[at], 16), block.shape[0]), :] = block[...]


def assemble_body(starts, *refs):
    place_rows(refs[-1], starts, refs[:-1])


def assemble(starts, blocks, rows):
    out = jax.ShapeDtypeStruct((rows, blocks[0].shape[1]), bf16)
    return pl.pallas_call(
        assemble_body,
        grid=(1,),
        in_specs=[pl.BlockSpec(memory_space=pltpu.SMEM)] + entire(blocks),
        out_specs=entire([out])[0],
        out_shape=out,
        compiler_params=pltpu.CompilerParams(vmem_limit_bytes=48 * 1024 * 1024),
        name="assemble",
    )(starts, *blocks)


def pack_body(places, *refs):
    whole = refs[-1]
    for number, source, start, width in places:
        whole[:, start : start + width] = refs[number][:, source : source + width]


def pack(arrays, places, after):
    columns = max(start + width for _, _, start, width in places)
    out = jax.ShapeDtypeStruct((arrays[0].shape[0], columns), bf16)
    return pl.pallas_call(
        partial(pack_body, places),
        grid=(1,),
        in_specs=entire(arrays) + [anywhere()] * len(after),
        out_specs=entire([out])[0],
        out_shape=out,
        compiler_params=pltpu.CompilerParams(vmem_limit_bytes=32 * 1024 * 1024),
        name="pack",
    )(*arrays, *after)


def ring_groups():
    chips = ring_size()
    middle = [[chips // 2 - step, chips // 2 + step] for step in range(1, chips // 2)]
    return [[chips // 2]] + middle + [[0]]


def weight_grad_body(parts, groups, rows, extra, *refs):
    table = refs[0]
    first_in = refs[1 : 1 + parts]
    second_in = refs[1 + parts : 1 + 2 * parts]
    first_grads = refs[1 + 2 * parts : 1 + 3 * parts]
    second_grads = refs[1 + 3 * parts : 1 + 4 * parts]
    outs = refs[1 + 4 * parts + extra : -3]
    first_turned, second_turned, total = refs[-3:]
    part_rows = first_in[0].shape[0]
    first_width = first_grads[0].shape[1]

    @pl.when(pl.program_id(0) == 0)
    def _():
        for part in range(parts):
            span = pl.ds(part * part_rows, part_rows)
            first_turned[:, span] = first_in[part][...].T
            second_turned[:, span] = second_in[part][...].T

    def joined(pieces):
        if parts == 1:
            return pieces[0][...]
        return jnp.concatenate([piece[...] for piece in pieces], axis=0)

    total[:, :first_width] = dot(first_turned[...], joined(first_grads)).astype(bf16)
    total[:, first_width:] = dot(second_turned[...], joined(second_grads)).astype(bf16)
    count = sum(len(group) for group in groups)
    at = 0
    for number, group in enumerate(groups):
        for member in range(len(group)):
            mine = pl.multiple_of(table[at] * rows, rows)
            outs[number][member] = total[pl.ds(mine, rows), :]
            near = pl.multiple_of(table[count + at] * rows, rows)
            outs[len(groups) + number][member] = total[pl.ds(near, rows), :]
            at += 1


def weight_grads(first, second, first_grads, second_grads, steps, after, before=()):
    parts = len(first)
    part_rows, model = first[0].shape
    length = parts * part_rows
    first_width = first_grads[0].shape[1] // steps
    second_width = second_grads[0].shape[1] // steps
    width = first_width + second_width
    groups = ring_groups()
    count = 2 * ring_size()
    rows = model // count
    table = shard_table([place for group in groups for place in group])
    whole = pl.BlockSpec((part_rows, model), lambda i: (0, 0))
    outs = [jax.ShapeDtypeStruct((len(group), rows, steps * width), bf16) for group in groups] * 2
    out_specs = [
        pl.BlockSpec((len(group), rows, width), lambda i: (0, 0, i)) for group in groups
    ] * 2
    results = pl.pallas_call(
        partial(weight_grad_body, parts, groups, rows, len(after)),
        grid=(steps,),
        in_specs=[pl.BlockSpec(memory_space=pltpu.SMEM)]
        + [whole] * (2 * parts)
        + [pl.BlockSpec((part_rows, first_width), lambda i: (0, i))] * parts
        + [pl.BlockSpec((part_rows, second_width), lambda i: (0, i))] * parts
        + [anywhere()] * len(after),
        out_specs=out_specs,
        out_shape=outs,
        scratch_shapes=[
            pltpu.VMEM((model, length), bf16),
            pltpu.VMEM((model, length), bf16),
            pltpu.VMEM((model, width), bf16),
        ],
        compiler_params=pltpu.CompilerParams(vmem_limit_bytes=56 * 1024 * 1024),
        cost_estimate=pl.CostEstimate(
            flops=2 * length * model * steps * width,
            bytes_accessed=4 * model * steps * width,
            transcendentals=0,
        ),
        name="weight_grads",
    )(table, *first, *second, *first_grads, *second_grads, *after)
    mine = results[: len(groups)]
    near = list(results[len(groups) :])
    if before:
        near[0] = held(near[0], before)
    near = [swap(block, "fsdp") for block in near]
    return mine, near


def ring_call(body, operands, outs, after, name):
    return pl.pallas_call(
        body,
        grid=(1,),
        in_specs=entire(operands) + [anywhere()] * len(after),
        out_specs=entire(outs),
        out_shape=outs,
        compiler_params=pltpu.CompilerParams(vmem_limit_bytes=48 * 1024 * 1024),
        name=name,
    )(*operands, *after)


def both_cores(mine, near, member):
    return mine[member].astype(f32) + near[member].astype(f32)


def open_body(cut, mine, near, *refs):
    low, high = refs[-2:]
    total = both_cores(mine, near, 0).astype(bf16)
    low[...] = total[:, :cut]
    high[...] = total[:, cut:]


def step_body(cut, mine, near, down, up, *refs):
    ahead, behind = refs[-2:]
    columns = ahead.shape[1]
    ahead_sum = both_cores(mine, near, 0)
    behind_sum = both_cores(mine, near, 1)
    if down.shape[1] == columns:
        ahead[...] = (ahead_sum + down[...].astype(f32)).astype(bf16)
        behind[...] = (behind_sum + up[...].astype(f32)).astype(bf16)
    else:
        ahead[:, :cut] = (ahead_sum[:, :cut] + down[...].astype(f32)).astype(bf16)
        ahead[:, cut:] = ahead_sum[:, cut:].astype(bf16)
        behind[:, :cut] = behind_sum[:, :cut].astype(bf16)
        behind[:, cut:] = (behind_sum[:, cut:] + up[...].astype(f32)).astype(bf16)


def close_body(pieces, mine, near, down, up, *outs):
    total = both_cores(mine, near, 0) + down[...].astype(f32) + up[...].astype(f32)
    for start, width, number, place in pieces:
        outs[number][:, place : place + width] = total[:, start : start + width]


def ring_cut(columns):
    return columns // 2 // 128 * 128


def ring_pass(sums):
    return pass_on(sums[0], 1), pass_on(sums[1], -1)


def ring_open(blocks, after=()):
    mine, near = blocks
    rows, columns = mine[0].shape[1:]
    cut = ring_cut(columns)
    outs = [jax.ShapeDtypeStruct((rows, width), bf16) for width in (cut, columns - cut)]
    sums = ring_call(partial(open_body, cut), (mine[0], near[0]), outs, after, "ring_open")
    return ring_pass(sums), tuple(sums)


def ring_step(blocks, number, state, after=()):
    mine, near = blocks[0][number], blocks[1][number]
    rows, columns = mine.shape[1:]
    outs = [jax.ShapeDtypeStruct((rows, columns), bf16)] * 2
    body = partial(step_body, ring_cut(columns))
    sums = ring_call(body, (mine, near, *state), outs, after, "ring_step")
    return ring_pass(sums), tuple(sums)


def ring_close(blocks, state, pieces):
    mine, near = blocks[0][-1], blocks[1][-1]
    rows = mine.shape[1]
    sizes = {}
    for _, width, number, place in pieces:
        sizes[number] = max(sizes.get(number, 0), place + width)
    outs = [jax.ShapeDtypeStruct((rows, sizes[number]), f32) for number in range(len(sizes))]
    return ring_call(partial(close_body, pieces), (mine, near, *state), outs, (), "ring_close")


def ffn_body(width, count, extra, *refs):
    starts, rows_in, cotangent_in = refs[:3]
    blocks = refs[3 : 3 + count]
    out, grad, pairs, hiddens, out_sum, grad_sum, weights = refs[3 + count + extra :]
    step = pl.program_id(0)
    length = rows_in.shape[0]

    @pl.when(step == 0)
    def _():
        out_sum[...] = jnp.zeros_like(out_sum)
        grad_sum[...] = jnp.zeros_like(grad_sum)

    place_rows(weights, starts, blocks)
    pair_weights = weights[:, : 2 * width]
    down = weights[:, 2 * width :]
    chunk = min(256, length)
    for start in range(0, length, chunk):
        span = pl.ds(start, chunk)
        both = dot(rows_in[span, :], pair_weights)
        gate = both[:, :width]
        up = both[:, width:]
        hidden_grad = dot(cotangent_in[span, :], down)
        sigmoid = 0.5 + 0.5 * jnp.tanh(0.5 * gate)
        silu = gate * sigmoid
        hidden = (silu * up).astype(bf16)
        gate_grad = hidden_grad * up * (sigmoid + silu * (1.0 - sigmoid))
        up_grad = hidden_grad * silu
        pair = jnp.concatenate([gate_grad.astype(bf16), up_grad.astype(bf16)], axis=1)
        hiddens[span, :] = hidden
        pairs[span, :] = pair
        out_sum[span, :] += dot_transposed(hidden, down)
        grad_sum[span, :] += dot_transposed(pair, pair_weights)

    @pl.when(step == pl.num_programs(0) - 1)
    def _():
        out[...] = out_sum[...].astype(out.dtype)
        grad[...] = grad_sum[...].astype(grad.dtype)


def hidden_width(units):
    for width in (768, 256, 384, 128):
        if units % width == 0:
            return width
    return units


def feed_forward(rows, cotangent, starts, blocks, width, kind, after):
    length, model = rows.shape
    steps = blocks[0].shape[1] // (3 * width)
    whole = pl.BlockSpec((length, model), lambda i: (0, 0))
    sums = jax.ShapeDtypeStruct((length, model), kind)
    return pl.pallas_call(
        partial(ffn_body, width, len(blocks), len(after)),
        grid=(steps,),
        in_specs=[pl.BlockSpec(memory_space=pltpu.SMEM), whole, whole]
        + [pl.BlockSpec((block.shape[0], 3 * width), lambda i: (0, i)) for block in blocks]
        + [anywhere()] * len(after),
        out_specs=[
            whole,
            whole,
            pl.BlockSpec((length, 2 * width), lambda i: (0, i)),
            pl.BlockSpec((length, width), lambda i: (0, i)),
        ],
        out_shape=[
            sums,
            sums,
            jax.ShapeDtypeStruct((length, steps * 2 * width), bf16),
            jax.ShapeDtypeStruct((length, steps * width), bf16),
        ],
        scratch_shapes=[
            pltpu.VMEM((length, model), f32),
            pltpu.VMEM((length, model), f32),
            pltpu.VMEM((model, 3 * width), bf16),
        ],
        compiler_params=pltpu.CompilerParams(vmem_limit_bytes=56 * 1024 * 1024),
        cost_estimate=pl.CostEstimate(
            flops=12 * length * model * steps * width,
            bytes_accessed=8 * model * steps * width,
            transcendentals=length * steps * width,
        ),
        name="feed_forward",
    )(starts, rows, cotangent, *blocks, *after)


def lines(start, size):
    if isinstance(start, int):
        return pl.ds(start, size)
    return pl.ds(pl.multiple_of(start, size), size)


def part_starts(place, count, part_rows):
    if count == 1:
        return [0]
    return [place[0] * part_rows, (1 - place[0]) * part_rows]


def causal_block(size):
    keys = lax.broadcasted_iota(jnp.int32, (size, size), 0)
    queries = lax.broadcasted_iota(jnp.int32, (size, size), 1)
    return keys <= queries


def attend_body(count, extra, *refs):
    place, weights, query_gain, key_gain, cosine, sine = refs[:6]
    rows_in = refs[6 : 6 + count]
    refs = refs[:6] + refs[6 + extra :]
    branches = refs[6 + count : 6 + 2 * count]
    attended_out = refs[6 + 2 * count : 6 + 3 * count]
    raw, query_rows, key_rows, value_rows, attended, log_totals = refs[6 + 3 * count : 12 + 3 * count]
    rows, turned = refs[12 + 3 * count :]
    part_rows = rows_in[0].shape[0]
    length = rows.shape[0]
    heads = query_rows.shape[0] // HD
    kv_heads = key_rows.shape[0] // HD
    group_size = heads // kv_heads
    columns = (heads + 2 * kv_heads) * HD
    half = HD // 2
    starts = part_starts(place, count, part_rows)
    for part in range(count):
        rows[lines(starts[part], part_rows), :] = rows_in[part][...]

    chunk = min(256, columns)
    for first in range(0, columns, chunk):
        product = dot_transposed(weights[:, first : first + chunk].T, rows[...])
        for at in range(0, chunk, HD):
            head = (first + at) // HD
            values = product[at : at + HD]
            if head >= heads + kv_heads:
                start = (head - heads - kv_heads) * HD
                value_rows[start : start + HD, :] = values.astype(bf16)
                continue
            raw[first + at : first + at + HD, :] = values
            gain = query_gain if head < heads else key_gain
            scale = lax.rsqrt(jnp.mean(values * values, axis=0, keepdims=True) + eps)
            normed = values * scale * gain[...]
            top, bottom = normed[:half], normed[half:]
            top, bottom = (
                top * cosine[...] - bottom * sine[...],
                bottom * cosine[...] + top * sine[...],
            )
            if head < heads:
                target, start = query_rows, head * HD
                top = top.astype(bf16).astype(f32) * HD**-0.5
                bottom = bottom.astype(bf16).astype(f32) * HD**-0.5
            else:
                target, start = key_rows, (head - heads) * HD
            target[start : start + half, :] = top.astype(bf16)
            target[start + half : start + HD, :] = bottom.astype(bf16)

    block = min(256, length)
    causal = causal_block(block)

    def one_group(kv_head, carry):
        span = lines(kv_head * HD, HD)
        keys = key_rows[span, :].T
        values = value_rows[span, :]
        for member in range(group_size):
            head = kv_head * group_size + member
            for start in range(0, length, block):
                here = slice(start, start + block)
                query = query_rows[lines(head * HD, HD), here]
                weight = jnp.where(causal, jnp.exp(dot(keys[here], query)), 0.0)
                total = jnp.sum(weight, axis=0, keepdims=True)
                result = dot(values[:, here], weight.astype(bf16))
                if start:
                    weight = jnp.exp(dot(keys[:start], query))
                    total = total + jnp.sum(weight, axis=0, keepdims=True)
                    result = result + dot(values[:, :start], weight.astype(bf16))
                attended[lines(head * HD, HD), here] = (result * (1.0 / total)).astype(bf16)
                log_totals[head, :, here] = jnp.log(total)
        return carry

    lax.fori_loop(0, kv_heads, one_group, 0)
    turned[...] = attended[...].T
    for part in range(count):
        mine = turned[lines(starts[part], part_rows), :]
        attended_out[part][...] = mine
        branches[part][...] = dot_transposed(mine, weights[:, columns:]).astype(branches[part].dtype)


def attend(
    place, weights, query_gain, key_gain, cosine, sine, parts, query_columns, key_columns, after
):
    count = len(parts)
    part_rows, model = parts[0].shape
    length = count * part_rows
    heads = query_columns // HD
    shape = jax.ShapeDtypeStruct
    kinds = [f32] + [bf16] * (count - 1)
    outs = (
        [shape((part_rows, model), kind) for kind in kinds]
        + [shape((part_rows, query_columns), bf16)] * count
        + [
            shape((query_columns + key_columns, length), f32),
            shape((query_columns, length), bf16),
            shape((key_columns, length), bf16),
            shape((key_columns, length), bf16),
            shape((query_columns, length), bf16),
            shape((heads, 1, length), f32),
        ]
    )
    results = pl.pallas_call(
        partial(attend_body, count, len(after)),
        grid=(1,),
        in_specs=[pl.BlockSpec(memory_space=pltpu.SMEM)]
        + entire([weights, query_gain, key_gain, cosine, sine, *parts])
        + [anywhere()] * len(after),
        out_specs=entire(outs),
        out_shape=outs,
        scratch_shapes=[
            pltpu.VMEM((length, model), bf16),
            pltpu.VMEM((length, query_columns), bf16),
        ],
        compiler_params=pltpu.CompilerParams(vmem_limit_bytes=56 * 1024 * 1024),
        cost_estimate=pl.CostEstimate(
            flops=2 * length * model * (2 * query_columns + 2 * key_columns)
            + 8 * length * length * query_columns,
            bytes_accessed=16 * length * model,
            transcendentals=heads * length * length,
        ),
        name="attend",
    )(place, weights, query_gain, key_gain, cosine, sine, *parts, *after)
    return results[:count], results[count : 2 * count], results[2 * count :]


def attend_back_body(count, first_group, last_group, extra, *refs):
    place, weights, query_gain, key_gain, cosine, sine = refs[:6]
    raw, query_rows, key_rows, value_rows, attended, log_totals = refs[6:12]
    branch_in = refs[12 : 12 + count]
    refs = refs[12 + count :]
    if first_group:
        earlier = refs[:3]
        refs = refs[3:]
    if last_group * HD == key_rows.shape[0]:
        normed_in = refs[:count]
        refs = refs[count:]
    refs = refs[extra:]
    last = last_group * HD == key_rows.shape[0]
    if last:
        grads, raw_grads, refs = refs[:count], refs[count : 2 * count], refs[2 * count :]
        attn_gain_grad, refs = refs[0], refs[1:]
        query_gain_grad, key_gain_grad, turned_grads = refs[:3]
        rows, attended_grad, key_sum, value_sum, straight = refs[3:]
    else:
        turned_grads, query_gain_grad, key_gain_grad = refs[:3]
        rows, attended_grad, key_sum, value_sum = refs[3:]
    part_rows = branch_in[0].shape[0]
    length = rows.shape[0]
    heads = query_rows.shape[0] // HD
    kv_heads = key_rows.shape[0] // HD
    group_size = heads // kv_heads
    columns = (heads + 2 * kv_heads) * HD
    half = HD // 2
    starts = part_starts(place, count, part_rows)
    for part in range(count):
        rows[lines(starts[part], part_rows), :] = branch_in[part][...]
    stage_rows = (last_group - first_group) * group_size * HD
    chunk = min(256, stage_rows)
    begin = first_group * group_size * HD
    for first in range(begin, begin + stage_rows, chunk):
        piece = weights[:, columns + first : columns + first + chunk].T
        attended_grad[first : first + chunk, :] = dot_transposed(piece, rows[...]).astype(bf16)
    if first_group:
        turned_grads[...] = earlier[0][...]
        query_gain_grad[...] = earlier[1][...]
        key_gain_grad[...] = earlier[2][...]
    else:
        turned_grads[...] = jnp.zeros_like(turned_grads)
        query_gain_grad[...] = jnp.zeros_like(query_gain_grad)
        key_gain_grad[...] = jnp.zeros_like(key_gain_grad)
    block = min(256, length)
    causal = causal_block(block)

    def unprepare(grad, values, gain, gain_grad):
        top, bottom = grad[:half], grad[half:]
        grad = jnp.concatenate(
            [
                top * cosine[...] + bottom * sine[...],
                bottom * cosine[...] - top * sine[...],
            ],
            axis=0,
        )
        scale = lax.rsqrt(jnp.mean(values * values, axis=0, keepdims=True) + eps)
        normed = values * scale
        gain_grad[...] += jnp.sum(grad * normed, axis=1, keepdims=True)
        grad = grad * gain[...]
        inner = jnp.mean(grad * normed, axis=0, keepdims=True)
        return (scale * (grad - normed * inner)).astype(bf16)

    def one_group(kv_head, carry):
        span = lines(kv_head * HD, HD)
        keys_turned = key_rows[span, :]
        keys = keys_turned.T
        values = value_rows[span, :].T
        key_sum[...] = jnp.zeros_like(key_sum)
        value_sum[...] = jnp.zeros_like(value_sum)
        for member in range(group_size):
            head = kv_head * group_size + member
            head_span = lines(head * HD, HD)
            query_parts = []
            for start in range(0, length, block):
                here = slice(start, start + block)
                query = query_rows[head_span, here]
                grad = attended_grad[head_span, here]
                inner = jnp.sum(
                    grad.astype(f32) * attended[head_span, here].astype(f32), axis=0, keepdims=True
                )
                log_total = log_totals[head, :, here]
                query_grad = None
                for low, high in [(start, start + block)] + ([(0, start)] if start else []):
                    prob = jnp.exp(dot(keys[low:high], query) - log_total)
                    if low == start:
                        prob = jnp.where(causal, prob, 0.0)
                    prob_grad = dot(values[low:high], grad)
                    score_grad = (prob * (prob_grad - inner)).astype(bf16)
                    piece = dot(keys_turned[:, low:high], score_grad)
                    query_grad = piece if query_grad is None else query_grad + piece
                    key_sum[:, low:high] += dot_transposed(query, score_grad)
                    value_sum[:, low:high] += dot_transposed(grad, prob.astype(bf16))
                query_parts.append(query_grad * HD**-0.5)
            turned_grads[head_span, :] = unprepare(
                jnp.concatenate(query_parts, axis=1), raw[head_span, :], query_gain, query_gain_grad
            )
        key_span = lines((heads + kv_head) * HD, HD)
        turned_grads[key_span, :] = unprepare(
            key_sum[...], raw[key_span, :], key_gain, key_gain_grad
        )
        turned_grads[lines((heads + kv_heads + kv_head) * HD, HD), :] = value_sum[...].astype(bf16)
        return carry

    lax.fori_loop(first_group, last_group, one_group, 0)
    if last:
        straight[...] = turned_grads[...].T
        for part in range(count):
            mine = straight[lines(starts[part], part_rows), :]
            raw_grads[part][...] = mine
            grad = dot_transposed(mine, weights[:, :columns])
            grads[part][...] = grad.astype(grads[part].dtype)
            gain_sum = jnp.sum(grad * normed_in[part][...].astype(f32), axis=0, keepdims=True)
            attn_gain_grad[...] = attn_gain_grad[...] + gain_sum if part else gain_sum


def back_stages(kept):
    kv_heads = kept[2].shape[0] // HD
    if kv_heads % 4:
        return [(0, kv_heads)]
    quarter = kv_heads // 4
    return [(0, quarter), (quarter, 3 * quarter), (3 * quarter, kv_heads)]


def attend_back(fixed, kept, parts, normed, stage, earlier, after):
    count = len(parts)
    first_group, last_group = stage
    kv_heads = kept[2].shape[0] // HD
    part_rows, model = parts[0].shape
    length = count * part_rows
    query_columns = kept[1].shape[0]
    columns = query_columns + 2 * kept[2].shape[0]
    shape = jax.ShapeDtypeStruct
    last = last_group == kv_heads
    normed = normed if last else ()
    share = kv_heads // (last_group - first_group)
    gains = [shape((HD, 1), f32)] * 2
    turned = shape((columns, length), bf16)
    scratch = [
        pltpu.VMEM((length, model), bf16),
        pltpu.VMEM((query_columns, length), bf16),
        pltpu.VMEM((HD, length), f32),
        pltpu.VMEM((HD, length), f32),
    ]
    if last:
        outs = (
            [shape((part_rows, model), kind) for kind in [f32] + [bf16] * (count - 1)]
            + [shape((part_rows, columns), bf16)] * count
            + [shape((1, model), f32)]
            + gains
        )
        scratch = [pltpu.VMEM(turned.shape, bf16)] + scratch + [pltpu.VMEM((length, columns), bf16)]
    else:
        outs = [turned] + gains
    results = pl.pallas_call(
        partial(attend_back_body, count, first_group, last_group, len(after)),
        grid=(1,),
        in_specs=[pl.BlockSpec(memory_space=pltpu.SMEM)]
        + entire([*fixed[1:], *kept, *parts, *earlier, *normed])
        + [anywhere()] * len(after),
        out_specs=entire(outs),
        out_shape=outs,
        scratch_shapes=scratch,
        compiler_params=pltpu.CompilerParams(vmem_limit_bytes=56 * 1024 * 1024),
        cost_estimate=pl.CostEstimate(
            flops=(
                2 * length * model * (query_columns + columns)
                + 20 * length * length * query_columns
            )
            // share,
            bytes_accessed=16 * length * model,
            transcendentals=query_columns // HD * length * length // share,
        ),
        name="attend_back",
    )(*fixed, *kept, *parts, *earlier, *normed, *after)
    if not last:
        return results
    return results[:count], results[count : 2 * count], *results[2 * count :]


def on_device(
    tokens,
    out_cotangent,
    attn_gain,
    query_weight,
    key_weight,
    value_weight,
    query_gain,
    key_gain,
    out_weight,
    ffn_gain,
    gate_weight,
    up_weight,
    down_weight,
):
    shard, query_columns = query_weight.shape
    key_columns = key_weight.shape[1]
    qkv_columns = query_columns + 2 * key_columns
    units = gate_weight.shape[1]
    width = hidden_width(units)
    steps = units // width
    pieces = (query_weight, key_weight, value_weight, out_weight.T)
    firsts = [0, query_columns, query_columns + key_columns, qkv_columns]
    places = [(at, 0, firsts[at], piece.shape[1]) for at, piece in enumerate(pieces)]
    attn_starts, attn_blocks, attn_arrived = gather_ring(pack(pieces, places, ()), {})
    rows_in_all = shard * lax.axis_size("fsdp")
    attn_full = assemble(attn_starts, gather_near(attn_blocks), rows_in_all)
    pieces = (gate_weight, up_weight, down_weight.T)
    places = [
        (at, step * width, (3 * step + at) * width, width)
        for step in range(steps)
        for at in range(3)
    ]
    ffn_shard = pack(pieces, places, ())
    ffn_starts, ffn_pieces, ffn_arrived = gather_ring(ffn_shard, {1: attn_arrived[-1]})

    residual = tokens.astype(f32)
    normed, attn_norm_pull = jax.vjp(rms_norm, residual, attn_gain)
    normed_parts = widen(normed.astype(bf16))
    if len(normed_parts) == 2:
        cotangent_parts = widen(held(out_cotangent, normed_parts[1:]))
    else:
        cotangent_parts = widen(out_cotangent)
    length = len(normed_parts) * normed_parts[0].shape[0]
    cosine, sine = rotary_tables(length)
    place = lax.axis_index("tp").astype(jnp.int32).reshape(1)
    fixed = (place, attn_full, query_gain[:, None], key_gain[:, None], cosine, sine)
    branch, attended, kept = attend(
        *fixed, normed_parts, query_columns, key_columns, ffn_arrived[0]
    )
    branch = [*branch[:-1], held(branch[-1], (*cotangent_parts[1:], *ffn_arrived[1]))]
    middle = residual + narrow(branch)
    normed_ffn, ffn_norm_pull = jax.vjp(rms_norm, middle, ffn_gain)
    ffn_parts = widen(normed_ffn.astype(bf16))
    ffn_pieces = gather_near(ffn_pieces, ffn_parts[1:])
    results = []
    for at in reversed(range(len(ffn_parts))):
        after = [results[-1][1]] if results else []
        results.append(
            feed_forward(
                ffn_parts[at],
                cotangent_parts[at],
                ffn_starts,
                ffn_pieces,
                width,
                bf16 if at else f32,
                after,
            )
        )
    out_parts, grad_parts, pairs, hiddens = (list(item) for item in zip(*results[::-1]))
    ffn_normed_grad = narrow(grad_parts)
    middle_piece, ffn_gain_local = ffn_norm_pull(ffn_normed_grad)
    middle_grad = out_cotangent.astype(f32) + middle_piece
    branch_parts = widen(middle_grad.astype(bf16))

    ffn_blocks = weight_grads(
        ffn_parts,
        cotangent_parts,
        pairs,
        hiddens,
        steps,
        (branch_parts[0],),
        branch_parts[1:],
    )
    ffn_state, sent = ring_open(ffn_blocks)
    ffn_next, attn_next, last = 1, 1, ring_size() // 2
    out_other = [narrow_send(held(out_parts[-1], branch_parts[1:]))] if len(out_parts) == 2 else []
    back = ()
    for stage in back_stages(kept):
        back = attend_back(fixed, kept, branch_parts, normed_parts, stage, back, sent)
        done = back[1] if len(back) == 3 else back[2]
        if ffn_next < last:
            after = (done, *out_other) if ffn_next == 2 else (done,)
            ffn_state, sent = ring_step(ffn_blocks, ffn_next, ffn_state, after)
            ffn_next += 1
    if out_other:
        output = middle + out_parts[0] + out_other[0].astype(f32)
    else:
        output = middle + narrow(out_parts)
    output = output.astype(bf16)
    normed_grad, qkv_grad, attn_gain_local, query_gain_local, key_gain_local = back
    gains = jnp.concatenate(
        [
            attn_gain_local[0] / attn_gain,
            ffn_gain_local,
            query_gain_local[:, 0],
            key_gain_local[:, 0],
        ]
    )
    rounds = sum_rounds()
    while rounds and rounds[0][0] == "tp":
        gains = gains + swap(gains, *rounds.pop(0))
    grad_other = ()
    if len(normed_grad) == 2:
        grad_other = (narrow_send(held(normed_grad[1], (*sent, gains))),)
        normed_grad = normed_grad[0] + grad_other[0].astype(f32)
    else:
        normed_grad = narrow(normed_grad)
    attn_blocks = weight_grads(normed_parts, branch_parts, qkv_grad, attended, 1, sent)
    gains = gains + swap(gains, *rounds.pop(0))
    attn_state, sent = ring_open(attn_blocks, (gains, *ffn_state))
    while ffn_next < last or attn_next < last:
        if ffn_next < last:
            ffn_state, sent = ring_step(ffn_blocks, ffn_next, ffn_state)
            ffn_next += 1
        if attn_next < last:
            if rounds:
                gains = gains + swap(held(gains, sent), *rounds.pop(0))
            after = (*sent, gains) if attn_next < 2 else (*sent, gains, *grad_other)
            attn_state, sent = ring_step(attn_blocks, attn_next, attn_state, after)
            attn_next += 1
    for axis_name, bit in rounds:
        gains = gains + swap(gains, axis_name, bit)
    ffn_places = [
        (step * 3 * width + number * width, width, number, step * width)
        for step in range(steps)
        for number in range(3)
    ]
    gate_grad, up_grad, down_grad = ring_close(ffn_blocks, ffn_state, ffn_places)
    attn_places = [
        (0, query_columns, 0, 0),
        (query_columns, key_columns, 1, 0),
        (query_columns + key_columns, key_columns, 2, 0),
        (qkv_columns, query_columns, 3, 0),
    ]
    query_grad, key_grad, value_grad, out_grad = ring_close(attn_blocks, attn_state, attn_places)
    tokens_piece, _ = attn_norm_pull(normed_grad)
    tokens_grad = middle_grad + tokens_piece
    model = attn_gain.shape[0]
    return (
        output,
        tokens_grad,
        gains[:model],
        query_grad,
        key_grad,
        value_grad,
        gains[2 * model : 2 * model + HD],
        gains[2 * model + HD :],
        out_grad.T,
        gains[model : 2 * model],
        gate_grad,
        up_grad,
        down_grad.T,
    )


def solution(mesh):
    placed = (
        P(("fsdp", "tp"), None),
        P(("fsdp", "tp"), None),
        P(),
        P("fsdp", "tp"),
        P("fsdp", "tp"),
        P("fsdp", "tp"),
        P(),
        P(),
        P("tp", "fsdp"),
        P(),
        P("fsdp", "tp"),
        P("fsdp", "tp"),
        P("tp", "fsdp"),
    )
    return jax.shard_map(
        on_device,
        mesh=mesh,
        in_specs=placed,
        out_specs=(
            P(("fsdp", "tp"), None),
            P(("fsdp", "tp"), None),
            P(),
            P("fsdp", "tp"),
            P("fsdp", "tp"),
            P("fsdp", "tp"),
            P(),
            P(),
            P("tp", "fsdp"),
            P(),
            P("fsdp", "tp"),
            P("fsdp", "tp"),
            P("tp", "fsdp"),
        ),
        check_vma=False,
    )
```

```python
from functools import partial

import jax
import jax.numpy as jnp
from jax import lax
from jax.experimental import pallas as pl
from jax.experimental.pallas import tpu as pltpu
from jax.sharding import PartitionSpec as P

HD = 64

eps = 1e-05
theta_base = 1000000.0
f32 = jnp.float32
bf16 = jnp.bfloat16


def rms_norm(values, gain):
    return values * lax.rsqrt(jnp.mean(values * values, axis=-1, keepdims=True) + eps) * gain


def rotary_tables(length):
    half_size = HD // 2
    frequency = theta_base ** (-jnp.arange(half_size, dtype=f32) * 2.0 / HD)
    angles = frequency[:, None] * jnp.arange(length, dtype=f32)[None, :]
    return (jnp.cos(angles), jnp.sin(angles))


def dot(former, latter):
    return jnp.dot(former, latter, preferred_element_type=f32)


def dot_transposed(former, latter):
    return lax.dot_general(former, latter, (((1,), (1,)), ((), ())), preferred_element_type=f32)


def dot_leading(former, latter):
    return lax.dot_general(former, latter, (((0,), (0,)), ((), ())), preferred_element_type=f32)


def swap(values, axis_name, bit=1):
    count = lax.axis_size(axis_name)
    return lax.ppermute(values, axis_name, [(i, i ^ bit) for i in range(count)])


def anywhere():
    return pl.BlockSpec(memory_space=pl.ANY)


def entire(arrays):
    return [pl.BlockSpec(array.shape, lambda i, rank=array.ndim: (0,) * rank) for array in arrays]


def held_all(arrays, after):
    count = len(arrays)
    return pl.pallas_call(
        lambda *refs: None,
        in_specs=[anywhere()] * (count + len(after)),
        out_specs=[anywhere()] * count,
        out_shape=[jax.ShapeDtypeStruct(array.shape, array.dtype) for array in arrays],
        input_output_aliases={at: at for at in range(count)},
        name="held",
    )(*arrays, *after)


def held(values, after):
    return held_all([values], after)[0]


def widen(rows):
    if lax.axis_size("tp") == 2:
        return (rows, swap(rows, "tp"))
    return (lax.all_gather(rows, "tp", axis=0, tiled=True),)


def narrow_send(part):
    return swap(part.astype(bf16), "tp")


def narrow(parts):
    if len(parts) == 2:
        return parts[0].astype(f32) + narrow_send(parts[1]).astype(f32)
    return lax.psum_scatter(
        parts[0].astype(bf16), "tp", scatter_dimension=0, tiled=True
    ).astype(f32)


def ring_size():
    return lax.axis_size("fsdp") // 2


def chip_at(place):
    chips = ring_size()
    if isinstance(place, int):
        return 2 * place if place < chips // 2 else 2 * (chips - 1 - place) + 1
    return jnp.where(place < chips // 2, 2 * place, 2 * (chips - 1 - place) + 1)


def own_place():
    chip = lax.axis_index("fsdp") // 2
    return jnp.where(chip % 2 == 0, chip // 2, ring_size() - 1 - chip // 2)


def pass_on(values, direction):
    chips = ring_size()
    pairs = [
        (2 * chip_at(place) + core, 2 * chip_at((place + direction) % chips) + core)
        for place in range(chips)
        for core in range(2)
    ]
    return lax.ppermute(values, "fsdp", pairs)


def shard_table(ahead):
    core = lax.axis_index("fsdp") % 2
    chips = chip_at((own_place() + jnp.array(ahead, jnp.int32)) % ring_size())
    return jnp.concatenate([2 * chips + core, 2 * chips + 1 - core]).astype(jnp.int32)


def gather_ring(shard, ready):
    rows = shard.shape[0]
    half = rows // 2
    chips = ring_size()
    blocks, ahead, offset, arrived = [], [0], [0], []
    sent = [shard]
    for step in range(1, chips // 2 + 1):
        if step in ready:
            sent = held_all(sent, ready[step])
        blocks += sent
        down, up = sent[0], sent[-1]
        if step == chips // 2:
            down, up = down[:half], up[half:]
        sent = [pass_on(down, 1), pass_on(up, -1)]
        arrived.append(sent)
        ahead += [chips - step, step]
        offset += [0, half if step == chips // 2 else 0]
    blocks += sent
    starts = shard_table(ahead) * rows + jnp.array(offset * 2, jnp.int32)
    return starts, blocks, arrived


def gather_near(blocks, ready=()):
    ends = held_all(blocks[-2:], ready) if ready else blocks[-2:]
    blocks = [*blocks[:-2], *ends]
    return blocks + [swap(block, "fsdp") for block in blocks]


def place_rows(whole, starts, blocks):
    for at, block in enumerate(blocks):
        whole[pl.ds(pl.multiple_of(starts[at], 16), block.shape[0]), :] = block[...]


def assemble_body(starts, *refs):
    place_rows(refs[-1], starts, refs[:-1])


def assemble(starts, blocks, rows):
    out = jax.ShapeDtypeStruct((rows, blocks[0].shape[1]), bf16)
    return pl.pallas_call(
        assemble_body,
        grid=(1,),
        in_specs=[pl.BlockSpec(memory_space=pltpu.SMEM)] + entire(blocks),
        out_specs=entire([out])[0],
        out_shape=out,
        compiler_params=pltpu.CompilerParams(vmem_limit_bytes=48 * 1024 * 1024),
        name="assemble",
    )(starts, *blocks)


def pack_body(places, *refs):
    whole = refs[-1]
    for number, source, start, width in places:
        whole[:, start : start + width] = refs[number][:, source : source + width]


def pack(arrays, places, after):
    columns = max(start + width for _, _, start, width in places)
    out = jax.ShapeDtypeStruct((arrays[0].shape[0], columns), bf16)
    return pl.pallas_call(
        partial(pack_body, places),
        grid=(1,),
        in_specs=entire(arrays) + [anywhere()] * len(after),
        out_specs=entire([out])[0],
        out_shape=out,
        compiler_params=pltpu.CompilerParams(vmem_limit_bytes=32 * 1024 * 1024),
        name="pack",
    )(*arrays, *after)


def ring_groups():
    chips = ring_size()
    middle = [[chips // 2 - step, chips // 2 + step] for step in range(1, chips // 2)]
    return [[chips // 2]] + middle + [[0]]


def weight_grad_body(parts, groups, rows, tails, extra, *refs):
    table = refs[0]
    first_in = refs[1 : 1 + parts]
    second_in = refs[1 + parts : 1 + 2 * parts]
    first_grads, second_grads = refs[1 + 2 * parts : 3 + 2 * parts]
    tail = refs[3 + 2 * parts : 3 + 2 * parts + tails]
    outs = refs[3 + 2 * parts + tails + extra : -3]
    first_turned, second_turned, straight = refs[-3:]
    part_rows = first_in[0].shape[0]
    first_width = first_grads.shape[1]
    count = sum(len(group) for group in groups)

    @pl.when(pl.program_id(0) == 0)
    def _():
        for pieces, turned in ((first_in, first_turned), (second_in, second_turned)):
            for part in range(parts):
                span = pl.ds(part * part_rows, part_rows)
                straight[:, span] = pieces[part][...].T
            for at in range(2 * count):
                start = pl.multiple_of(table[at] * rows, rows)
                turned[at * rows : (at + 1) * rows, :] = straight[pl.ds(start, rows), :]

    for turned, grads, start in (
        (first_turned, first_grads, 0),
        (second_turned, second_grads, first_width),
    ):
        here = slice(start, start + grads.shape[1])
        for core in range(2):
            part = dot(turned[core * count * rows : (core + 1) * count * rows, :], grads[...])
            at = 0
            for number, group in enumerate(groups):
                for member in range(len(group)):
                    values = part[at * rows : (at + 1) * rows]
                    outs[core * len(groups) + number][member, :, here] = values.astype(bf16)
                    at += 1
    for piece in tail:
        for out in outs:
            for member in range(out.shape[0]):
                out[member, :, out.shape[2] - piece.shape[1] :] = piece[...]


def weight_grads(first, second, first_grads, second_grads, steps, after, before=(), tail=()):
    parts = len(first)
    part_rows, model = first[0].shape
    length = parts * part_rows
    first_width = first_grads.shape[1] // steps
    second_width = second_grads.shape[1] // steps
    width = first_width + second_width + sum(piece.shape[1] for piece in tail)
    groups = ring_groups()
    count = 2 * ring_size()
    rows = model // count
    table = shard_table([place for group in groups for place in group])
    whole = pl.BlockSpec((part_rows, model), lambda i: (0, 0))
    outs = [jax.ShapeDtypeStruct((len(group), rows, steps * width), bf16) for group in groups] * 2
    out_specs = [
        pl.BlockSpec((len(group), rows, width), lambda i: (0, 0, i)) for group in groups
    ] * 2
    results = pl.pallas_call(
        partial(weight_grad_body, parts, groups, rows, len(tail), len(after)),
        grid=(steps,),
        in_specs=[pl.BlockSpec(memory_space=pltpu.SMEM)]
        + [whole] * (2 * parts)
        + [pl.BlockSpec((length, first_width), lambda i: (0, i))]
        + [pl.BlockSpec((length, second_width), lambda i: (0, i))]
        + entire(tail)
        + [anywhere()] * len(after),
        out_specs=out_specs,
        out_shape=outs,
        scratch_shapes=[
            pltpu.VMEM((model, length), bf16),
            pltpu.VMEM((model, length), bf16),
            pltpu.VMEM((model, length), bf16),
        ],
        compiler_params=pltpu.CompilerParams(vmem_limit_bytes=56 * 1024 * 1024),
        cost_estimate=pl.CostEstimate(
            flops=2 * length * model * steps * width,
            bytes_accessed=4 * model * steps * width,
            transcendentals=0,
        ),
        name="weight_grads",
    )(table, *first, *second, first_grads, second_grads, *tail, *after)
    mine = results[: len(groups)]
    near = list(results[len(groups) :])
    if before:
        near[0] = held(near[0], before)
    near = [swap(block, "fsdp") for block in near]
    return mine, near


def ring_call(body, operands, outs, after, name):
    return pl.pallas_call(
        body,
        grid=(1,),
        in_specs=entire(operands) + [anywhere()] * len(after),
        out_specs=entire(outs),
        out_shape=outs,
        compiler_params=pltpu.CompilerParams(vmem_limit_bytes=48 * 1024 * 1024),
        name=name,
    )(*operands, *after)


def both_cores(mine, near, member):
    return mine[member].astype(f32) + near[member].astype(f32)


def open_body(cut, mine, near, *refs):
    low, high = refs[-2:]
    total = both_cores(mine, near, 0).astype(bf16)
    low[...] = total[:, :cut]
    high[...] = total[:, cut:]


def step_body(cut, mine, near, down, up, *refs):
    ahead, behind = refs[-2:]
    columns = ahead.shape[1]
    ahead_sum = both_cores(mine, near, 0)
    behind_sum = both_cores(mine, near, 1)
    if down.shape[1] == columns:
        ahead[...] = (ahead_sum + down[...].astype(f32)).astype(bf16)
        behind[...] = (behind_sum + up[...].astype(f32)).astype(bf16)
    else:
        ahead[:, :cut] = (ahead_sum[:, :cut] + down[...].astype(f32)).astype(bf16)
        ahead[:, cut:] = ahead_sum[:, cut:].astype(bf16)
        behind[:, :cut] = behind_sum[:, :cut].astype(bf16)
        behind[:, cut:] = (behind_sum[:, cut:] + up[...].astype(f32)).astype(bf16)


def close_body(pieces, mine, near, down, up, *outs):
    total = both_cores(mine, near, 0) + down[...].astype(f32) + up[...].astype(f32)
    for start, width, number, place in pieces:
        outs[number][:, place : place + width] = total[:, start : start + width]


def ring_cut(columns):
    return columns // 2 // 128 * 128


def ring_pass(sums):
    return pass_on(sums[0], 1), pass_on(sums[1], -1)


def ring_open(blocks, after=()):
    mine, near = blocks
    rows, columns = mine[0].shape[1:]
    cut = ring_cut(columns)
    outs = [jax.ShapeDtypeStruct((rows, width), bf16) for width in (cut, columns - cut)]
    sums = ring_call(partial(open_body, cut), (mine[0], near[0]), outs, after, "ring_open")
    return ring_pass(sums), tuple(sums)


def ring_step(blocks, number, state, after=()):
    mine, near = blocks[0][number], blocks[1][number]
    rows, columns = mine.shape[1:]
    outs = [jax.ShapeDtypeStruct((rows, columns), bf16)] * 2
    body = partial(step_body, ring_cut(columns))
    sums = ring_call(body, (mine, near, *state), outs, after, "ring_step")
    return ring_pass(sums), tuple(sums)


def ring_close(blocks, state, pieces):
    mine, near = blocks[0][-1], blocks[1][-1]
    rows = mine.shape[1]
    sizes = {}
    for _, width, number, place in pieces:
        sizes[number] = max(sizes.get(number, 0), place + width)
    outs = [jax.ShapeDtypeStruct((rows, sizes[number]), f32) for number in range(len(sizes))]
    return ring_call(partial(close_body, pieces), (mine, near, *state), outs, (), "ring_close")


def ffn_body(width, count, extra, *refs):
    starts, rows_in, cotangent_in = refs[:3]
    blocks = refs[3 : 3 + count]
    out, grad, pairs, hiddens, out_sum, grad_sum, weights = refs[3 + count + extra :]
    step = pl.program_id(0)
    length = rows_in.shape[0]

    @pl.when(step == 0)
    def _():
        out_sum[...] = jnp.zeros_like(out_sum)
        grad_sum[...] = jnp.zeros_like(grad_sum)

    place_rows(weights, starts, blocks)
    pair_weights = weights[:, : 2 * width]
    down = weights[:, 2 * width :]
    chunk = min(256, length)
    for start in range(0, length, chunk):
        span = pl.ds(start, chunk)
        both = dot(rows_in[span, :], pair_weights)
        gate = both[:, :width]
        up = both[:, width:]
        hidden_grad = dot(cotangent_in[span, :], down)
        sigmoid = 0.5 + 0.5 * jnp.tanh(0.5 * gate)
        silu = gate * sigmoid
        hidden = (silu * up).astype(bf16)
        gate_grad = hidden_grad * up * (sigmoid + silu * (1.0 - sigmoid))
        up_grad = hidden_grad * silu
        pair = jnp.concatenate([gate_grad.astype(bf16), up_grad.astype(bf16)], axis=1)
        hiddens[span, :] = hidden
        pairs[span, :] = pair
        out_sum[span, :] += dot_transposed(hidden, down)
        grad_sum[span, :] += dot_transposed(pair, pair_weights)

    @pl.when(step == pl.num_programs(0) - 1)
    def _():
        out[...] = out_sum[...].astype(out.dtype)
        grad[...] = grad_sum[...].astype(grad.dtype)


def hidden_width(units):
    for width in (768, 256, 384, 128):
        if units % width == 0:
            return width
    return units


def feed_forward(rows, cotangent, starts, blocks, width, kind, part, parts, earlier, after):
    length, model = rows.shape
    steps = blocks[0].shape[1] // (3 * width)
    whole = pl.BlockSpec((length, model), lambda i: (0, 0))
    sums = jax.ShapeDtypeStruct((length, model), kind)
    return pl.pallas_call(
        partial(ffn_body, width, len(blocks), len(earlier) + len(after)),
        grid=(steps,),
        in_specs=[pl.BlockSpec(memory_space=pltpu.SMEM), whole, whole]
        + [pl.BlockSpec((block.shape[0], 3 * width), lambda i: (0, i)) for block in blocks]
        + [anywhere()] * (len(earlier) + len(after)),
        input_output_aliases={3 + len(blocks) + at: 2 + at for at in range(len(earlier))},
        out_specs=[
            whole,
            whole,
            pl.BlockSpec((length, 2 * width), lambda i: (part, i)),
            pl.BlockSpec((length, width), lambda i: (part, i)),
        ],
        out_shape=[
            sums,
            sums,
            jax.ShapeDtypeStruct((parts * length, steps * 2 * width), bf16),
            jax.ShapeDtypeStruct((parts * length, steps * width), bf16),
        ],
        scratch_shapes=[
            pltpu.VMEM((length, model), f32),
            pltpu.VMEM((length, model), f32),
            pltpu.VMEM((model, 3 * width), bf16),
        ],
        compiler_params=pltpu.CompilerParams(vmem_limit_bytes=56 * 1024 * 1024),
        cost_estimate=pl.CostEstimate(
            flops=12 * length * model * steps * width,
            bytes_accessed=8 * model * steps * width,
            transcendentals=length * steps * width,
        ),
        name="feed_forward",
    )(starts, rows, cotangent, *blocks, *earlier, *after)


def lines(start, size):
    if isinstance(start, int):
        return pl.ds(start, size)
    return pl.ds(pl.multiple_of(start, size), size)


def part_starts(place, count, part_rows):
    if count == 1:
        return [0]
    return [place[0] * part_rows, (1 - place[0]) * part_rows]


def causal_block(size):
    keys = lax.broadcasted_iota(jnp.int32, (size, size), 0)
    queries = lax.broadcasted_iota(jnp.int32, (size, size), 1)
    return keys <= queries


def attend_body(count, extra, *refs):
    place, weights, query_gain, key_gain, cosine, sine = refs[:6]
    rows_in = refs[6 : 6 + count]
    refs = refs[:6] + refs[6 + extra :]
    branches = refs[6 + count : 6 + 2 * count]
    attended_out = refs[6 + 2 * count]
    raw, query_rows, key_rows, value_rows, attended, log_totals = refs[7 + 2 * count : 13 + 2 * count]
    rows, turned = refs[13 + 2 * count :]
    part_rows = rows_in[0].shape[0]
    length = rows.shape[0]
    heads = query_rows.shape[0] // HD
    kv_heads = key_rows.shape[0] // HD
    group_size = heads // kv_heads
    columns = (heads + 2 * kv_heads) * HD
    half = HD // 2
    starts = part_starts(place, count, part_rows)
    for part in range(count):
        rows[lines(starts[part], part_rows), :] = rows_in[part][...]

    chunk = min(256, columns)
    for first in range(0, columns, chunk):
        product = dot_transposed(weights[:, first : first + chunk].T, rows[...])
        for at in range(0, chunk, HD):
            head = (first + at) // HD
            values = product[at : at + HD]
            if head >= heads + kv_heads:
                start = (head - heads - kv_heads) * HD
                value_rows[start : start + HD, :] = values.astype(bf16)
                continue
            raw[first + at : first + at + HD, :] = values
            gain = query_gain if head < heads else key_gain
            scale = lax.rsqrt(jnp.mean(values * values, axis=0, keepdims=True) + eps)
            normed = values * scale * gain[...]
            top, bottom = normed[:half], normed[half:]
            top, bottom = (
                top * cosine[...] - bottom * sine[...],
                bottom * cosine[...] + top * sine[...],
            )
            if head < heads:
                target, start = query_rows, head * HD
                top = top.astype(bf16).astype(f32) * HD**-0.5
                bottom = bottom.astype(bf16).astype(f32) * HD**-0.5
            else:
                target, start = key_rows, (head - heads) * HD
            target[start : start + half, :] = top.astype(bf16)
            target[start + half : start + HD, :] = bottom.astype(bf16)

    block = min(256, length)
    causal = causal_block(block)

    def one_group(kv_head, carry):
        span = lines(kv_head * HD, HD)
        keys = key_rows[span, :].T
        values = value_rows[span, :]
        for member in range(group_size):
            head = kv_head * group_size + member
            for start in range(0, length, block):
                here = slice(start, start + block)
                query = query_rows[lines(head * HD, HD), here]
                weight = jnp.where(causal, jnp.exp(dot(keys[here], query)), 0.0)
                total = jnp.sum(weight, axis=0, keepdims=True)
                result = dot(values[:, here], weight.astype(bf16))
                if start:
                    weight = jnp.exp(dot(keys[:start], query))
                    total = total + jnp.sum(weight, axis=0, keepdims=True)
                    result = result + dot(values[:, :start], weight.astype(bf16))
                attended[lines(head * HD, HD), here] = (result * (1.0 / total)).astype(bf16)
                log_totals[head, :, here] = jnp.log(total)
        return carry

    lax.fori_loop(0, kv_heads, one_group, 0)
    turned[...] = attended[...].T
    for part in range(count):
        mine = turned[lines(starts[part], part_rows), :]
        attended_out[part * part_rows : (part + 1) * part_rows, :] = mine
        branches[part][...] = dot_transposed(mine, weights[:, columns:]).astype(branches[part].dtype)


def attend(
    place, weights, query_gain, key_gain, cosine, sine, parts, query_columns, key_columns, after
):
    count = len(parts)
    part_rows, model = parts[0].shape
    length = count * part_rows
    heads = query_columns // HD
    shape = jax.ShapeDtypeStruct
    kinds = [f32] + [bf16] * (count - 1)
    outs = (
        [shape((part_rows, model), kind) for kind in kinds]
        + [shape((length, query_columns), bf16)]
        + [
            shape((query_columns + key_columns, length), f32),
            shape((query_columns, length), bf16),
            shape((key_columns, length), bf16),
            shape((key_columns, length), bf16),
            shape((query_columns, length), bf16),
            shape((heads, 1, length), f32),
        ]
    )
    results = pl.pallas_call(
        partial(attend_body, count, len(after)),
        grid=(1,),
        in_specs=[pl.BlockSpec(memory_space=pltpu.SMEM)]
        + entire([weights, query_gain, key_gain, cosine, sine, *parts])
        + [anywhere()] * len(after),
        out_specs=entire(outs),
        out_shape=outs,
        scratch_shapes=[
            pltpu.VMEM((length, model), bf16),
            pltpu.VMEM((length, query_columns), bf16),
        ],
        compiler_params=pltpu.CompilerParams(vmem_limit_bytes=56 * 1024 * 1024),
        cost_estimate=pl.CostEstimate(
            flops=2 * length * model * (2 * query_columns + 2 * key_columns)
            + 8 * length * length * query_columns,
            bytes_accessed=16 * length * model,
            transcendentals=heads * length * length,
        ),
        name="attend",
    )(place, weights, query_gain, key_gain, cosine, sine, *parts, *after)
    return results[:count], results[count], results[count + 1 :]


def attend_back_body(count, first_group, last_group, extra, *refs):
    place, weights, query_gain, key_gain, cosine, sine = refs[:6]
    raw, query_rows, key_rows, value_rows, attended, log_totals = refs[6:12]
    branch_in = refs[12 : 12 + count]
    refs = refs[12 + count :]
    if first_group:
        earlier = refs[:3]
        refs = refs[3:]
    if last_group * HD == key_rows.shape[0]:
        normed_in = refs[:count]
        refs = refs[count:]
    refs = refs[extra:]
    last = last_group * HD == key_rows.shape[0]
    if last:
        grads, raw_grads, refs = refs[:count], refs[count], refs[count + 1 :]
        attn_gain_grad, refs = refs[0], refs[1:]
        query_gain_grad, key_gain_grad, turned_grads = refs[:3]
        rows, attended_grad, key_sum, value_sum, straight = refs[3:]
    else:
        turned_grads, query_gain_grad, key_gain_grad = refs[:3]
        rows, attended_grad, key_sum, value_sum = refs[3:]
    part_rows = branch_in[0].shape[0]
    length = rows.shape[0]
    heads = query_rows.shape[0] // HD
    kv_heads = key_rows.shape[0] // HD
    group_size = heads // kv_heads
    columns = (heads + 2 * kv_heads) * HD
    half = HD // 2
    starts = part_starts(place, count, part_rows)
    for part in range(count):
        rows[lines(starts[part], part_rows), :] = branch_in[part][...]
    stage_rows = (last_group - first_group) * group_size * HD
    chunk = min(256, stage_rows)
    begin = first_group * group_size * HD
    for first in range(begin, begin + stage_rows, chunk):
        piece = weights[:, columns + first : columns + first + chunk].T
        attended_grad[first : first + chunk, :] = dot_transposed(piece, rows[...]).astype(bf16)
    if first_group:
        turned_grads[...] = earlier[0][...]
        query_gain_grad[...] = earlier[1][...]
        key_gain_grad[...] = earlier[2][...]
    else:
        turned_grads[...] = jnp.zeros_like(turned_grads)
        query_gain_grad[...] = jnp.zeros_like(query_gain_grad)
        key_gain_grad[...] = jnp.zeros_like(key_gain_grad)
    block = min(256, length)
    causal = causal_block(block)

    def unprepare(grad, values, gain, gain_grad):
        top, bottom = grad[:half], grad[half:]
        grad = jnp.concatenate(
            [
                top * cosine[...] + bottom * sine[...],
                bottom * cosine[...] - top * sine[...],
            ],
            axis=0,
        )
        scale = lax.rsqrt(jnp.mean(values * values, axis=0, keepdims=True) + eps)
        normed = values * scale
        gain_grad[...] += jnp.sum(grad * normed, axis=1, keepdims=True)
        grad = grad * gain[...]
        inner = jnp.mean(grad * normed, axis=0, keepdims=True)
        return (scale * (grad - normed * inner)).astype(bf16)

    def one_group(kv_head, carry):
        span = lines(kv_head * HD, HD)
        keys_turned = key_rows[span, :]
        keys = keys_turned.T
        values = value_rows[span, :].T
        key_sum[...] = jnp.zeros_like(key_sum)
        value_sum[...] = jnp.zeros_like(value_sum)
        for member in range(group_size):
            head = kv_head * group_size + member
            head_span = lines(head * HD, HD)
            query_parts = []
            for start in range(0, length, block):
                here = slice(start, start + block)
                query = query_rows[head_span, here]
                grad = attended_grad[head_span, here]
                inner = jnp.sum(
                    grad.astype(f32) * attended[head_span, here].astype(f32), axis=0, keepdims=True
                )
                log_total = log_totals[head, :, here]
                query_grad = None
                for low, high in [(start, start + block)] + ([(0, start)] if start else []):
                    prob = jnp.exp(dot(keys[low:high], query) - log_total)
                    if low == start:
                        prob = jnp.where(causal, prob, 0.0)
                    prob_grad = dot(values[low:high], grad)
                    score_grad = (prob * (prob_grad - inner)).astype(bf16)
                    piece = dot(keys_turned[:, low:high], score_grad)
                    query_grad = piece if query_grad is None else query_grad + piece
                    key_sum[:, low:high] += dot_transposed(query, score_grad)
                    value_sum[:, low:high] += dot_transposed(grad, prob.astype(bf16))
                query_parts.append(query_grad * HD**-0.5)
            turned_grads[head_span, :] = unprepare(
                jnp.concatenate(query_parts, axis=1), raw[head_span, :], query_gain, query_gain_grad
            )
        key_span = lines((heads + kv_head) * HD, HD)
        turned_grads[key_span, :] = unprepare(
            key_sum[...], raw[key_span, :], key_gain, key_gain_grad
        )
        turned_grads[lines((heads + kv_heads + kv_head) * HD, HD), :] = value_sum[...].astype(bf16)
        return carry

    lax.fori_loop(first_group, last_group, one_group, 0)
    if last:
        straight[...] = turned_grads[...].T
        for part in range(count):
            mine = straight[lines(starts[part], part_rows), :]
            raw_grads[part * part_rows : (part + 1) * part_rows, :] = mine
            grad = dot_transposed(mine, weights[:, :columns])
            grads[part][...] = grad.astype(grads[part].dtype)
            gain_sum = jnp.sum(grad * normed_in[part][...].astype(f32), axis=0, keepdims=True)
            attn_gain_grad[...] = attn_gain_grad[...] + gain_sum if part else gain_sum


def back_stages(kept):
    kv_heads = kept[2].shape[0] // HD
    if kv_heads % 4:
        return [(0, kv_heads)]
    quarter = kv_heads // 4
    return [(0, quarter), (quarter, 3 * quarter), (3 * quarter, kv_heads)]


def attend_back(fixed, kept, parts, normed, stage, earlier, after):
    count = len(parts)
    first_group, last_group = stage
    kv_heads = kept[2].shape[0] // HD
    part_rows, model = parts[0].shape
    length = count * part_rows
    query_columns = kept[1].shape[0]
    columns = query_columns + 2 * kept[2].shape[0]
    shape = jax.ShapeDtypeStruct
    last = last_group == kv_heads
    normed = normed if last else ()
    share = kv_heads // (last_group - first_group)
    gains = [shape((HD, 1), f32)] * 2
    turned = shape((columns, length), bf16)
    scratch = [
        pltpu.VMEM((length, model), bf16),
        pltpu.VMEM((query_columns, length), bf16),
        pltpu.VMEM((HD, length), f32),
        pltpu.VMEM((HD, length), f32),
    ]
    if last:
        outs = (
            [shape((part_rows, model), kind) for kind in [f32] + [bf16] * (count - 1)]
            + [shape((length, columns), bf16)]
            + [shape((1, model), f32)]
            + gains
        )
        scratch = [pltpu.VMEM(turned.shape, bf16)] + scratch + [pltpu.VMEM((length, columns), bf16)]
    else:
        outs = [turned] + gains
    results = pl.pallas_call(
        partial(attend_back_body, count, first_group, last_group, len(after)),
        grid=(1,),
        in_specs=[pl.BlockSpec(memory_space=pltpu.SMEM)]
        + entire([*fixed[1:], *kept, *parts, *earlier, *normed])
        + [anywhere()] * len(after),
        out_specs=entire(outs),
        out_shape=outs,
        scratch_shapes=scratch,
        compiler_params=pltpu.CompilerParams(vmem_limit_bytes=56 * 1024 * 1024),
        cost_estimate=pl.CostEstimate(
            flops=(
                2 * length * model * (query_columns + columns)
                + 20 * length * length * query_columns
            )
            // share,
            bytes_accessed=16 * length * model,
            transcendentals=query_columns // HD * length * length // share,
        ),
        name="attend_back",
    )(*fixed, *kept, *parts, *earlier, *normed, *after)
    if not last:
        return results
    return results[:count], *results[count:]


def on_device(
    tokens,
    out_cotangent,
    attn_gain,
    query_weight,
    key_weight,
    value_weight,
    query_gain,
    key_gain,
    out_weight,
    ffn_gain,
    gate_weight,
    up_weight,
    down_weight,
):
    shard, query_columns = query_weight.shape
    key_columns = key_weight.shape[1]
    qkv_columns = query_columns + 2 * key_columns
    units = gate_weight.shape[1]
    width = hidden_width(units)
    steps = units // width
    pieces = (query_weight, key_weight, value_weight, out_weight.T)
    firsts = [0, query_columns, query_columns + key_columns, qkv_columns]
    places = [(at, 0, firsts[at], piece.shape[1]) for at, piece in enumerate(pieces)]
    attn_starts, attn_blocks, attn_arrived = gather_ring(pack(pieces, places, ()), {})
    rows_in_all = shard * lax.axis_size("fsdp")
    attn_full = assemble(attn_starts, gather_near(attn_blocks), rows_in_all)
    pieces = (gate_weight, up_weight, down_weight.T)
    places = [
        (at, step * width, (3 * step + at) * width, width)
        for step in range(steps)
        for at in range(3)
    ]
    ffn_shard = pack(pieces, places, ())
    ffn_starts, ffn_pieces, ffn_arrived = gather_ring(ffn_shard, {1: attn_arrived[-1]})

    residual = tokens.astype(f32)
    normed, attn_norm_pull = jax.vjp(rms_norm, residual, attn_gain)
    normed_parts = widen(normed.astype(bf16))
    if len(normed_parts) == 2:
        cotangent_parts = widen(held(out_cotangent, normed_parts[1:]))
    else:
        cotangent_parts = widen(out_cotangent)
    length = len(normed_parts) * normed_parts[0].shape[0]
    cosine, sine = rotary_tables(length)
    place = lax.axis_index("tp").astype(jnp.int32).reshape(1)
    fixed = (place, attn_full, query_gain[:, None], key_gain[:, None], cosine, sine)
    branch, attended, kept = attend(
        *fixed, normed_parts, query_columns, key_columns, ffn_arrived[0]
    )
    branch = [*branch[:-1], held(branch[-1], (*cotangent_parts[1:], *ffn_arrived[1]))]
    middle = residual + narrow(branch)
    normed_ffn, ffn_norm_pull = jax.vjp(rms_norm, middle, ffn_gain)
    ffn_parts = widen(normed_ffn.astype(bf16))
    ffn_pieces = gather_near(ffn_pieces, ffn_parts[1:])
    parts = len(ffn_parts)
    out_parts, grad_parts, kept_ffn = [None] * parts, [None] * parts, ()
    for at in reversed(range(parts)):
        out_parts[at], grad_parts[at], *kept_ffn = feed_forward(
            ffn_parts[at],
            cotangent_parts[at],
            ffn_starts,
            ffn_pieces,
            width,
            bf16 if at else f32,
            at,
            parts,
            kept_ffn,
            grad_parts[at + 1 :],
        )
    pairs, hiddens = kept_ffn
    ffn_normed_grad = narrow(grad_parts)
    middle_piece, ffn_gain_local = ffn_norm_pull(ffn_normed_grad)
    middle_grad = out_cotangent.astype(f32) + middle_piece
    branch_parts = widen(middle_grad.astype(bf16))

    ffn_blocks = weight_grads(
        ffn_parts,
        cotangent_parts,
        pairs,
        hiddens,
        steps,
        (branch_parts[0],),
        branch_parts[1:],
    )
    ffn_state, sent = ring_open(ffn_blocks)
    ffn_next, attn_next, last = 1, 1, ring_size() // 2
    out_other = [narrow_send(held(out_parts[-1], branch_parts[1:]))] if len(out_parts) == 2 else []
    back = ()
    for stage in back_stages(kept):
        back = attend_back(fixed, kept, branch_parts, normed_parts, stage, back, sent)
        done = back[1] if len(back) == 3 else back[2]
        if ffn_next < last:
            after = (done, *out_other) if ffn_next == 2 else (done,)
            ffn_state, sent = ring_step(ffn_blocks, ffn_next, ffn_state, after)
            ffn_next += 1
    if out_other:
        output = middle + out_parts[0] + out_other[0].astype(f32)
    else:
        output = middle + narrow(out_parts)
    output = output.astype(bf16)
    normed_grad, qkv_grad, attn_gain_local, query_gain_local, key_gain_local = back
    gains = jnp.concatenate(
        [
            attn_gain_local[0] / attn_gain,
            ffn_gain_local,
            query_gain_local[:, 0],
            key_gain_local[:, 0],
        ]
    )
    bit = 1
    while bit < lax.axis_size("tp"):
        gains = gains + swap(gains, "tp", bit)
        bit *= 2
    gain_count = gains.shape[0]
    gains = jnp.pad(gains.astype(bf16), (0, shard * 128 - gain_count)).reshape(shard, 128)
    grad_other = ()
    if len(normed_grad) == 2:
        grad_other = (narrow_send(held(normed_grad[1], (*sent, gains))),)
        normed_grad = normed_grad[0] + grad_other[0].astype(f32)
    else:
        normed_grad = narrow(normed_grad)
    attn_blocks = weight_grads(
        normed_parts, branch_parts, qkv_grad, attended, 1, sent, tail=(gains,)
    )
    attn_state, sent = ring_open(attn_blocks, (output, *ffn_state))
    while ffn_next < last or attn_next < last:
        if ffn_next < last:
            ffn_state, sent = ring_step(ffn_blocks, ffn_next, ffn_state)
            ffn_next += 1
        if attn_next < last:
            after = sent if attn_next < 2 else (*sent, *grad_other)
            attn_state, sent = ring_step(attn_blocks, attn_next, attn_state, after)
            attn_next += 1
    ffn_places = [
        (step * 3 * width + number * width, width, number, step * width)
        for step in range(steps)
        for number in range(3)
    ]
    gate_grad, up_grad, down_grad = ring_close(ffn_blocks, ffn_state, ffn_places)
    attn_places = [
        (0, query_columns, 0, 0),
        (query_columns, key_columns, 1, 0),
        (query_columns + key_columns, key_columns, 2, 0),
        (qkv_columns, query_columns, 3, 0),
        (qkv_columns + query_columns, 128, 4, 0),
    ]
    query_grad, key_grad, value_grad, out_grad, gains = ring_close(attn_blocks, attn_state, attn_places)
    tokens_piece, _ = attn_norm_pull(normed_grad)
    tokens_grad = middle_grad + tokens_piece
    model = attn_gain.shape[0]
    gains = gains.reshape(-1)[:gain_count]
    return (
        output,
        tokens_grad,
        gains[:model],
        query_grad,
        key_grad,
        value_grad,
        gains[2 * model : 2 * model + HD],
        gains[2 * model + HD :],
        out_grad.T,
        gains[model : 2 * model],
        gate_grad,
        up_grad,
        down_grad.T,
    )


def solution(mesh):
    placed = (
        P(("fsdp", "tp"), None),
        P(("fsdp", "tp"), None),
        P(),
        P("fsdp", "tp"),
        P("fsdp", "tp"),
        P("fsdp", "tp"),
        P(),
        P(),
        P("tp", "fsdp"),
        P(),
        P("fsdp", "tp"),
        P("fsdp", "tp"),
        P("tp", "fsdp"),
    )
    return jax.shard_map(
        on_device,
        mesh=mesh,
        in_specs=placed,
        out_specs=(
            P(("fsdp", "tp"), None),
            P(("fsdp", "tp"), None),
            P(),
            P("fsdp", "tp"),
            P("fsdp", "tp"),
            P("fsdp", "tp"),
            P(),
            P(),
            P("tp", "fsdp"),
            P(),
            P("fsdp", "tp"),
            P("fsdp", "tp"),
            P("tp", "fsdp"),
        ),
        check_vma=False,
    )
```

```python
from functools import partial

import jax
import jax.numpy as jnp
from jax import lax
from jax.experimental import pallas as pl
from jax.experimental.pallas import tpu as pltpu
from jax.sharding import PartitionSpec as P

HD = 64

eps = 1e-05
theta_base = 1000000.0
f32 = jnp.float32
bf16 = jnp.bfloat16


def rms_norm(values, gain):
    return values * lax.rsqrt(jnp.mean(values * values, axis=-1, keepdims=True) + eps) * gain


def rotary_tables(length):
    half_size = HD // 2
    frequency = theta_base ** (-jnp.arange(half_size, dtype=f32) * 2.0 / HD)
    angles = frequency[:, None] * jnp.arange(length, dtype=f32)[None, :]
    return (jnp.cos(angles), jnp.sin(angles))


def dot(former, latter):
    return jnp.dot(former, latter, preferred_element_type=f32)


def dot_transposed(former, latter):
    return lax.dot_general(former, latter, (((1,), (1,)), ((), ())), preferred_element_type=f32)


def dot_leading(former, latter):
    return lax.dot_general(former, latter, (((0,), (0,)), ((), ())), preferred_element_type=f32)


def swap(values, axis_name, bit=1):
    count = lax.axis_size(axis_name)
    return lax.ppermute(values, axis_name, [(i, i ^ bit) for i in range(count)])


def anywhere():
    return pl.BlockSpec(memory_space=pl.ANY)


def entire(arrays):
    return [pl.BlockSpec(array.shape, lambda i, rank=array.ndim: (0,) * rank) for array in arrays]


def held_all(arrays, after):
    count = len(arrays)
    return pl.pallas_call(
        lambda *refs: None,
        in_specs=[anywhere()] * (count + len(after)),
        out_specs=[anywhere()] * count,
        out_shape=[jax.ShapeDtypeStruct(array.shape, array.dtype) for array in arrays],
        input_output_aliases={at: at for at in range(count)},
        name="held",
    )(*arrays, *after)


def held(values, after):
    return held_all([values], after)[0]


def widen(rows):
    if lax.axis_size("tp") == 2:
        return (rows, swap(rows, "tp"))
    return (lax.all_gather(rows, "tp", axis=0, tiled=True),)


def narrow_send(part):
    return swap(part.astype(bf16), "tp")


def narrow(parts):
    if len(parts) == 2:
        return parts[0].astype(f32) + narrow_send(parts[1]).astype(f32)
    return lax.psum_scatter(
        parts[0].astype(bf16), "tp", scatter_dimension=0, tiled=True
    ).astype(f32)


def ring_size():
    return lax.axis_size("fsdp") // 2


def chip_at(place):
    chips = ring_size()
    if isinstance(place, int):
        return 2 * place if place < chips // 2 else 2 * (chips - 1 - place) + 1
    return jnp.where(place < chips // 2, 2 * place, 2 * (chips - 1 - place) + 1)


def own_place():
    chip = lax.axis_index("fsdp") // 2
    return jnp.where(chip % 2 == 0, chip // 2, ring_size() - 1 - chip // 2)


def pass_on(values, direction):
    chips = ring_size()
    pairs = [
        (2 * chip_at(place) + core, 2 * chip_at((place + direction) % chips) + core)
        for place in range(chips)
        for core in range(2)
    ]
    return lax.ppermute(values, "fsdp", pairs)


def shard_table(ahead):
    core = lax.axis_index("fsdp") % 2
    chips = chip_at((own_place() + jnp.array(ahead, jnp.int32)) % ring_size())
    return jnp.concatenate([2 * chips + core, 2 * chips + 1 - core]).astype(jnp.int32)


def gather_ring(shard, ready):
    rows = shard.shape[0]
    half = rows // 2
    chips = ring_size()
    blocks, ahead, offset, arrived = [], [0], [0], []
    sent = [shard]
    for step in range(1, chips // 2 + 1):
        if step in ready:
            sent = held_all(sent, ready[step])
        blocks += sent
        down, up = sent[0], sent[-1]
        if step == chips // 2:
            down, up = down[:half], up[half:]
        sent = [pass_on(down, 1), pass_on(up, -1)]
        arrived.append(sent)
        ahead += [chips - step, step]
        offset += [0, half if step == chips // 2 else 0]
    blocks += sent
    starts = shard_table(ahead) * rows + jnp.array(offset * 2, jnp.int32)
    return starts, blocks, arrived


def gather_near(blocks, ready=()):
    ends = held_all(blocks[-2:], ready) if ready else blocks[-2:]
    blocks = [*blocks[:-2], *ends]
    return blocks + [swap(block, "fsdp") for block in blocks]


def place_rows(whole, starts, blocks):
    for at, block in enumerate(blocks):
        whole[pl.ds(pl.multiple_of(starts[at], 16), block.shape[0]), :] = block[...]


def assemble_body(starts, *refs):
    place_rows(refs[-1], starts, refs[:-1])


def assemble(starts, blocks, rows):
    out = jax.ShapeDtypeStruct((rows, blocks[0].shape[1]), bf16)
    return pl.pallas_call(
        assemble_body,
        grid=(1,),
        in_specs=[pl.BlockSpec(memory_space=pltpu.SMEM)] + entire(blocks),
        out_specs=entire([out])[0],
        out_shape=out,
        compiler_params=pltpu.CompilerParams(vmem_limit_bytes=48 * 1024 * 1024),
        name="assemble",
    )(starts, *blocks)


def pack_body(places, *refs):
    whole = refs[-1]
    for number, source, start, width in places:
        whole[:, start : start + width] = refs[number][:, source : source + width]


def pack(arrays, places, after):
    columns = max(start + width for _, _, start, width in places)
    out = jax.ShapeDtypeStruct((arrays[0].shape[0], columns), bf16)
    return pl.pallas_call(
        partial(pack_body, places),
        grid=(1,),
        in_specs=entire(arrays) + [anywhere()] * len(after),
        out_specs=entire([out])[0],
        out_shape=out,
        compiler_params=pltpu.CompilerParams(vmem_limit_bytes=32 * 1024 * 1024),
        name="pack",
    )(*arrays, *after)


def ring_groups():
    chips = ring_size()
    middle = [[chips // 2 - step, chips // 2 + step] for step in range(1, chips // 2)]
    return [[chips // 2]] + middle + [[0]]


def weight_grad_body(parts, groups, rows, tails, extra, *refs):
    table = refs[0]
    first_in = refs[1 : 1 + parts]
    second_in = refs[1 + parts : 1 + 2 * parts]
    first_grads, second_grads = refs[1 + 2 * parts : 3 + 2 * parts]
    tail = refs[3 + 2 * parts : 3 + 2 * parts + tails]
    outs = refs[3 + 2 * parts + tails + extra : -3]
    first_turned, second_turned, straight = refs[-3:]
    part_rows = first_in[0].shape[0]
    first_width = first_grads.shape[1]
    count = sum(len(group) for group in groups)

    @pl.when(pl.program_id(0) == 0)
    def _():
        for pieces, turned in ((first_in, first_turned), (second_in, second_turned)):
            for part in range(parts):
                span = pl.ds(part * part_rows, part_rows)
                straight[:, span] = pieces[part][...].T
            for at in range(2 * count):
                start = pl.multiple_of(table[at] * rows, rows)
                turned[at * rows : (at + 1) * rows, :] = straight[pl.ds(start, rows), :]

    for turned, grads, start in (
        (first_turned, first_grads, 0),
        (second_turned, second_grads, first_width),
    ):
        here = slice(start, start + grads.shape[1])
        for core in range(2):
            part = dot(turned[core * count * rows : (core + 1) * count * rows, :], grads[...])
            at = 0
            for number, group in enumerate(groups):
                for member in range(len(group)):
                    values = part[at * rows : (at + 1) * rows]
                    outs[core * len(groups) + number][member, :, here] = values.astype(bf16)
                    at += 1
    for piece in tail:
        for out in outs:
            for member in range(out.shape[0]):
                out[member, :, out.shape[2] - piece.shape[1] :] = piece[...]


def weight_grads(first, second, first_grads, second_grads, steps, after, before=(), tail=()):
    parts = len(first)
    part_rows, model = first[0].shape
    length = parts * part_rows
    first_width = first_grads.shape[1] // steps
    second_width = second_grads.shape[1] // steps
    width = first_width + second_width + sum(piece.shape[1] for piece in tail)
    groups = ring_groups()
    count = 2 * ring_size()
    rows = model // count
    table = shard_table([place for group in groups for place in group])
    whole = pl.BlockSpec((part_rows, model), lambda i: (0, 0))
    outs = [jax.ShapeDtypeStruct((len(group), rows, steps * width), bf16) for group in groups] * 2
    out_specs = [
        pl.BlockSpec((len(group), rows, width), lambda i: (0, 0, i)) for group in groups
    ] * 2
    results = pl.pallas_call(
        partial(weight_grad_body, parts, groups, rows, len(tail), len(after)),
        grid=(steps,),
        in_specs=[pl.BlockSpec(memory_space=pltpu.SMEM)]
        + [whole] * (2 * parts)
        + [pl.BlockSpec((length, first_width), lambda i: (0, i))]
        + [pl.BlockSpec((length, second_width), lambda i: (0, i))]
        + entire(tail)
        + [anywhere()] * len(after),
        out_specs=out_specs,
        out_shape=outs,
        scratch_shapes=[
            pltpu.VMEM((model, length), bf16),
            pltpu.VMEM((model, length), bf16),
            pltpu.VMEM((model, length), bf16),
        ],
        compiler_params=pltpu.CompilerParams(vmem_limit_bytes=56 * 1024 * 1024),
        cost_estimate=pl.CostEstimate(
            flops=2 * length * model * steps * width,
            bytes_accessed=4 * model * steps * width,
            transcendentals=0,
        ),
        name="weight_grads",
    )(table, *first, *second, first_grads, second_grads, *tail, *after)
    mine = results[: len(groups)]
    near = list(results[len(groups) :])
    if before:
        near[0] = held(near[0], before)
    near = [swap(block, "fsdp") for block in near]
    return mine, near


def ring_call(body, operands, outs, after, name):
    return pl.pallas_call(
        body,
        grid=(1,),
        in_specs=entire(operands) + [anywhere()] * len(after),
        out_specs=entire(outs),
        out_shape=outs,
        compiler_params=pltpu.CompilerParams(vmem_limit_bytes=48 * 1024 * 1024),
        name=name,
    )(*operands, *after)


def both_cores(mine, near, member):
    return mine[member].astype(f32) + near[member].astype(f32)


def open_body(cut, mine, near, *refs):
    low, high = refs[-2:]
    total = both_cores(mine, near, 0).astype(bf16)
    low[...] = total[:, :cut]
    high[...] = total[:, cut:]


def step_body(cut, mine, near, down, up, *refs):
    ahead, behind = refs[-2:]
    columns = ahead.shape[1]
    ahead_sum = both_cores(mine, near, 0)
    behind_sum = both_cores(mine, near, 1)
    if down.shape[1] == columns:
        ahead[...] = (ahead_sum + down[...].astype(f32)).astype(bf16)
        behind[...] = (behind_sum + up[...].astype(f32)).astype(bf16)
    else:
        ahead[:, :cut] = (ahead_sum[:, :cut] + down[...].astype(f32)).astype(bf16)
        ahead[:, cut:] = ahead_sum[:, cut:].astype(bf16)
        behind[:, :cut] = behind_sum[:, :cut].astype(bf16)
        behind[:, cut:] = (behind_sum[:, cut:] + up[...].astype(f32)).astype(bf16)


def close_body(pieces, mine, near, down, up, *outs):
    total = both_cores(mine, near, 0) + down[...].astype(f32) + up[...].astype(f32)
    for start, width, number, place in pieces:
        outs[number][:, place : place + width] = total[:, start : start + width]


def ring_cut(columns):
    return columns // 2 // 128 * 128


def ring_pass(sums):
    return pass_on(sums[0], 1), pass_on(sums[1], -1)


def ring_open(blocks, after=()):
    mine, near = blocks
    rows, columns = mine[0].shape[1:]
    cut = ring_cut(columns)
    outs = [jax.ShapeDtypeStruct((rows, width), bf16) for width in (cut, columns - cut)]
    sums = ring_call(partial(open_body, cut), (mine[0], near[0]), outs, after, "ring_open")
    return ring_pass(sums), tuple(sums)


def ring_step(blocks, number, state, after=()):
    mine, near = blocks[0][number], blocks[1][number]
    rows, columns = mine.shape[1:]
    outs = [jax.ShapeDtypeStruct((rows, columns), bf16)] * 2
    body = partial(step_body, ring_cut(columns))
    sums = ring_call(body, (mine, near, *state), outs, after, "ring_step")
    return ring_pass(sums), tuple(sums)


def ring_close(blocks, state, pieces):
    mine, near = blocks[0][-1], blocks[1][-1]
    rows = mine.shape[1]
    sizes = {}
    for _, width, number, place in pieces:
        sizes[number] = max(sizes.get(number, 0), place + width)
    outs = [jax.ShapeDtypeStruct((rows, sizes[number]), f32) for number in range(len(sizes))]
    return ring_call(partial(close_body, pieces), (mine, near, *state), outs, (), "ring_close")


def ffn_body(width, count, extra, *refs):
    starts, rows_in, cotangent_in = refs[:3]
    blocks = refs[3 : 3 + count]
    out, grad, pairs, hiddens, out_sum, grad_sum, weights = refs[3 + count + extra :]
    step = pl.program_id(0)
    length = rows_in.shape[0]

    @pl.when(step == 0)
    def _():
        out_sum[...] = jnp.zeros_like(out_sum)
        grad_sum[...] = jnp.zeros_like(grad_sum)

    place_rows(weights, starts, blocks)
    pair_weights = weights[:, : 2 * width]
    down = weights[:, 2 * width :]
    chunk = min(256, length)
    for start in range(0, length, chunk):
        span = pl.ds(start, chunk)
        both = dot(rows_in[span, :], pair_weights)
        gate = both[:, :width]
        up = both[:, width:]
        hidden_grad = dot(cotangent_in[span, :], down)
        sigmoid = 0.5 + 0.5 * jnp.tanh(0.5 * gate)
        silu = gate * sigmoid
        hidden = (silu * up).astype(bf16)
        gate_grad = hidden_grad * up * (sigmoid + silu * (1.0 - sigmoid))
        up_grad = hidden_grad * silu
        pair = jnp.concatenate([gate_grad.astype(bf16), up_grad.astype(bf16)], axis=1)
        hiddens[span, :] = hidden
        pairs[span, :] = pair
        out_sum[span, :] += dot_transposed(hidden, down)
        grad_sum[span, :] += dot_transposed(pair, pair_weights)

    @pl.when(step == pl.num_programs(0) - 1)
    def _():
        out[...] = out_sum[...].astype(out.dtype)
        grad[...] = grad_sum[...].astype(grad.dtype)


def hidden_width(units):
    for width in (768, 256, 384, 128):
        if units % width == 0:
            return width
    return units


def feed_forward(rows, cotangent, starts, blocks, width, kind, part, parts, earlier, after):
    length, model = rows.shape
    steps = blocks[0].shape[1] // (3 * width)
    whole = pl.BlockSpec((length, model), lambda i: (0, 0))
    sums = jax.ShapeDtypeStruct((length, model), kind)
    return pl.pallas_call(
        partial(ffn_body, width, len(blocks), len(earlier) + len(after)),
        grid=(steps,),
        in_specs=[pl.BlockSpec(memory_space=pltpu.SMEM), whole, whole]
        + [pl.BlockSpec((block.shape[0], 3 * width), lambda i: (0, i)) for block in blocks]
        + [anywhere()] * (len(earlier) + len(after)),
        input_output_aliases={3 + len(blocks) + at: 2 + at for at in range(len(earlier))},
        out_specs=[
            whole,
            whole,
            pl.BlockSpec((length, 2 * width), lambda i: (part, i)),
            pl.BlockSpec((length, width), lambda i: (part, i)),
        ],
        out_shape=[
            sums,
            sums,
            jax.ShapeDtypeStruct((parts * length, steps * 2 * width), bf16),
            jax.ShapeDtypeStruct((parts * length, steps * width), bf16),
        ],
        scratch_shapes=[
            pltpu.VMEM((length, model), f32),
            pltpu.VMEM((length, model), f32),
            pltpu.VMEM((model, 3 * width), bf16),
        ],
        compiler_params=pltpu.CompilerParams(vmem_limit_bytes=56 * 1024 * 1024),
        cost_estimate=pl.CostEstimate(
            flops=12 * length * model * steps * width,
            bytes_accessed=8 * model * steps * width,
            transcendentals=length * steps * width,
        ),
        name="feed_forward",
    )(starts, rows, cotangent, *blocks, *earlier, *after)


def lines(start, size):
    if isinstance(start, int):
        return pl.ds(start, size)
    return pl.ds(pl.multiple_of(start, size), size)


def part_starts(place, count, part_rows):
    if count == 1:
        return [0]
    return [place[0] * part_rows, (1 - place[0]) * part_rows]


def causal_block(size):
    keys = lax.broadcasted_iota(jnp.int32, (size, size), 0)
    queries = lax.broadcasted_iota(jnp.int32, (size, size), 1)
    return keys <= queries


def attend_body(count, groups, *refs):
    place, weights, query_gain, key_gain, cosine, sine = refs[:6]
    rows_in = refs[6 : 6 + count]
    raw, query_rows, key_rows, value_rows, attended, log_totals, rows = refs[6 + count :]
    part_rows = rows_in[0].shape[0]
    length = rows.shape[0]
    heads = query_rows.shape[0] // HD
    kv_heads = key_rows.shape[0] // HD
    columns = (heads + 2 * kv_heads) * HD
    half = HD // 2
    starts = part_starts(place, count, part_rows)
    for part in range(count):
        rows[lines(starts[part], part_rows), :] = rows_in[part][...]

    chunk = min(256, columns)
    for first in range(0, columns, chunk):
        product = dot_transposed(weights[:, first : first + chunk].T, rows[...])
        for at in range(0, chunk, HD):
            head = (first + at) // HD
            values = product[at : at + HD]
            if head >= heads + kv_heads:
                start = (head - heads - kv_heads) * HD
                value_rows[start : start + HD, :] = values.astype(bf16)
                continue
            raw[first + at : first + at + HD, :] = values
            gain = query_gain if head < heads else key_gain
            scale = lax.rsqrt(jnp.mean(values * values, axis=0, keepdims=True) + eps)
            normed = values * scale * gain[...]
            top, bottom = normed[:half], normed[half:]
            top, bottom = (
                top * cosine[...] - bottom * sine[...],
                bottom * cosine[...] + top * sine[...],
            )
            if head < heads:
                target, start = query_rows, head * HD
                top = top.astype(bf16).astype(f32) * HD**-0.5
                bottom = bottom.astype(bf16).astype(f32) * HD**-0.5
            else:
                target, start = key_rows, (head - heads) * HD
            target[start : start + half, :] = top.astype(bf16)
            target[start + half : start + HD, :] = bottom.astype(bf16)

    attend_groups(query_rows, key_rows, value_rows, attended, log_totals, 0, groups)


def attend_groups(query_rows, key_rows, value_rows, attended, log_totals, first, last):
    length = query_rows.shape[1]
    group_size = query_rows.shape[0] // key_rows.shape[0]
    block = min(256, length)
    causal = causal_block(block)

    def one_group(kv_head, carry):
        span = lines(kv_head * HD, HD)
        keys = key_rows[span, :].T
        values = value_rows[span, :]
        for member in range(group_size):
            head = kv_head * group_size + member
            for start in range(0, length, block):
                here = slice(start, start + block)
                query = query_rows[lines(head * HD, HD), here]
                weight = jnp.where(causal, jnp.exp(dot(keys[here], query)), 0.0)
                total = jnp.sum(weight, axis=0, keepdims=True)
                result = dot(values[:, here], weight.astype(bf16))
                if start:
                    weight = jnp.exp(dot(keys[:start], query))
                    total = total + jnp.sum(weight, axis=0, keepdims=True)
                    result = result + dot(values[:, :start], weight.astype(bf16))
                attended[lines(head * HD, HD), here] = (result * (1.0 / total)).astype(bf16)
                log_totals[head, :, here] = jnp.log(total)
        return carry

    if last > first:
        lax.fori_loop(first, last, one_group, 0)


def attend_rest_body(count, groups, *refs):
    place, weights, query_rows, key_rows, value_rows, attended_first, totals_first = refs[:7]
    refs = refs[7:]
    branches = refs[:count]
    attended_out, attended, log_totals, turned = refs[count:]
    kv_heads = key_rows.shape[0] // HD
    part_rows = branches[0].shape[0]
    done = groups * query_rows.shape[0] // kv_heads
    if groups:
        attended[:done, :] = attended_first[:done, :]
        log_totals[: done // HD] = totals_first[: done // HD]
    attend_groups(query_rows, key_rows, value_rows, attended, log_totals, groups, kv_heads)
    starts = part_starts(place, count, part_rows)
    turned[...] = attended[...].T
    for part in range(count):
        mine = turned[lines(starts[part], part_rows), :]
        attended_out[part * part_rows : (part + 1) * part_rows, :] = mine
        branches[part][...] = dot_transposed(mine, weights[...]).astype(branches[part].dtype)


def attend_first(
    place, weights, query_gain, key_gain, cosine, sine, parts, query_columns, key_columns
):
    count = len(parts)
    part_rows, model = parts[0].shape
    length = count * part_rows
    heads = query_columns // HD
    shape = jax.ShapeDtypeStruct
    groups = key_columns // HD // 2
    attended = [
        shape((query_columns, length), bf16),
        shape((heads, 1, length), f32),
    ]
    outs = [
        shape((query_columns + key_columns, length), f32),
        shape((query_columns, length), bf16),
        shape((key_columns, length), bf16),
        shape((key_columns, length), bf16),
    ] + attended
    return pl.pallas_call(
        partial(attend_body, count, groups),
        grid=(1,),
        in_specs=[pl.BlockSpec(memory_space=pltpu.SMEM)]
        + entire([weights, query_gain, key_gain, cosine, sine, *parts]),
        out_specs=entire(outs),
        out_shape=outs,
        scratch_shapes=[pltpu.VMEM((length, model), bf16)],
        compiler_params=pltpu.CompilerParams(vmem_limit_bytes=56 * 1024 * 1024),
        cost_estimate=attend_cost(length, model, query_columns),
        name="attend",
    )(place, weights, query_gain, key_gain, cosine, sine, *parts)


def attend_cost(length, model, query_columns):
    return pl.CostEstimate(
        flops=4 * length * model * query_columns + 4 * length * length * query_columns,
        bytes_accessed=8 * length * model,
        transcendentals=query_columns // HD * length * length // 2,
    )


def attend_rest(place, weights, kept, count):
    shape = jax.ShapeDtypeStruct
    model = weights.shape[0]
    query_columns, length = kept[1].shape
    key_columns = kept[2].shape[0]
    part_rows = length // count
    groups = key_columns // HD // 2
    columns = query_columns + 2 * key_columns
    kinds = [f32] + [bf16] * (count - 1)
    outs = (
        [shape((part_rows, model), kind) for kind in kinds]
        + [shape((length, query_columns), bf16)]
        + [shape(array.shape, array.dtype) for array in kept[4:]]
    )
    results = pl.pallas_call(
        partial(attend_rest_body, count, groups),
        grid=(1,),
        in_specs=[
            pl.BlockSpec(memory_space=pltpu.SMEM),
            pl.BlockSpec((model, query_columns), lambda i: (0, columns // query_columns)),
        ]
        + entire(kept[1:]),
        out_specs=entire(outs),
        out_shape=outs,
        scratch_shapes=[pltpu.VMEM((length, query_columns), bf16)],
        compiler_params=pltpu.CompilerParams(vmem_limit_bytes=56 * 1024 * 1024),
        cost_estimate=attend_cost(length, model, query_columns),
        name="attend_rest",
    )(place, weights, *kept[1:])
    return results[:count], results[count], (*kept[:4], *results[count + 1 :])


def attend_back_body(count, first_group, last_group, extra, *refs):
    place, weights, query_gain, key_gain, cosine, sine = refs[:6]
    raw, query_rows, key_rows, value_rows, attended, log_totals = refs[6:12]
    branch_in = refs[12 : 12 + count]
    refs = refs[12 + count :]
    if first_group:
        earlier = refs[:3]
        refs = refs[3:]
    if last_group * HD == key_rows.shape[0]:
        normed_in = refs[:count]
        refs = refs[count:]
    refs = refs[extra:]
    last = last_group * HD == key_rows.shape[0]
    if last:
        grads, raw_grads, refs = refs[:count], refs[count], refs[count + 1 :]
        attn_gain_grad, refs = refs[0], refs[1:]
        query_gain_grad, key_gain_grad, turned_grads = refs[:3]
        rows, attended_grad, key_sum, value_sum, straight = refs[3:]
    else:
        turned_grads, query_gain_grad, key_gain_grad = refs[:3]
        rows, attended_grad, key_sum, value_sum = refs[3:]
    part_rows = branch_in[0].shape[0]
    length = rows.shape[0]
    heads = query_rows.shape[0] // HD
    kv_heads = key_rows.shape[0] // HD
    group_size = heads // kv_heads
    columns = (heads + 2 * kv_heads) * HD
    half = HD // 2
    starts = part_starts(place, count, part_rows)
    for part in range(count):
        rows[lines(starts[part], part_rows), :] = branch_in[part][...]
    stage_rows = (last_group - first_group) * group_size * HD
    chunk = min(256, stage_rows)
    begin = first_group * group_size * HD
    for first in range(begin, begin + stage_rows, chunk):
        piece = weights[:, columns + first : columns + first + chunk].T
        attended_grad[first : first + chunk, :] = dot_transposed(piece, rows[...]).astype(bf16)
    if first_group:
        turned_grads[...] = earlier[0][...]
        query_gain_grad[...] = earlier[1][...]
        key_gain_grad[...] = earlier[2][...]
    else:
        turned_grads[...] = jnp.zeros_like(turned_grads)
        query_gain_grad[...] = jnp.zeros_like(query_gain_grad)
        key_gain_grad[...] = jnp.zeros_like(key_gain_grad)
    block = min(256, length)
    causal = causal_block(block)

    def unprepare(grad, values, gain, gain_grad):
        top, bottom = grad[:half], grad[half:]
        grad = jnp.concatenate(
            [
                top * cosine[...] + bottom * sine[...],
                bottom * cosine[...] - top * sine[...],
            ],
            axis=0,
        )
        scale = lax.rsqrt(jnp.mean(values * values, axis=0, keepdims=True) + eps)
        normed = values * scale
        gain_grad[...] += jnp.sum(grad * normed, axis=1, keepdims=True)
        grad = grad * gain[...]
        inner = jnp.mean(grad * normed, axis=0, keepdims=True)
        return (scale * (grad - normed * inner)).astype(bf16)

    def one_group(kv_head, carry):
        span = lines(kv_head * HD, HD)
        keys_turned = key_rows[span, :]
        keys = keys_turned.T
        values = value_rows[span, :].T
        key_sum[...] = jnp.zeros_like(key_sum)
        value_sum[...] = jnp.zeros_like(value_sum)
        for member in range(group_size):
            head = kv_head * group_size + member
            head_span = lines(head * HD, HD)
            query_parts = []
            for start in range(0, length, block):
                here = slice(start, start + block)
                query = query_rows[head_span, here]
                grad = attended_grad[head_span, here]
                inner = jnp.sum(
                    grad.astype(f32) * attended[head_span, here].astype(f32), axis=0, keepdims=True
                )
                log_total = log_totals[head, :, here]
                query_grad = None
                for low, high in [(start, start + block)] + ([(0, start)] if start else []):
                    prob = jnp.exp(dot(keys[low:high], query) - log_total)
                    if low == start:
                        prob = jnp.where(causal, prob, 0.0)
                    prob_grad = dot(values[low:high], grad)
                    score_grad = (prob * (prob_grad - inner)).astype(bf16)
                    piece = dot(keys_turned[:, low:high], score_grad)
                    query_grad = piece if query_grad is None else query_grad + piece
                    key_sum[:, low:high] += dot_transposed(query, score_grad)
                    value_sum[:, low:high] += dot_transposed(grad, prob.astype(bf16))
                query_parts.append(query_grad * HD**-0.5)
            turned_grads[head_span, :] = unprepare(
                jnp.concatenate(query_parts, axis=1), raw[head_span, :], query_gain, query_gain_grad
            )
        key_span = lines((heads + kv_head) * HD, HD)
        turned_grads[key_span, :] = unprepare(
            key_sum[...], raw[key_span, :], key_gain, key_gain_grad
        )
        turned_grads[lines((heads + kv_heads + kv_head) * HD, HD), :] = value_sum[...].astype(bf16)
        return carry

    lax.fori_loop(first_group, last_group, one_group, 0)
    if last:
        straight[...] = turned_grads[...].T
        for part in range(count):
            mine = straight[lines(starts[part], part_rows), :]
            raw_grads[part * part_rows : (part + 1) * part_rows, :] = mine
            grad = dot_transposed(mine, weights[:, :columns])
            grads[part][...] = grad.astype(grads[part].dtype)
            gain_sum = jnp.sum(grad * normed_in[part][...].astype(f32), axis=0, keepdims=True)
            attn_gain_grad[...] = attn_gain_grad[...] + gain_sum if part else gain_sum


def back_stages(kept):
    kv_heads = kept[2].shape[0] // HD
    if kv_heads % 4:
        return [(0, kv_heads)]
    quarter = kv_heads // 4
    return [(0, quarter), (quarter, 3 * quarter), (3 * quarter, kv_heads)]


def attend_back(fixed, kept, parts, normed, stage, earlier, after):
    count = len(parts)
    first_group, last_group = stage
    kv_heads = kept[2].shape[0] // HD
    part_rows, model = parts[0].shape
    length = count * part_rows
    query_columns = kept[1].shape[0]
    columns = query_columns + 2 * kept[2].shape[0]
    shape = jax.ShapeDtypeStruct
    last = last_group == kv_heads
    normed = normed if last else ()
    share = kv_heads // (last_group - first_group)
    gains = [shape((HD, 1), f32)] * 2
    turned = shape((columns, length), bf16)
    scratch = [
        pltpu.VMEM((length, model), bf16),
        pltpu.VMEM((query_columns, length), bf16),
        pltpu.VMEM((HD, length), f32),
        pltpu.VMEM((HD, length), f32),
    ]
    if last:
        outs = (
            [shape((part_rows, model), kind) for kind in [f32] + [bf16] * (count - 1)]
            + [shape((length, columns), bf16)]
            + [shape((1, model), f32)]
            + gains
        )
        scratch = [pltpu.VMEM(turned.shape, bf16)] + scratch + [pltpu.VMEM((length, columns), bf16)]
    else:
        outs = [turned] + gains
    results = pl.pallas_call(
        partial(attend_back_body, count, first_group, last_group, len(after)),
        grid=(1,),
        in_specs=[pl.BlockSpec(memory_space=pltpu.SMEM)]
        + entire([*fixed[1:], *kept, *parts, *earlier, *normed])
        + [anywhere()] * len(after),
        out_specs=entire(outs),
        out_shape=outs,
        scratch_shapes=scratch,
        compiler_params=pltpu.CompilerParams(vmem_limit_bytes=56 * 1024 * 1024),
        cost_estimate=pl.CostEstimate(
            flops=(
                2 * length * model * (query_columns + columns)
                + 20 * length * length * query_columns
            )
            // share,
            bytes_accessed=16 * length * model,
            transcendentals=query_columns // HD * length * length // share,
        ),
        name="attend_back",
    )(*fixed, *kept, *parts, *earlier, *normed, *after)
    if not last:
        return results
    return results[:count], *results[count:]


def on_device(
    tokens,
    out_cotangent,
    attn_gain,
    query_weight,
    key_weight,
    value_weight,
    query_gain,
    key_gain,
    out_weight,
    ffn_gain,
    gate_weight,
    up_weight,
    down_weight,
):
    shard, query_columns = query_weight.shape
    key_columns = key_weight.shape[1]
    qkv_columns = query_columns + 2 * key_columns
    units = gate_weight.shape[1]
    width = hidden_width(units)
    steps = units // width
    pieces = (query_weight, key_weight, value_weight, out_weight.T)
    firsts = [0, query_columns, query_columns + key_columns, qkv_columns]
    places = [(at, 0, firsts[at], piece.shape[1]) for at, piece in enumerate(pieces)]
    attn_starts, attn_blocks, attn_arrived = gather_ring(pack(pieces, places, ()), {})
    rows_in_all = shard * lax.axis_size("fsdp")
    attn_full = assemble(attn_starts, gather_near(attn_blocks), rows_in_all)
    pieces = (gate_weight, up_weight, down_weight.T)
    places = [
        (at, step * width, (3 * step + at) * width, width)
        for step in range(steps)
        for at in range(3)
    ]
    ffn_shard = pack(pieces, places, ())

    residual = tokens.astype(f32)
    normed, attn_norm_pull = jax.vjp(rms_norm, residual, attn_gain)
    normed_parts = widen(normed.astype(bf16))
    if len(normed_parts) == 2:
        cotangent_parts = widen(held(out_cotangent, normed_parts[1:]))
    else:
        cotangent_parts = widen(out_cotangent)
    length = len(normed_parts) * normed_parts[0].shape[0]
    cosine, sine = rotary_tables(length)
    place = lax.axis_index("tp").astype(jnp.int32).reshape(1)
    fixed = (place, attn_full, query_gain[:, None], key_gain[:, None], cosine, sine)
    kept = attend_first(*fixed, normed_parts, query_columns, key_columns)
    ffn_starts, ffn_pieces, ffn_arrived = gather_ring(
        ffn_shard, {1: attn_arrived[-1], 2: [kept[-1]]}
    )
    branch, attended, kept = attend_rest(place, attn_full, kept, len(normed_parts))
    branch = [*branch[:-1], held(branch[-1], (*cotangent_parts[1:], *ffn_arrived[1]))]
    middle = residual + narrow(branch)
    normed_ffn, ffn_norm_pull = jax.vjp(rms_norm, middle, ffn_gain)
    ffn_parts = widen(normed_ffn.astype(bf16))
    ffn_pieces = gather_near(ffn_pieces, ffn_parts[1:])
    parts = len(ffn_parts)
    out_parts, grad_parts, kept_ffn = [None] * parts, [None] * parts, ()
    for at in reversed(range(parts)):
        out_parts[at], grad_parts[at], *kept_ffn = feed_forward(
            ffn_parts[at],
            cotangent_parts[at],
            ffn_starts,
            ffn_pieces,
            width,
            bf16 if at else f32,
            at,
            parts,
            kept_ffn,
            grad_parts[at + 1 :],
        )
    pairs, hiddens = kept_ffn
    ffn_normed_grad = narrow(grad_parts)
    middle_piece, ffn_gain_local = ffn_norm_pull(ffn_normed_grad)
    middle_grad = out_cotangent.astype(f32) + middle_piece
    branch_parts = widen(middle_grad.astype(bf16))

    ffn_blocks = weight_grads(
        ffn_parts,
        cotangent_parts,
        pairs,
        hiddens,
        steps,
        (branch_parts[0],),
        branch_parts[1:],
    )
    ffn_state, sent = ring_open(ffn_blocks)
    ffn_next, attn_next, last = 1, 1, ring_size() // 2
    out_other = [narrow_send(held(out_parts[-1], branch_parts[1:]))] if len(out_parts) == 2 else []
    back = ()
    for stage in back_stages(kept):
        back = attend_back(fixed, kept, branch_parts, normed_parts, stage, back, sent)
        done = back[1] if len(back) == 3 else back[2]
        if ffn_next < last:
            after = (done, *out_other) if ffn_next == 2 else (done,)
            ffn_state, sent = ring_step(ffn_blocks, ffn_next, ffn_state, after)
            ffn_next += 1
    if out_other:
        output = middle + out_parts[0] + out_other[0].astype(f32)
    else:
        output = middle + narrow(out_parts)
    output = output.astype(bf16)
    normed_grad, qkv_grad, attn_gain_local, query_gain_local, key_gain_local = back
    gains = jnp.concatenate(
        [
            attn_gain_local[0] / attn_gain,
            ffn_gain_local,
            query_gain_local[:, 0],
            key_gain_local[:, 0],
        ]
    )
    bit = 1
    while bit < lax.axis_size("tp"):
        gains = gains + swap(gains, "tp", bit)
        bit *= 2
    gain_count = gains.shape[0]
    gains = jnp.pad(gains.astype(bf16), (0, shard * 128 - gain_count)).reshape(shard, 128)
    grad_other = ()
    if len(normed_grad) == 2:
        grad_other = (narrow_send(held(normed_grad[1], (*sent, gains))),)
        normed_grad = normed_grad[0] + grad_other[0].astype(f32)
    else:
        normed_grad = narrow(normed_grad)
    attn_blocks = weight_grads(
        normed_parts, branch_parts, qkv_grad, attended, 1, sent, tail=(gains,)
    )
    attn_state, sent = ring_open(attn_blocks, (output, *ffn_state))
    while ffn_next < last or attn_next < last:
        if ffn_next < last:
            ffn_state, sent = ring_step(ffn_blocks, ffn_next, ffn_state)
            ffn_next += 1
        if attn_next < last:
            after = sent if attn_next < 2 else (*sent, *grad_other)
            attn_state, sent = ring_step(attn_blocks, attn_next, attn_state, after)
            attn_next += 1
    ffn_places = [
        (step * 3 * width + number * width, width, number, step * width)
        for step in range(steps)
        for number in range(3)
    ]
    gate_grad, up_grad, down_grad = ring_close(ffn_blocks, ffn_state, ffn_places)
    attn_places = [
        (0, query_columns, 0, 0),
        (query_columns, key_columns, 1, 0),
        (query_columns + key_columns, key_columns, 2, 0),
        (qkv_columns, query_columns, 3, 0),
        (qkv_columns + query_columns, 128, 4, 0),
    ]
    query_grad, key_grad, value_grad, out_grad, gains = ring_close(attn_blocks, attn_state, attn_places)
    tokens_piece, _ = attn_norm_pull(normed_grad)
    tokens_grad = middle_grad + tokens_piece
    model = attn_gain.shape[0]
    gains = gains.reshape(-1)[:gain_count]
    return (
        output,
        tokens_grad,
        gains[:model],
        query_grad,
        key_grad,
        value_grad,
        gains[2 * model : 2 * model + HD],
        gains[2 * model + HD :],
        out_grad.T,
        gains[model : 2 * model],
        gate_grad,
        up_grad,
        down_grad.T,
    )


def solution(mesh):
    placed = (
        P(("fsdp", "tp"), None),
        P(("fsdp", "tp"), None),
        P(),
        P("fsdp", "tp"),
        P("fsdp", "tp"),
        P("fsdp", "tp"),
        P(),
        P(),
        P("tp", "fsdp"),
        P(),
        P("fsdp", "tp"),
        P("fsdp", "tp"),
        P("tp", "fsdp"),
    )
    return jax.shard_map(
        on_device,
        mesh=mesh,
        in_specs=placed,
        out_specs=(
            P(("fsdp", "tp"), None),
            P(("fsdp", "tp"), None),
            P(),
            P("fsdp", "tp"),
            P("fsdp", "tp"),
            P("fsdp", "tp"),
            P(),
            P(),
            P("tp", "fsdp"),
            P(),
            P("fsdp", "tp"),
            P("fsdp", "tp"),
            P("tp", "fsdp"),
        ),
        check_vma=False,
    )
```

```python
from functools import partial

import jax
import jax.numpy as jnp
from jax import lax
from jax.experimental import pallas as pl
from jax.experimental.pallas import tpu as pltpu
from jax.sharding import PartitionSpec as P

HD = 64

eps = 1e-05
theta_base = 1000000.0
f32 = jnp.float32
bf16 = jnp.bfloat16


def rms_norm(values, gain):
    return values * lax.rsqrt(jnp.mean(values * values, axis=-1, keepdims=True) + eps) * gain


def rotary_tables(length):
    half_size = HD // 2
    frequency = theta_base ** (-jnp.arange(half_size, dtype=f32) * 2.0 / HD)
    angles = frequency[:, None] * jnp.arange(length, dtype=f32)[None, :]
    return (jnp.cos(angles), jnp.sin(angles))


def dot(former, latter):
    return jnp.dot(former, latter, preferred_element_type=f32)


def dot_transposed(former, latter):
    return lax.dot_general(former, latter, (((1,), (1,)), ((), ())), preferred_element_type=f32)


def dot_leading(former, latter):
    return lax.dot_general(former, latter, (((0,), (0,)), ((), ())), preferred_element_type=f32)


def swap(values, axis_name, bit=1):
    count = lax.axis_size(axis_name)
    return lax.ppermute(values, axis_name, [(i, i ^ bit) for i in range(count)])


def anywhere():
    return pl.BlockSpec(memory_space=pl.ANY)


def entire(arrays):
    return [pl.BlockSpec(array.shape, lambda i, rank=array.ndim: (0,) * rank) for array in arrays]


def held_all(arrays, after):
    count = len(arrays)
    return pl.pallas_call(
        lambda *refs: None,
        in_specs=[anywhere()] * (count + len(after)),
        out_specs=[anywhere()] * count,
        out_shape=[jax.ShapeDtypeStruct(array.shape, array.dtype) for array in arrays],
        input_output_aliases={at: at for at in range(count)},
        name="held",
    )(*arrays, *after)


def held(values, after):
    return held_all([values], after)[0]


def widen(rows):
    if lax.axis_size("tp") == 2:
        return (rows, swap(rows, "tp"))
    return (lax.all_gather(rows, "tp", axis=0, tiled=True),)


def narrow_send(part):
    return swap(part.astype(bf16), "tp")


def narrow(parts):
    if len(parts) == 2:
        return parts[0].astype(f32) + narrow_send(parts[1]).astype(f32)
    return lax.psum_scatter(
        parts[0].astype(bf16), "tp", scatter_dimension=0, tiled=True
    ).astype(f32)


def ring_size():
    return lax.axis_size("fsdp") // 2


def chip_at(place):
    chips = ring_size()
    if isinstance(place, int):
        return 2 * place if place < chips // 2 else 2 * (chips - 1 - place) + 1
    return jnp.where(place < chips // 2, 2 * place, 2 * (chips - 1 - place) + 1)


def own_place():
    chip = lax.axis_index("fsdp") // 2
    return jnp.where(chip % 2 == 0, chip // 2, ring_size() - 1 - chip // 2)


def pass_on(values, direction):
    chips = ring_size()
    pairs = [
        (2 * chip_at(place) + core, 2 * chip_at((place + direction) % chips) + core)
        for place in range(chips)
        for core in range(2)
    ]
    return lax.ppermute(values, "fsdp", pairs)


def shard_table(ahead):
    core = lax.axis_index("fsdp") % 2
    chips = chip_at((own_place() + jnp.array(ahead, jnp.int32)) % ring_size())
    return jnp.concatenate([2 * chips + core, 2 * chips + 1 - core]).astype(jnp.int32)


def gather_ring(shard, ready):
    rows = shard.shape[0]
    half = rows // 2
    chips = ring_size()
    blocks, ahead, offset, arrived = [], [0], [0], []
    sent = [shard]
    for step in range(1, chips // 2 + 1):
        if step in ready:
            sent = held_all(sent, ready[step])
        blocks += sent
        down, up = sent[0], sent[-1]
        if step == chips // 2:
            down, up = down[:half], up[half:]
        sent = [pass_on(down, 1), pass_on(up, -1)]
        arrived.append(sent)
        ahead += [chips - step, step]
        offset += [0, half if step == chips // 2 else 0]
    blocks += sent
    starts = shard_table(ahead) * rows + jnp.array(offset * 2, jnp.int32)
    return starts, blocks, arrived


def gather_near(blocks, ready=()):
    ends = held_all(blocks[-2:], ready) if ready else blocks[-2:]
    blocks = [*blocks[:-2], *ends]
    return blocks + [swap(block, "fsdp") for block in blocks]


def place_rows(whole, starts, blocks):
    for at, block in enumerate(blocks):
        whole[pl.ds(pl.multiple_of(starts[at], 16), block.shape[0]), :] = block[...]


def assemble_body(starts, *refs):
    place_rows(refs[-1], starts, refs[:-1])


def assemble(starts, blocks, rows):
    out = jax.ShapeDtypeStruct((rows, blocks[0].shape[1]), bf16)
    return pl.pallas_call(
        assemble_body,
        grid=(1,),
        in_specs=[pl.BlockSpec(memory_space=pltpu.SMEM)] + entire(blocks),
        out_specs=entire([out])[0],
        out_shape=out,
        compiler_params=pltpu.CompilerParams(vmem_limit_bytes=48 * 1024 * 1024),
        name="assemble",
    )(starts, *blocks)


def pack_body(places, *refs):
    whole = refs[-1]
    for number, source, start, width in places:
        whole[:, start : start + width] = refs[number][:, source : source + width]


def pack(arrays, places, after):
    columns = max(start + width for _, _, start, width in places)
    out = jax.ShapeDtypeStruct((arrays[0].shape[0], columns), bf16)
    return pl.pallas_call(
        partial(pack_body, places),
        grid=(1,),
        in_specs=entire(arrays) + [anywhere()] * len(after),
        out_specs=entire([out])[0],
        out_shape=out,
        compiler_params=pltpu.CompilerParams(vmem_limit_bytes=32 * 1024 * 1024),
        name="pack",
    )(*arrays, *after)


def ring_groups():
    chips = ring_size()
    middle = [[chips // 2 - step, chips // 2 + step] for step in range(1, chips // 2)]
    return [[chips // 2]] + middle + [[0]]


def weight_grad_body(parts, groups, rows, tails, extra, *refs):
    table = refs[0]
    first_in = refs[1 : 1 + parts]
    second_in = refs[1 + parts : 1 + 2 * parts]
    first_grads, second_grads = refs[1 + 2 * parts : 3 + 2 * parts]
    tail = refs[3 + 2 * parts : 3 + 2 * parts + tails]
    outs = refs[3 + 2 * parts + tails + extra : -3]
    first_turned, second_turned, straight = refs[-3:]
    part_rows = first_in[0].shape[0]
    first_width = first_grads.shape[1]
    count = sum(len(group) for group in groups)

    @pl.when(pl.program_id(0) == 0)
    def _():
        for pieces, turned in ((first_in, first_turned), (second_in, second_turned)):
            for part in range(parts):
                span = pl.ds(part * part_rows, part_rows)
                straight[:, span] = pieces[part][...].T
            for at in range(2 * count):
                start = pl.multiple_of(table[at] * rows, rows)
                turned[at * rows : (at + 1) * rows, :] = straight[pl.ds(start, rows), :]

    for turned, grads, start in (
        (first_turned, first_grads, 0),
        (second_turned, second_grads, first_width),
    ):
        here = slice(start, start + grads.shape[1])
        for core in range(2):
            part = dot(turned[core * count * rows : (core + 1) * count * rows, :], grads[...])
            at = 0
            for number, group in enumerate(groups):
                for member in range(len(group)):
                    values = part[at * rows : (at + 1) * rows]
                    outs[core * len(groups) + number][member, :, here] = values.astype(bf16)
                    at += 1
    for piece in tail:
        for out in outs:
            for member in range(out.shape[0]):
                out[member, :, out.shape[2] - piece.shape[1] :] = piece[...]


def weight_grads(first, second, first_grads, second_grads, steps, after, before=(), tail=()):
    parts = len(first)
    part_rows, model = first[0].shape
    length = parts * part_rows
    first_width = first_grads.shape[1] // steps
    second_width = second_grads.shape[1] // steps
    width = first_width + second_width + sum(piece.shape[1] for piece in tail)
    groups = ring_groups()
    count = 2 * ring_size()
    rows = model // count
    table = shard_table([place for group in groups for place in group])
    whole = pl.BlockSpec((part_rows, model), lambda i: (0, 0))
    outs = [jax.ShapeDtypeStruct((len(group), rows, steps * width), bf16) for group in groups] * 2
    out_specs = [
        pl.BlockSpec((len(group), rows, width), lambda i: (0, 0, i)) for group in groups
    ] * 2
    results = pl.pallas_call(
        partial(weight_grad_body, parts, groups, rows, len(tail), len(after)),
        grid=(steps,),
        in_specs=[pl.BlockSpec(memory_space=pltpu.SMEM)]
        + [whole] * (2 * parts)
        + [pl.BlockSpec((length, first_width), lambda i: (0, i))]
        + [pl.BlockSpec((length, second_width), lambda i: (0, i))]
        + entire(tail)
        + [anywhere()] * len(after),
        out_specs=out_specs,
        out_shape=outs,
        scratch_shapes=[
            pltpu.VMEM((model, length), bf16),
            pltpu.VMEM((model, length), bf16),
            pltpu.VMEM((model, length), bf16),
        ],
        compiler_params=pltpu.CompilerParams(vmem_limit_bytes=56 * 1024 * 1024),
        cost_estimate=pl.CostEstimate(
            flops=2 * length * model * steps * width,
            bytes_accessed=4 * model * steps * width,
            transcendentals=0,
        ),
        name="weight_grads",
    )(table, *first, *second, first_grads, second_grads, *tail, *after)
    mine = results[: len(groups)]
    near = list(results[len(groups) :])
    if before:
        near[0] = held(near[0], before)
    near = [swap(block, "fsdp") for block in near]
    return mine, near


def ring_call(body, operands, outs, after, name):
    return pl.pallas_call(
        body,
        grid=(1,),
        in_specs=entire(operands) + [anywhere()] * len(after),
        out_specs=entire(outs),
        out_shape=outs,
        compiler_params=pltpu.CompilerParams(vmem_limit_bytes=48 * 1024 * 1024),
        name=name,
    )(*operands, *after)


def both_cores(mine, near, member):
    return mine[member].astype(f32) + near[member].astype(f32)


def open_body(cut, mine, near, *refs):
    low, high = refs[-2:]
    total = both_cores(mine, near, 0).astype(bf16)
    low[...] = total[:, :cut]
    high[...] = total[:, cut:]


def step_body(cut, mine, near, down, up, *refs):
    ahead, behind = refs[-2:]
    columns = ahead.shape[1]
    ahead_sum = both_cores(mine, near, 0)
    behind_sum = both_cores(mine, near, 1)
    if down.shape[1] == columns:
        ahead[...] = (ahead_sum + down[...].astype(f32)).astype(bf16)
        behind[...] = (behind_sum + up[...].astype(f32)).astype(bf16)
    else:
        ahead[:, :cut] = (ahead_sum[:, :cut] + down[...].astype(f32)).astype(bf16)
        ahead[:, cut:] = ahead_sum[:, cut:].astype(bf16)
        behind[:, :cut] = behind_sum[:, :cut].astype(bf16)
        behind[:, cut:] = (behind_sum[:, cut:] + up[...].astype(f32)).astype(bf16)


def step_halves_body(first, mine, near, down, up, *refs):
    ahead, behind = refs[-2:]
    low = pl.program_id(0) == 0
    ahead_sum = both_cores(mine, near, 0)
    behind_sum = both_cores(mine, near, 1)
    down_part, up_part = down[...].astype(f32), up[...].astype(f32)
    if first:
        down_part = jnp.where(low, down_part, 0.0)
        up_part = jnp.where(low, 0.0, up_part)
    ahead[...] = (ahead_sum + down_part).astype(bf16)
    behind[...] = (behind_sum + up_part).astype(bf16)


def close_body(pieces, mine, near, down, up, *outs):
    total = both_cores(mine, near, 0) + down[...].astype(f32) + up[...].astype(f32)
    for start, width, number, place in pieces:
        outs[number][:, place : place + width] = total[:, start : start + width]


def ring_cut(columns):
    return columns // 2 // 128 * 128


def ring_pass(sums):
    return pass_on(sums[0], 1), pass_on(sums[1], -1)


def ring_open(blocks, after=()):
    mine, near = blocks
    rows, columns = mine[0].shape[1:]
    cut = ring_cut(columns)
    outs = [jax.ShapeDtypeStruct((rows, width), bf16) for width in (cut, columns - cut)]
    sums = ring_call(partial(open_body, cut), (mine[0], near[0]), outs, after, "ring_open")
    return ring_pass(sums), tuple(sums)


def ring_step(blocks, number, state, after=()):
    mine, near = blocks[0][number], blocks[1][number]
    rows, columns = mine.shape[1:]
    outs = [jax.ShapeDtypeStruct((rows, columns), bf16)] * 2
    cut = ring_cut(columns)
    if 2 * cut == columns:
        first = state[0].shape[1] == cut
        pair = pl.BlockSpec((2, rows, cut), lambda i: (0, 0, i))
        block = pl.BlockSpec((rows, cut), lambda i: (0, i))
        state_block = pl.BlockSpec((rows, cut), lambda i: (0, 0)) if first else block
        sums = pl.pallas_call(
            partial(step_halves_body, first),
            grid=(2,),
            in_specs=[pair, pair, state_block, state_block] + [anywhere()] * len(after),
            out_specs=[block, block],
            out_shape=outs,
            compiler_params=pltpu.CompilerParams(vmem_limit_bytes=48 * 1024 * 1024),
            name="ring_step",
        )(mine, near, *state, *after)
    else:
        body = partial(step_body, cut)
        sums = ring_call(body, (mine, near, *state), outs, after, "ring_step")
    return ring_pass(sums), tuple(sums)


def ring_close(blocks, state, pieces):
    mine, near = blocks[0][-1], blocks[1][-1]
    rows = mine.shape[1]
    sizes = {}
    for _, width, number, place in pieces:
        sizes[number] = max(sizes.get(number, 0), place + width)
    outs = [jax.ShapeDtypeStruct((rows, sizes[number]), f32) for number in range(len(sizes))]
    return ring_call(partial(close_body, pieces), (mine, near, *state), outs, (), "ring_close")


def ffn_body(width, count, extra, *refs):
    starts, rows_in, cotangent_in = refs[:3]
    blocks = refs[3 : 3 + count]
    out, grad, pairs, hiddens, out_sum, grad_sum, weights = refs[3 + count + extra :]
    step = pl.program_id(0)
    length = rows_in.shape[0]

    @pl.when(step == 0)
    def _():
        out_sum[...] = jnp.zeros_like(out_sum)
        grad_sum[...] = jnp.zeros_like(grad_sum)

    place_rows(weights, starts, blocks)
    pair_weights = weights[:, : 2 * width]
    down = weights[:, 2 * width :]
    chunk = min(256, length)
    for start in range(0, length, chunk):
        span = pl.ds(start, chunk)
        both = dot(rows_in[span, :], pair_weights)
        gate = both[:, :width]
        up = both[:, width:]
        hidden_grad = dot(cotangent_in[span, :], down)
        sigmoid = 0.5 + 0.5 * jnp.tanh(0.5 * gate)
        silu = gate * sigmoid
        hidden = (silu * up).astype(bf16)
        gate_grad = hidden_grad * up * (sigmoid + silu * (1.0 - sigmoid))
        up_grad = hidden_grad * silu
        pair = jnp.concatenate([gate_grad.astype(bf16), up_grad.astype(bf16)], axis=1)
        hiddens[span, :] = hidden
        pairs[span, :] = pair
        out_sum[span, :] += dot_transposed(hidden, down)
        grad_sum[span, :] += dot_transposed(pair, pair_weights)

    @pl.when(step == pl.num_programs(0) - 1)
    def _():
        out[...] = out_sum[...].astype(out.dtype)
        grad[...] = grad_sum[...].astype(grad.dtype)


def hidden_width(units):
    for width in (768, 256, 384, 128):
        if units % width == 0:
            return width
    return units


def feed_forward(rows, cotangent, starts, blocks, width, kind, part, parts, earlier, after):
    length, model = rows.shape
    steps = blocks[0].shape[1] // (3 * width)
    whole = pl.BlockSpec((length, model), lambda i: (0, 0))
    sums = jax.ShapeDtypeStruct((length, model), kind)
    return pl.pallas_call(
        partial(ffn_body, width, len(blocks), len(earlier) + len(after)),
        grid=(steps,),
        in_specs=[pl.BlockSpec(memory_space=pltpu.SMEM), whole, whole]
        + [pl.BlockSpec((block.shape[0], 3 * width), lambda i: (0, i)) for block in blocks]
        + [anywhere()] * (len(earlier) + len(after)),
        input_output_aliases={3 + len(blocks) + at: 2 + at for at in range(len(earlier))},
        out_specs=[
            whole,
            whole,
            pl.BlockSpec((length, 2 * width), lambda i: (part, i)),
            pl.BlockSpec((length, width), lambda i: (part, i)),
        ],
        out_shape=[
            sums,
            sums,
            jax.ShapeDtypeStruct((parts * length, steps * 2 * width), bf16),
            jax.ShapeDtypeStruct((parts * length, steps * width), bf16),
        ],
        scratch_shapes=[
            pltpu.VMEM((length, model), f32),
            pltpu.VMEM((length, model), f32),
            pltpu.VMEM((model, 3 * width), bf16),
        ],
        compiler_params=pltpu.CompilerParams(vmem_limit_bytes=56 * 1024 * 1024),
        cost_estimate=pl.CostEstimate(
            flops=12 * length * model * steps * width,
            bytes_accessed=8 * model * steps * width,
            transcendentals=length * steps * width,
        ),
        name="feed_forward",
    )(starts, rows, cotangent, *blocks, *earlier, *after)


def lines(start, size):
    if isinstance(start, int):
        return pl.ds(start, size)
    return pl.ds(pl.multiple_of(start, size), size)


def part_starts(place, count, part_rows):
    if count == 1:
        return [0]
    return [place[0] * part_rows, (1 - place[0]) * part_rows]


def causal_block(size):
    keys = lax.broadcasted_iota(jnp.int32, (size, size), 0)
    queries = lax.broadcasted_iota(jnp.int32, (size, size), 1)
    return keys <= queries


def attend_body(count, extra, *refs):
    place, weights, query_gain, key_gain, cosine, sine = refs[:6]
    rows_in = refs[6 : 6 + count]
    refs = refs[:6] + refs[6 + extra :]
    branches = refs[6 + count : 6 + 2 * count]
    attended_out = refs[6 + 2 * count]
    raw, query_rows, key_rows, value_rows, attended, log_totals = refs[7 + 2 * count : 13 + 2 * count]
    rows, turned = refs[13 + 2 * count :]
    part_rows = rows_in[0].shape[0]
    length = rows.shape[0]
    heads = query_rows.shape[0] // HD
    kv_heads = key_rows.shape[0] // HD
    group_size = heads // kv_heads
    columns = (heads + 2 * kv_heads) * HD
    half = HD // 2
    starts = part_starts(place, count, part_rows)
    for part in range(count):
        rows[lines(starts[part], part_rows), :] = rows_in[part][...]

    chunk = min(256, columns)
    for first in range(0, columns, chunk):
        product = dot_transposed(weights[:, first : first + chunk].T, rows[...])
        for at in range(0, chunk, HD):
            head = (first + at) // HD
            values = product[at : at + HD]
            if head >= heads + kv_heads:
                start = (head - heads - kv_heads) * HD
                value_rows[start : start + HD, :] = values.astype(bf16)
                continue
            raw[first + at : first + at + HD, :] = values
            gain = query_gain if head < heads else key_gain
            scale = lax.rsqrt(jnp.mean(values * values, axis=0, keepdims=True) + eps)
            normed = values * scale * gain[...]
            top, bottom = normed[:half], normed[half:]
            top, bottom = (
                top * cosine[...] - bottom * sine[...],
                bottom * cosine[...] + top * sine[...],
            )
            if head < heads:
                target, start = query_rows, head * HD
                top = top.astype(bf16).astype(f32) * HD**-0.5
                bottom = bottom.astype(bf16).astype(f32) * HD**-0.5
            else:
                target, start = key_rows, (head - heads) * HD
            target[start : start + half, :] = top.astype(bf16)
            target[start + half : start + HD, :] = bottom.astype(bf16)

    block = min(256, length)
    causal = causal_block(block)

    def one_group(kv_head, carry):
        span = lines(kv_head * HD, HD)
        keys = key_rows[span, :].T
        values = value_rows[span, :]
        for member in range(group_size):
            head = kv_head * group_size + member
            for start in range(0, length, block):
                here = slice(start, start + block)
                query = query_rows[lines(head * HD, HD), here]
                weight = jnp.where(causal, jnp.exp(dot(keys[here], query)), 0.0)
                total = jnp.sum(weight, axis=0, keepdims=True)
                result = dot(values[:, here], weight.astype(bf16))
                if start:
                    weight = jnp.exp(dot(keys[:start], query))
                    total = total + jnp.sum(weight, axis=0, keepdims=True)
                    result = result + dot(values[:, :start], weight.astype(bf16))
                attended[lines(head * HD, HD), here] = (result * (1.0 / total)).astype(bf16)
                log_totals[head, :, here] = jnp.log(total)
        return carry

    lax.fori_loop(0, kv_heads, one_group, 0)
    turned[...] = attended[...].T
    for part in range(count):
        mine = turned[lines(starts[part], part_rows), :]
        attended_out[part * part_rows : (part + 1) * part_rows, :] = mine
        branches[part][...] = dot_transposed(mine, weights[:, columns:]).astype(branches[part].dtype)


def attend(
    place, weights, query_gain, key_gain, cosine, sine, parts, query_columns, key_columns, after
):
    count = len(parts)
    part_rows, model = parts[0].shape
    length = count * part_rows
    heads = query_columns // HD
    shape = jax.ShapeDtypeStruct
    kinds = [f32] + [bf16] * (count - 1)
    outs = (
        [shape((part_rows, model), kind) for kind in kinds]
        + [shape((length, query_columns), bf16)]
        + [
            shape((query_columns + key_columns, length), f32),
            shape((query_columns, length), bf16),
            shape((key_columns, length), bf16),
            shape((key_columns, length), bf16),
            shape((query_columns, length), bf16),
            shape((heads, 1, length), f32),
        ]
    )
    results = pl.pallas_call(
        partial(attend_body, count, len(after)),
        grid=(1,),
        in_specs=[pl.BlockSpec(memory_space=pltpu.SMEM)]
        + entire([weights, query_gain, key_gain, cosine, sine, *parts])
        + [anywhere()] * len(after),
        out_specs=entire(outs),
        out_shape=outs,
        scratch_shapes=[
            pltpu.VMEM((length, model), bf16),
            pltpu.VMEM((length, query_columns), bf16),
        ],
        compiler_params=pltpu.CompilerParams(vmem_limit_bytes=56 * 1024 * 1024),
        cost_estimate=pl.CostEstimate(
            flops=2 * length * model * (2 * query_columns + 2 * key_columns)
            + 8 * length * length * query_columns,
            bytes_accessed=16 * length * model,
            transcendentals=heads * length * length,
        ),
        name="attend",
    )(place, weights, query_gain, key_gain, cosine, sine, *parts, *after)
    return results[:count], results[count], results[count + 1 :]


def attend_back_body(count, first_group, last_group, extra, *refs):
    place, weights, query_gain, key_gain, cosine, sine = refs[:6]
    raw, query_rows, key_rows, value_rows, attended, log_totals = refs[6:12]
    branch_in = refs[12 : 12 + count]
    refs = refs[12 + count :]
    if first_group:
        earlier = refs[:3]
        refs = refs[3:]
    if last_group * HD == key_rows.shape[0]:
        normed_in = refs[:count]
        refs = refs[count:]
    refs = refs[extra:]
    last = last_group * HD == key_rows.shape[0]
    if last:
        grads, raw_grads, refs = refs[:count], refs[count], refs[count + 1 :]
        attn_gain_grad, refs = refs[0], refs[1:]
        query_gain_grad, key_gain_grad, turned_grads = refs[:3]
        rows, attended_grad, key_sum, value_sum, straight = refs[3:]
    else:
        turned_grads, query_gain_grad, key_gain_grad = refs[:3]
        rows, attended_grad, key_sum, value_sum = refs[3:]
    part_rows = branch_in[0].shape[0]
    length = rows.shape[0]
    heads = query_rows.shape[0] // HD
    kv_heads = key_rows.shape[0] // HD
    group_size = heads // kv_heads
    columns = (heads + 2 * kv_heads) * HD
    half = HD // 2
    starts = part_starts(place, count, part_rows)
    for part in range(count):
        rows[lines(starts[part], part_rows), :] = branch_in[part][...]
    stage_rows = (last_group - first_group) * group_size * HD
    chunk = min(256, stage_rows)
    begin = first_group * group_size * HD
    out_first = columns if last else 0
    for first in range(begin, begin + stage_rows, chunk):
        piece = weights[:, out_first + first : out_first + first + chunk].T
        attended_grad[first : first + chunk, :] = dot_transposed(piece, rows[...]).astype(bf16)
    if first_group:
        turned_grads[...] = earlier[0][...]
        query_gain_grad[...] = earlier[1][...]
        key_gain_grad[...] = earlier[2][...]
    else:
        turned_grads[...] = jnp.zeros_like(turned_grads)
        query_gain_grad[...] = jnp.zeros_like(query_gain_grad)
        key_gain_grad[...] = jnp.zeros_like(key_gain_grad)
    block = min(256, length)
    causal = causal_block(block)

    def unprepare(grad, values, gain, gain_grad):
        top, bottom = grad[:half], grad[half:]
        grad = jnp.concatenate(
            [
                top * cosine[...] + bottom * sine[...],
                bottom * cosine[...] - top * sine[...],
            ],
            axis=0,
        )
        scale = lax.rsqrt(jnp.mean(values * values, axis=0, keepdims=True) + eps)
        normed = values * scale
        gain_grad[...] += jnp.sum(grad * normed, axis=1, keepdims=True)
        grad = grad * gain[...]
        inner = jnp.mean(grad * normed, axis=0, keepdims=True)
        return (scale * (grad - normed * inner)).astype(bf16)

    def one_group(kv_head, carry):
        span = lines(kv_head * HD, HD)
        keys_turned = key_rows[span, :]
        keys = keys_turned.T
        values = value_rows[span, :].T
        key_sum[...] = jnp.zeros_like(key_sum)
        value_sum[...] = jnp.zeros_like(value_sum)
        for member in range(group_size):
            head = kv_head * group_size + member
            head_span = lines(head * HD, HD)
            query_parts = []
            for start in range(0, length, block):
                here = slice(start, start + block)
                query = query_rows[head_span, here]
                grad = attended_grad[head_span, here]
                inner = jnp.sum(
                    grad.astype(f32) * attended[head_span, here].astype(f32), axis=0, keepdims=True
                )
                log_total = log_totals[head, :, here]
                query_grad = None
                for low, high in [(start, start + block)] + ([(0, start)] if start else []):
                    prob = jnp.exp(dot(keys[low:high], query) - log_total)
                    if low == start:
                        prob = jnp.where(causal, prob, 0.0)
                    prob_grad = dot(values[low:high], grad)
                    score_grad = (prob * (prob_grad - inner)).astype(bf16)
                    piece = dot(keys_turned[:, low:high], score_grad)
                    query_grad = piece if query_grad is None else query_grad + piece
                    key_sum[:, low:high] += dot_transposed(query, score_grad)
                    value_sum[:, low:high] += dot_transposed(grad, prob.astype(bf16))
                query_parts.append(query_grad * HD**-0.5)
            turned_grads[head_span, :] = unprepare(
                jnp.concatenate(query_parts, axis=1), raw[head_span, :], query_gain, query_gain_grad
            )
        key_span = lines((heads + kv_head) * HD, HD)
        turned_grads[key_span, :] = unprepare(
            key_sum[...], raw[key_span, :], key_gain, key_gain_grad
        )
        turned_grads[lines((heads + kv_heads + kv_head) * HD, HD), :] = value_sum[...].astype(bf16)
        return carry

    lax.fori_loop(first_group, last_group, one_group, 0)
    if last:
        straight[...] = turned_grads[...].T
        for part in range(count):
            mine = straight[lines(starts[part], part_rows), :]
            raw_grads[part * part_rows : (part + 1) * part_rows, :] = mine
            grad = dot_transposed(mine, weights[:, :columns])
            grads[part][...] = grad.astype(grads[part].dtype)
            gain_sum = jnp.sum(grad * normed_in[part][...].astype(f32), axis=0, keepdims=True)
            attn_gain_grad[...] = attn_gain_grad[...] + gain_sum if part else gain_sum


def back_stages(kept):
    kv_heads = kept[2].shape[0] // HD
    if kv_heads % 4:
        return [(0, kv_heads)]
    quarter = kv_heads // 4
    return [(0, quarter), (quarter, 3 * quarter), (3 * quarter, kv_heads)]


def attend_back(fixed, kept, parts, normed, stage, earlier, after):
    count = len(parts)
    first_group, last_group = stage
    kv_heads = kept[2].shape[0] // HD
    part_rows, model = parts[0].shape
    length = count * part_rows
    query_columns = kept[1].shape[0]
    columns = query_columns + 2 * kept[2].shape[0]
    shape = jax.ShapeDtypeStruct
    last = last_group == kv_heads
    normed = normed if last else ()
    share = kv_heads // (last_group - first_group)
    gains = [shape((HD, 1), f32)] * 2
    turned = shape((columns, length), bf16)
    scratch = [
        pltpu.VMEM((length, model), bf16),
        pltpu.VMEM((query_columns, length), bf16),
        pltpu.VMEM((HD, length), f32),
        pltpu.VMEM((HD, length), f32),
    ]
    if last:
        outs = (
            [shape((part_rows, model), kind) for kind in [f32] + [bf16] * (count - 1)]
            + [shape((length, columns), bf16)]
            + [shape((1, model), f32)]
            + gains
        )
        scratch = [pltpu.VMEM(turned.shape, bf16)] + scratch + [pltpu.VMEM((length, columns), bf16)]
    else:
        outs = [turned] + gains
    results = pl.pallas_call(
        partial(attend_back_body, count, first_group, last_group, len(after)),
        grid=(1,),
        in_specs=[pl.BlockSpec(memory_space=pltpu.SMEM)]
        + (
            entire(fixed[1:2])
            if last
            else [pl.BlockSpec((model, query_columns), lambda i: (0, columns // query_columns))]
        )
        + entire([*fixed[2:], *kept, *parts, *earlier, *normed])
        + [anywhere()] * len(after),
        out_specs=entire(outs),
        out_shape=outs,
        scratch_shapes=scratch,
        compiler_params=pltpu.CompilerParams(vmem_limit_bytes=56 * 1024 * 1024),
        cost_estimate=pl.CostEstimate(
            flops=(
                2 * length * model * (query_columns + columns)
                + 20 * length * length * query_columns
            )
            // share,
            bytes_accessed=16 * length * model,
            transcendentals=query_columns // HD * length * length // share,
        ),
        name="attend_back",
    )(*fixed, *kept, *parts, *earlier, *normed, *after)
    if not last:
        return results
    return results[:count], *results[count:]


def on_device(
    tokens,
    out_cotangent,
    attn_gain,
    query_weight,
    key_weight,
    value_weight,
    query_gain,
    key_gain,
    out_weight,
    ffn_gain,
    gate_weight,
    up_weight,
    down_weight,
):
    shard, query_columns = query_weight.shape
    key_columns = key_weight.shape[1]
    qkv_columns = query_columns + 2 * key_columns
    units = gate_weight.shape[1]
    width = hidden_width(units)
    steps = units // width
    pieces = (query_weight, key_weight, value_weight, out_weight.T)
    firsts = [0, query_columns, query_columns + key_columns, qkv_columns]
    places = [(at, 0, firsts[at], piece.shape[1]) for at, piece in enumerate(pieces)]
    attn_starts, attn_blocks, attn_arrived = gather_ring(pack(pieces, places, ()), {})
    rows_in_all = shard * lax.axis_size("fsdp")
    attn_full = assemble(attn_starts, gather_near(attn_blocks), rows_in_all)
    pieces = (gate_weight, up_weight, down_weight.T)
    places = [
        (at, step * width, (3 * step + at) * width, width)
        for step in range(steps)
        for at in range(3)
    ]
    ffn_shard = pack(pieces, places, ())
    ffn_starts, ffn_pieces, ffn_arrived = gather_ring(ffn_shard, {1: attn_arrived[-1]})

    residual = tokens.astype(f32)
    normed, attn_norm_pull = jax.vjp(rms_norm, residual, attn_gain)
    normed_parts = widen(normed.astype(bf16))
    if len(normed_parts) == 2:
        cotangent_parts = widen(held(out_cotangent, normed_parts[1:]))
    else:
        cotangent_parts = widen(out_cotangent)
    length = len(normed_parts) * normed_parts[0].shape[0]
    cosine, sine = rotary_tables(length)
    place = lax.axis_index("tp").astype(jnp.int32).reshape(1)
    fixed = (place, attn_full, query_gain[:, None], key_gain[:, None], cosine, sine)
    branch, attended, kept = attend(
        *fixed, normed_parts, query_columns, key_columns, ffn_arrived[0]
    )
    branch = [*branch[:-1], held(branch[-1], (*cotangent_parts[1:], *ffn_arrived[1]))]
    middle = residual + narrow(branch)
    normed_ffn, ffn_norm_pull = jax.vjp(rms_norm, middle, ffn_gain)
    ffn_parts = widen(normed_ffn.astype(bf16))
    ffn_pieces = gather_near(ffn_pieces, ffn_parts[1:])
    parts = len(ffn_parts)
    out_parts, grad_parts, kept_ffn = [None] * parts, [None] * parts, ()
    for at in reversed(range(parts)):
        out_parts[at], grad_parts[at], *kept_ffn = feed_forward(
            ffn_parts[at],
            cotangent_parts[at],
            ffn_starts,
            ffn_pieces,
            width,
            bf16 if at else f32,
            at,
            parts,
            kept_ffn,
            grad_parts[at + 1 :],
        )
    pairs, hiddens = kept_ffn
    ffn_normed_grad = narrow(grad_parts)
    middle_piece, ffn_gain_local = ffn_norm_pull(ffn_normed_grad)
    middle_grad = out_cotangent.astype(f32) + middle_piece
    branch_parts = widen(middle_grad.astype(bf16))

    ffn_blocks = weight_grads(
        ffn_parts,
        cotangent_parts,
        pairs,
        hiddens,
        steps,
        (branch_parts[0],),
        branch_parts[1:],
    )
    ffn_state, sent = ring_open(ffn_blocks)
    ffn_next, attn_next, last = 1, 1, ring_size() // 2
    out_other = [narrow_send(held(out_parts[-1], branch_parts[1:]))] if len(out_parts) == 2 else []
    back = ()
    for stage in back_stages(kept):
        back = attend_back(fixed, kept, branch_parts, normed_parts, stage, back, sent)
        done = back[1] if len(back) == 3 else back[2]
        if ffn_next < last:
            after = (done, *out_other) if ffn_next == 2 else (done,)
            ffn_state, sent = ring_step(ffn_blocks, ffn_next, ffn_state, after)
            ffn_next += 1
    if out_other:
        output = middle + out_parts[0] + out_other[0].astype(f32)
    else:
        output = middle + narrow(out_parts)
    output = output.astype(bf16)
    normed_grad, qkv_grad, attn_gain_local, query_gain_local, key_gain_local = back
    gains = jnp.concatenate(
        [
            attn_gain_local[0] / attn_gain,
            ffn_gain_local,
            query_gain_local[:, 0],
            key_gain_local[:, 0],
        ]
    )
    bit = 1
    while bit < lax.axis_size("tp"):
        gains = gains + swap(gains, "tp", bit)
        bit *= 2
    gain_count = gains.shape[0]
    gains = jnp.pad(gains.astype(bf16), (0, shard * 128 - gain_count)).reshape(shard, 128)
    grad_other = ()
    if len(normed_grad) == 2:
        grad_other = (narrow_send(held(normed_grad[1], (*sent, gains))),)
        normed_grad = normed_grad[0] + grad_other[0].astype(f32)
    else:
        normed_grad = narrow(normed_grad)
    attn_blocks = weight_grads(
        normed_parts, branch_parts, qkv_grad, attended, 1, sent, tail=(gains,)
    )
    attn_state, sent = ring_open(attn_blocks, (output, *ffn_state))
    while ffn_next < last or attn_next < last:
        if ffn_next < last:
            ffn_state, sent = ring_step(ffn_blocks, ffn_next, ffn_state)
            ffn_next += 1
        if attn_next < last:
            after = sent if attn_next < 2 else (*sent, *grad_other)
            attn_state, sent = ring_step(attn_blocks, attn_next, attn_state, after)
            attn_next += 1
    ffn_places = [
        (step * 3 * width + number * width, width, number, step * width)
        for step in range(steps)
        for number in range(3)
    ]
    gate_grad, up_grad, down_grad = ring_close(ffn_blocks, ffn_state, ffn_places)
    attn_places = [
        (0, query_columns, 0, 0),
        (query_columns, key_columns, 1, 0),
        (query_columns + key_columns, key_columns, 2, 0),
        (qkv_columns, query_columns, 3, 0),
        (qkv_columns + query_columns, 128, 4, 0),
    ]
    query_grad, key_grad, value_grad, out_grad, gains = ring_close(attn_blocks, attn_state, attn_places)
    tokens_piece, _ = attn_norm_pull(normed_grad)
    tokens_grad = middle_grad + tokens_piece
    model = attn_gain.shape[0]
    gains = gains.reshape(-1)[:gain_count]
    return (
        output,
        tokens_grad,
        gains[:model],
        query_grad,
        key_grad,
        value_grad,
        gains[2 * model : 2 * model + HD],
        gains[2 * model + HD :],
        out_grad.T,
        gains[model : 2 * model],
        gate_grad,
        up_grad,
        down_grad.T,
    )


def solution(mesh):
    placed = (
        P(("fsdp", "tp"), None),
        P(("fsdp", "tp"), None),
        P(),
        P("fsdp", "tp"),
        P("fsdp", "tp"),
        P("fsdp", "tp"),
        P(),
        P(),
        P("tp", "fsdp"),
        P(),
        P("fsdp", "tp"),
        P("fsdp", "tp"),
        P("tp", "fsdp"),
    )
    return jax.shard_map(
        on_device,
        mesh=mesh,
        in_specs=placed,
        out_specs=(
            P(("fsdp", "tp"), None),
            P(("fsdp", "tp"), None),
            P(),
            P("fsdp", "tp"),
            P("fsdp", "tp"),
            P("fsdp", "tp"),
            P(),
            P(),
            P("tp", "fsdp"),
            P(),
            P("fsdp", "tp"),
            P("fsdp", "tp"),
            P("tp", "fsdp"),
        ),
        check_vma=False,
    )
```
